128 devices in a mesh: march: 32 (over x, y, core), cross: 4 (over z).
Axes of the slice: x: 4, y: 4, z: 4, core: 2. Of those that a mesh axis runs over, the one named last changes fastest.
Arguments:
- velocity_guess: float32 [128, 512, 512], P('march', 'cross'), may hold values from -6 to 6
- damping: float32 [128, 512, 512], P('march', 'cross'), may hold values from 0.001 to 0.5
- inflow: float32 [512, 512], P('cross'), may hold values from -6 to 6
- disc_rows: int32 [256], replicated, may hold values from 0 to 511, as said below
- owner: int32 [256], replicated, may hold values from 0 to 31, as said below
- blade: bfloat16 [32, 512, 512], P('march', None, 'cross'), may hold values from -0.25 to 0.25
Outputs:
- velocity: float32 [128, 512, 512], P('march', 'cross')
- pressure: float32 [128, 512, 512], P('march', 'cross')
The draws below stay inside these ranges and needn't reach their ends.
Inputs may be any that keep to these rules, and one draw needn't show every extreme that they name: `disc_rows`: the 256 disc rows are distinct. Every owner owns at least one disc row.
All inputs are finite; a program needn't handle non-finite values.
Results may differ from the reference program's by a relative error of at most 0.001.
Values may be sent and summed in bfloat16 or wider, within the bound.
No kernel may reach another device: no remote copies, remote signals or barrier semaphores. Data moves between devices by JAX's collectives and lax.ppermute only.
A program may use at most 128 MiB of HBM per device.

```python
import math
import jax
import jax.numpy as jnp
from jax import lax

NC = 512
R = 256
SWEEPS = 2
NS = 128
DISC_STATION = 64
OWNERS = 32
N_MARCH = 32
N_CROSS = 4


def draw_disc_rows(key, part):
    key = jax.random.fold_in(key, 11)
    key_rows, key_order = jax.random.split(key)
    block = NC // N_CROSS
    lasts = jnp.arange(N_CROSS, dtype=jnp.int32) * block + (block - 1)
    picks = jax.random.permutation(key_rows, N_CROSS * (block - 1))[:R - N_CROSS].astype(jnp.int32)
    others = picks // (block - 1) * block + picks % (block - 1)
    rows_all = jnp.concatenate([lasts, others.astype(jnp.int32)])
    order = jax.random.permutation(key_order, R)
    return rows_all[order].astype(jnp.int32)


def draw_owner(key, part):
    key = jax.random.fold_in(key, 23)
    key_base, key_one, key_two, key_map, key_order = jax.random.split(key, 5)
    base = jax.random.permutation(key_base, N_MARCH).astype(jnp.int32)
    first = jax.random.randint(key_one, (R - N_MARCH,), 0, N_MARCH, dtype=jnp.int32)
    second = jax.random.randint(key_two, (R - N_MARCH,), 0, N_MARCH, dtype=jnp.int32)
    mapping = jax.random.permutation(key_map, N_MARCH).astype(jnp.int32)
    extra = mapping[jnp.minimum(first, second)]
    owners_all = jnp.concatenate([base, extra.astype(jnp.int32)])
    order = jax.random.permutation(key_order, R)
    return owners_all[order].astype(jnp.int32)


def shard_levels(rng, dims, cuts, least, largest):
    factor_of, own = 1.0, jax.random.fold_in(rng, 6)
    for axis_at, blocks in cuts:
        heights = jnp.exp(jax.random.uniform(jax.random.fold_in(own, axis_at), (blocks,), jnp.float32, least / len(cuts), largest / len(cuts)))
        factor_of = factor_of * jnp.repeat(heights, dims[axis_at] // blocks).reshape([-1 if axis == axis_at else 1 for axis in range(len(dims))])
    return factor_of


def noise(key, shape, deviation, reach, pieces=(), held_as=jnp.bfloat16):
    result = jax.random.normal(key, shape, jnp.float32) * deviation
    if len(pieces) > 0:
        result = shard_levels(key, shape, pieces, -0.22, 0.18) * result
    return jnp.clip(result, min=-reach, max=reach).astype(held_as)


def setup_inputs(seed: int = 0) -> dict:
    key_of = jax.random.split(jax.random.key(seed), 7)
    return {
        "velocity_guess": noise(key_of[0], (NS, NC, NC), 1.0, 6.0, ((0, 32), (1, 4)), jnp.float32),
        "damping": jnp.clip(jnp.exp(math.log(0.5) - 6.214608 * jax.random.uniform(key_of[1], (NS, NC, NC), jnp.float32) ** shard_levels(key_of[1], (NS, NC, NC), ((0, 32), (1, 4)), -0.2, 0.2)), 0.001, 0.5),
        "inflow": noise(key_of[2], (NC, NC), 1.0, 6.0, ((0, 4),), jnp.float32),
        "disc_rows": draw_disc_rows(jax.random.fold_in(key_of[6], 71), 0),
        "owner": draw_owner(jax.random.fold_in(key_of[6], 71), 0),
        "blade": noise(key_of[5], (OWNERS, NC, NC), NC ** -0.5, 0.25, ((0, 32), (2, 4))),
    }


SOURCE_GAIN = 0.04
SCREENING = 0.001
VISCOSITY = 0.1
DRAG_RATE = 0.01

def sine_table(length):
    ordinal = jnp.arange(length, dtype=jnp.int32) + 1
    product = ordinal[:, None] * ordinal[None, :] % (2 * (length + 1))
    return jnp.sqrt(2.0 / (length + 1)) * jnp.sin(jnp.pi * product.astype(jnp.float32) / (length + 1))

def eigen_values(length):
    ordinal = jnp.arange(length, dtype=jnp.int32) + 1
    return 2.0 - 2.0 * jnp.cos(jnp.pi * ordinal.astype(jnp.float32) / (length + 1))

def reference(velocity_guess, damping, inflow, disc_rows, owner, blade):
    highest = lax.Precision.HIGHEST
    transform = sine_table(NC)
    spectrum = eigen_values(NC)
    divisor = SCREENING + spectrum[:, None] + spectrum[None, :]
    current = velocity_guess
    pressure = jnp.zeros_like(velocity_guess)
    station_ids = jnp.arange(NS, dtype=jnp.int32)
    for sweep_index in range(SWEEPS):
        upstream = jnp.concatenate([inflow[None], current[:-1]], axis=0)
        source = SOURCE_GAIN * (current - upstream)
        spectral = jnp.einsum('sjk,kl->sjl', source, transform, precision=highest)
        spectral = jnp.einsum('ij,sjl->sil', transform, spectral, precision=highest) / divisor
        spectral = jnp.einsum('ij,sjl->sil', transform, spectral, precision=highest)
        pressure = jnp.einsum('sjk,kl->sjl', spectral, transform, precision=highest)
        following = jnp.concatenate([pressure[1:], jnp.zeros_like(pressure[:1])], axis=0)
        gradient = following - pressure
        padded = jnp.pad(current, ((0, 0), (1, 1), (1, 1)))
        laplace = padded[:, 2:, 1:-1] + padded[:, :-2, 1:-1] + padded[:, 1:-1, 2:] + padded[:, 1:-1, :-2] - 4.0 * current
        disc_velocity = current[DISC_STATION][disc_rows].astype(jnp.bfloat16)

        def one_owner(running, scanned):
            owner_id, table_piece = scanned
            response = jnp.dot(disc_velocity, table_piece, preferred_element_type=jnp.float32)
            return (running + jnp.where((owner == owner_id)[:, None], jnp.tanh(response), 0.0), None)
        forces, _ = lax.scan(one_owner, jnp.zeros((R, NC), jnp.float32), (jnp.arange(OWNERS, dtype=jnp.int32), blade))
        force_plane = jnp.zeros((NC, NC), jnp.float32).at[disc_rows].set(forces)
        decay = 1.0 - (damping + DRAG_RATE * jnp.abs(current))
        increment = VISCOSITY * laplace - gradient

        def advance(state_plane, scanned):
            decay_k, term_k, station = scanned
            extra = jnp.where(station == DISC_STATION, force_plane, 0.0)
            state_plane = decay_k * state_plane + (term_k + extra)
            return (state_plane, state_plane)
        _, current = lax.scan(advance, inflow, (decay, increment, station_ids))
    return (current, pressure)
```

```python
import ml_dtypes
import numpy as np
import jax
import jax.numpy as jnp
from jax import lax
from jax.experimental import pallas as pl
from jax.experimental.pallas import tpu as pltpu
from jax.sharding import PartitionSpec as P

SWEEPS = 2
SOURCE_GAIN = 0.04
SCREENING = 0.001
VISCOSITY = 0.1
DRAG_RATE = 0.01

F32 = jnp.float32
BF16 = jnp.bfloat16
SUB = 8
LANE = 128
PARAMS = pltpu.CompilerParams(vmem_limit_bytes=32 * 1024 * 1024)
VMEM = pl.BlockSpec(memory_space=pltpu.VMEM)
SMEM = pl.BlockSpec(memory_space=pltpu.SMEM)


def tables(length):
    ordinal = np.arange(1, length + 1)
    product = np.outer(ordinal, ordinal) % (2 * (length + 1))
    sine = np.sqrt(2.0 / (length + 1)) * np.sin(np.pi * product / (length + 1))
    high = sine.astype(np.float32).astype(ml_dtypes.bfloat16)
    low = (sine - high.astype(np.float64)).astype(np.float32).astype(ml_dtypes.bfloat16)
    values = 2.0 - 2.0 * np.cos(np.pi * ordinal / (length + 1))
    inverse = 1.0 / (SCREENING + values[:, None] + values[None, :])
    return high, low, inverse.astype(np.float32)


def split(value):
    high = value.astype(BF16)
    return high, (value - high.astype(F32)).astype(BF16)


def groups(rows):
    return [(g, slice(SUB * g, SUB * g + SUB)) for g in range(rows // SUB)]


def to_chunks(ref, g, value):
    for h in range(2):
        for q in range(2):
            at = (2 * h + q) * LANE
            ref[2 * g + h, SUB * q : SUB * q + SUB, :] = value[:, at : at + LANE]


def from_chunks(ref, g):
    parts = []
    for h in range(2):
        for q in range(2):
            parts.append(ref[2 * g + h, SUB * q : SUB * q + SUB, :])
    return jnp.concatenate(parts, axis=1)


def decay_of(value, damping):
    return 1.0 - (damping + DRAG_RATE * jnp.abs(value))


def source_kernel(place, current, upstream, *outs):
    c = place[0]
    stations = current.shape[0]
    for r in range(stations):
        s = lax.rem(c + r, stations)
        before = jnp.maximum(s - 1, 0)
        for _, rows in groups(current.shape[1]):
            previous = jnp.where(s == 0, upstream[rows], current[before, rows])
            outs[r][rows] = SOURCE_GAIN * (current[s, rows] - previous)


def decay_kernel(current, damping, decay, scale):
    for g, rows in groups(current.shape[1]):
        product = None
        for s in range(current.shape[0]):
            d = decay_of(current[s, rows], damping[s, rows])
            decay[s, rows] = d
            product = d if product is None else product * d
        to_chunks(scale, g, product)


def laplace_kernel(current, above, below, term):
    stations, height, width = current.shape
    lane = lax.broadcasted_iota(jnp.int32, (SUB, width), 1)
    for s in range(stations):
        for g, rows in groups(height):
            here = current[s, rows]
            lo, hi = SUB * g, SUB * g + SUB
            if g == 0:
                up = jnp.concatenate([above[s : s + 1], current[s, 0 : SUB - 1]], axis=0)
            else:
                up = current[s, lo - 1 : hi - 1]
            if hi == height:
                down = jnp.concatenate([current[s, lo + 1 : hi], below[s : s + 1]], axis=0)
            else:
                down = current[s, lo + 1 : hi + 1]
            left = jnp.where(lane == 0, 0.0, pltpu.roll(here, 1, 1))
            right = jnp.where(lane == width - 1, 0.0, pltpu.roll(here, width - 1, 1))
            term[s, rows] = VISCOSITY * (up + down + left + right - 4.0 * here)


def solve_kernel(place, x0, x1, x2, x3, high, low, inverse, p0, p1, p2, p3, plane):
    c = place[0]
    inputs, outputs = (x0, x1, x2, x3), (p0, p1, p2, p3)
    count = len(inputs)
    height = x0.shape[0]
    for r, ref in enumerate(inputs):
        b = lax.rem(c - r + count, count)
        plane[pl.ds(pl.multiple_of(b * height, height), height), :] = ref[...]
    sh, sl = high[...], low[...]
    by_left = jnp.concatenate([sh, sh, sl], axis=1)
    by_right = jnp.concatenate([sh, sl, sh], axis=0)

    def right(value):
        vh, vl = split(value)
        return jnp.dot(
            jnp.concatenate([vh, vh, vl], axis=1), by_right, preferred_element_type=F32
        )

    def left(value):
        vh, vl = split(value)
        return jnp.dot(
            by_left, jnp.concatenate([vh, vl, vh], axis=0), preferred_element_type=F32
        )

    modes = left(right(plane[...])) * inverse[...]
    plane[...] = right(left(modes))
    for r, ref in enumerate(outputs):
        b = lax.rem(c + r, count)
        ref[...] = plane[pl.ds(pl.multiple_of(b * height, height), height), :]


def disc_kernel(d0, d1, d2, d3, owners, blade, f0, f1, f2, f3, rows, total):
    step = pl.program_id(0)
    height = d0.shape[0]

    @pl.when(step == 0)
    def _():
        for r, ref in enumerate((d0, d1, d2, d3)):
            rows[height * r : height * (r + 1)] = ref[...]
        total[...] = jnp.zeros_like(total)

    per_step = blade.shape[0]
    for j in range(0, per_step, 2):
        pair = jnp.concatenate([blade[j], blade[j + 1]], axis=1)
        response = jnp.dot(rows[...], pair, preferred_element_type=F32)
        first = step * per_step + j
        kept = jnp.where(owners[...] == first, response[:, :LANE], total[...])
        total[...] = jnp.where(owners[...] == first + 1, response[:, LANE:], kept)

    @pl.when(step == pl.num_programs(0) - 1)
    def _():
        for r, ref in enumerate((f0, f1, f2, f3)):
            ref[...] = jnp.tanh(total[height * r : height * (r + 1)])


def offset_kernel(
    place, p0, p1, p2, p3, f0, f1, f2, f3, decay, term, inflow, pressure, lead, force, offset
):
    c = place[0]
    first = place[1]
    pieces, forces = (p0, p1, p2, p3), (f0, f1, f2, f3)
    count = len(pieces)
    width = inflow.shape[1] // count
    for r in range(count):
        s = lax.rem(c - r + count, count)
        pressure[s] = pieces[r][...]
        b = lax.rem(c + r, count)
        force[:, pl.ds(pl.multiple_of(b * width, width), width)] = forces[r][...]
    for g, rows in groups(inflow.shape[0]):
        start = pressure[0, rows]
        lead[rows] = start
        state = jnp.where(first == 1, inflow[rows] + start, 0.0)
        for s in range(count):
            d = decay[s, rows]
            t = term[s, rows]
            if s == 0:
                t = t + force[rows]
            state = d * state + (t + (1.0 - d) * pressure[s, rows])
        to_chunks(offset, g, state)


def scan_kernel(scale, offset, entering):
    entering[0] = jnp.zeros_like(entering[0])
    state = offset[0]
    for m in range(1, scale.shape[0]):
        entering[m] = state
        state = scale[m] * state + offset[m]


def march_rows(first, g, rows, entering, pressure, following, decay, term, force, inflow):
    stations = decay.shape[0]
    ahead = pressure[0, rows]
    state = jnp.where(first == 1, inflow[rows], from_chunks(entering, g) - ahead)
    states = [state]
    for s in range(stations):
        here = ahead
        ahead = following[rows] if s == stations - 1 else pressure[s + 1, rows]
        t = term[s, rows]
        if s == 0:
            t = t + force[rows]
        state = decay[s, rows] * state + (t - (ahead - here))
        states.append(state)
    return states


def middle_kernel(
    place, entering, pressure, following, decay, term, force, inflow, damping,
    current, decay_new, scale, s0, s1, s2, s3, top, bottom, disc, source,
):
    c = place[0]
    first = place[1]
    stations, height, _ = current.shape
    for g, rows in groups(height):
        states = march_rows(
            first, g, rows, entering, pressure, following, decay, term, force, inflow
        )
        product = None
        for s in range(stations):
            value = states[s + 1]
            current[s, rows] = value
            source[s, rows] = SOURCE_GAIN * (value - states[s])
            d = decay_of(value, damping[s, rows])
            decay_new[s, rows] = d
            product = d if product is None else product * d
            if g == 0:
                top[s : s + 1] = value[0:1]
            if SUB * (g + 1) == height:
                bottom[s : s + 1] = value[SUB - 1 : SUB]
        to_chunks(scale, g, product)
    disc[...] = current[0].astype(BF16)
    for r, ref in enumerate((s0, s1, s2, s3)):
        ref[...] = source[lax.rem(c + r, stations)]


def last_kernel(
    place, entering, pressure, following, decay, term, force, inflow, current
):
    first = place[1]
    for g, rows in groups(current.shape[1]):
        states = march_rows(
            first, g, rows, entering, pressure, following, decay, term, force, inflow
        )
        for s in range(current.shape[0]):
            current[s, rows] = states[s + 1]


def call(kernel, outs, args, scratch=(), cost=None, scalars=0):
    return pl.pallas_call(
        kernel,
        out_shape=[jax.ShapeDtypeStruct(shape, dtype) for shape, dtype in outs],
        in_specs=[SMEM] * scalars + [VMEM] * (len(args) - scalars),
        out_specs=[VMEM] * len(outs),
        scratch_shapes=list(scratch),
        compiler_params=PARAMS,
        cost_estimate=cost,
    )(*args)


def cost(flops, size):
    return pl.CostEstimate(flops=int(flops), bytes_accessed=int(size), transcendentals=0)


def local(velocity_guess, damping, inflow, disc_rows, owner, blade):
    stations, height, width = velocity_guess.shape
    march_size = lax.axis_size("march")
    cross_size = lax.axis_size("cross")
    march_index = lax.axis_index("march")
    cross_index = lax.axis_index("cross")
    disc_slab = stations * march_size // 2 // stations
    at_disc = march_index == disc_slab
    first = (march_index == 0).astype(jnp.int32)
    place = jnp.stack([cross_index.astype(jnp.int32), first])
    high, low, inverse = (jnp.asarray(t) for t in tables(width))

    slab = (stations, height, width)
    plane = (height, width)
    chunks = (march_size, height * width // march_size // LANE, LANE)
    mib = 4 * stations * height * width

    def turn(value, steps):
        return lax.ppermute(
            value, "cross", [(i, (i + steps) % cross_size) for i in range(cross_size)]
        )

    def turn_disc(value, steps):
        base = disc_slab * cross_size
        return lax.ppermute(
            value,
            ("march", "cross"),
            [(base + i, base + (i + steps) % cross_size) for i in range(cross_size)],
        )

    def exchange(blocks):
        return [blocks[0]] + [turn(blocks[r], r) for r in range(1, cross_size)]

    def along(value, axis, steps):
        count = lax.axis_size(axis)
        return lax.ppermute(
            value, axis, [(i, i + steps) for i in range(count) if 0 <= i + steps < count]
        )

    def across_march(value):
        return lax.all_to_all(value, "march", split_axis=0, concat_axis=0, tiled=True)

    turns = jnp.repeat(jnp.arange(cross_size, dtype=jnp.int32), height)
    ids = (cross_index - turns + cross_size) % cross_size * height + jnp.tile(
        jnp.arange(height, dtype=jnp.int32), cross_size
    )
    owners = jnp.max(
        jnp.where(ids[:, None] == disc_rows[None, :], owner[None, :], -1), axis=1
    )
    owners = jnp.where(at_disc, owners, -1)
    owners = jnp.broadcast_to(owners[:, None], (cross_size * height, LANE))
    blades = lax.all_gather(blade, "march", axis=0, tiled=True)

    upstream = along(velocity_guess[-1], "march", 1)
    upstream = jnp.where(first == 1, inflow, upstream)
    current = velocity_guess
    disc = current[0].astype(BF16)
    top, bottom = current[:, 0], current[:, -1]
    decay, scale = call(
        decay_kernel, [(slab, F32), (chunks, F32)], (current, damping), cost=cost(4e6, 3.25 * mib)
    )
    source = call(
        source_kernel,
        [(plane, F32)] * stations,
        (place, current, upstream),
        cost=cost(1e6, 2 * mib),
        scalars=1,
    )
    for sweep_index in range(SWEEPS):
        arrived = exchange(source)
        scales = across_march(scale)
        above = along(bottom, "cross", 1)
        below = along(top, "cross", -1)
        rows = [disc] + [turn_disc(disc, r) for r in range(1, cross_size)]
        (term,) = call(
            laplace_kernel, [(slab, F32)], (current, above, below), cost=cost(4e6, 2 * mib)
        )
        solved = call(
            solve_kernel,
            [(plane, F32)] * cross_size,
            (place, *arrived, high, low, inverse),
            scratch=[pltpu.VMEM((width, width), F32)],
            cost=cost(3 * 8 * width**3, 5 * mib),
            scalars=1,
        )
        piece = (height, LANE)
        per_step = 4
        fixed = lambda shape: pl.BlockSpec(shape, lambda i: (0,) * len(shape))
        forces = pl.pallas_call(
            disc_kernel,
            grid=(march_size // per_step,),
            out_shape=[jax.ShapeDtypeStruct(piece, F32)] * cross_size,
            in_specs=[fixed(plane)] * cross_size
            + [
                fixed(owners.shape),
                pl.BlockSpec((per_step, width, LANE), lambda i: (i, 0, 0)),
            ],
            out_specs=[fixed(piece)] * cross_size,
            scratch_shapes=[
                pltpu.VMEM((width, width), BF16),
                pltpu.VMEM((width, LANE), F32),
            ],
            compiler_params=PARAMS,
            cost_estimate=cost(2 * march_size * width * width * LANE, 5 * mib),
        )(*rows, owners, blades)
        forces = [forces[0]] + [turn_disc(forces[r], -r) for r in range(1, cross_size)]
        pieces = exchange(solved)
        pressure, lead, force, offset = call(
            offset_kernel,
            [(slab, F32), (plane, F32), (plane, F32), (chunks, F32)],
            (place, *pieces, *forces, decay, term, inflow),
            cost=cost(4e6, 5 * mib),
            scalars=1,
        )
        following = along(lead, "march", -1)
        (entering,) = call(
            scan_kernel,
            [(chunks, F32)],
            (scales, across_march(offset)),
            cost=cost(1e5, mib),
        )
        entering = across_march(entering)
        common = (place, entering, pressure, following, decay, term, force, inflow)
        if sweep_index < SWEEPS - 1:
            outs = call(
                middle_kernel,
                [(slab, F32), (slab, F32), (chunks, F32)]
                + [(plane, F32)] * stations
                + [((stations, width), F32)] * 2
                + [(plane, BF16)],
                common + (damping,),
                scratch=[pltpu.VMEM(slab, F32)],
                cost=cost(8e6, 8 * mib),
                scalars=1,
            )
            current, decay, scale = outs[:3]
            source = outs[3 : 3 + stations]
            top, bottom, disc = outs[3 + stations :]
        else:
            (current,) = call(
                last_kernel, [(slab, F32)], common, cost=cost(4e6, 5 * mib), scalars=1
            )
    return (current, pressure)


def solution(mesh):
    in_specs = (
        P("march", "cross", None),
        P("march", "cross", None),
        P("cross", None),
        P(),
        P(),
        P("march", None, "cross"),
    )
    out_specs = (P("march", "cross", None), P("march", "cross", None))
    return jax.shard_map(local, mesh=mesh, in_specs=in_specs, out_specs=out_specs, check_vma=False)
```

```python
import ml_dtypes
import numpy as np
import jax
import jax.numpy as jnp
from jax import lax
from jax.experimental import pallas as pl
from jax.experimental.pallas import tpu as pltpu
from jax.sharding import PartitionSpec as P

SWEEPS = 2
SOURCE_GAIN = 0.04
SCREENING = 0.001
VISCOSITY = 0.1
DRAG_RATE = 0.01

F32 = jnp.float32
BF16 = jnp.bfloat16
SUB = 8
LANE = 128
EDGE = 8
STEPS = 4
MIB = 1024 * 1024
VMEM = pl.BlockSpec(memory_space=pltpu.VMEM)
SMEM = pl.BlockSpec(memory_space=pltpu.SMEM)


def tables(length):
    ordinal = np.arange(1, length + 1)
    product = np.outer(ordinal, ordinal) % (2 * (length + 1))
    sine = np.sqrt(2.0 / (length + 1)) * np.sin(np.pi * product / (length + 1))
    high = sine.astype(np.float32).astype(ml_dtypes.bfloat16)
    low = (sine - high.astype(np.float64)).astype(np.float32).astype(ml_dtypes.bfloat16)
    values = 2.0 - 2.0 * np.cos(np.pi * ordinal / (length + 1))
    inverse = 1.0 / (SCREENING + values[:, None] + values[None, :])
    return high, low, inverse.astype(np.float32)


def split(value):
    high = value.astype(BF16)
    return high, (value - high.astype(F32)).astype(BF16)


def groups(rows):
    return [(g, slice(SUB * g, SUB * g + SUB)) for g in range(rows // SUB)]


def to_chunks(ref, g, value):
    for h in range(2):
        for q in range(2):
            at = (2 * h + q) * LANE
            ref[2 * g + h, SUB * q : SUB * q + SUB, :] = value[:, at : at + LANE]


def from_chunks(ref, g):
    parts = []
    for h in range(2):
        for q in range(2):
            parts.append(ref[2 * g + h, SUB * q : SUB * q + SUB, :])
    return jnp.concatenate(parts, axis=1)


def decay_of(value, damping):
    return 1.0 - (damping + DRAG_RATE * jnp.abs(value))


def send_order(place, i, source, outs):
    count, height, _ = source.shape
    at = pl.multiple_of(i * height, height)
    for r, ref in enumerate(outs):
        ref[pl.ds(at, height), :] = source[lax.rem(place[0] + r, count)]


def send_edges(current, outs):
    stations, height, width = current.shape
    i = pl.program_id(0)
    total = outs[1].shape[0]
    empty = jnp.zeros((EDGE - stations, width), F32)

    @pl.when(i == pl.num_programs(0) - 1)
    def _():
        rows = [current[s, height - 1 : height] for s in range(stations)]
        outs[1][total - EDGE : total] = jnp.concatenate(rows + [empty], axis=0)

    @pl.when(i == 0)
    def _():
        rows = [current[s, 0:1] for s in range(stations)]
        outs[-1][total - EDGE : total] = jnp.concatenate(rows + [empty], axis=0)


def source_kernel(place, current, upstream, inflow, x0, x1, x2, x3, source):
    stations, height, _ = current.shape
    for _, rows in groups(height):
        previous = jnp.where(place[1] == 1, inflow[rows], upstream[rows])
        for s in range(stations):
            here = current[s, rows]
            source[s, rows] = SOURCE_GAIN * (here - previous)
            previous = here
    outs = (x0, x1, x2, x3)
    send_order(place, pl.program_id(0), source, outs)
    send_edges(current, outs)


def decay_kernel(place, current, damping, decay, scale):
    for g, rows in groups(current.shape[1]):
        product = None
        for s in range(current.shape[0]):
            d = decay_of(current[s, rows], damping[s, rows])
            decay[s, rows] = d
            product = d if product is None else product * d
        to_chunks(scale, g, product)


def laplace_kernel(place, current, before, after, term):
    stations, height, width = current.shape
    above = jnp.where(place[2] == 1, 0.0, before[height : height + EDGE])
    below = jnp.where(place[3] == 1, 0.0, after[height : height + EDGE])
    lane = lax.broadcasted_iota(jnp.int32, (SUB, width), 1)
    for s in range(stations):
        for g, rows in groups(height):
            here = current[s, rows]
            lo, hi = SUB * g, SUB * g + SUB
            if g == 0:
                up = jnp.concatenate([above[s : s + 1], current[s, 0 : SUB - 1]], axis=0)
            else:
                up = current[s, lo - 1 : hi - 1]
            if hi == height:
                down = jnp.concatenate([current[s, lo + 1 : hi], below[s : s + 1]], axis=0)
            else:
                down = current[s, lo + 1 : hi + 1]
            left = jnp.where(lane == 0, 0.0, pltpu.roll(here, 1, 1))
            right = jnp.where(lane == width - 1, 0.0, pltpu.roll(here, width - 1, 1))
            term[s, rows] = VISCOSITY * (up + down + left + right - 4.0 * here)


def solve_kernel(
    place, x0, x1, x2, x3, high_far, low_far, inverse_far, p0, p1, p2, p3,
    plane, high, low, inverse, arrivals,
):
    c = place[0]
    copies = [
        pltpu.make_async_copy(far_ref, ref, arrivals.at[i])
        for i, (far_ref, ref) in enumerate(
            ((high_far, high), (low_far, low), (inverse_far, inverse))
        )
    ]
    for copy in copies:
        copy.start()
    inputs, outputs = (x0, x1, x2, x3), (p0, p1, p2, p3)
    count = len(inputs)
    height = p0.shape[0]
    for r, ref in enumerate(inputs):
        b = lax.rem(c - r + count, count)
        plane[pl.ds(pl.multiple_of(b * height, height), height), :] = ref[0:height]
    copies[0].wait()
    copies[1].wait()
    sh, sl = high[...], low[...]
    by_left = jnp.concatenate([sh, sh, sl], axis=1)
    by_right = jnp.concatenate([sh, sl, sh], axis=0)

    def right(value):
        vh, vl = split(value)
        return jnp.dot(
            jnp.concatenate([vh, vh, vl], axis=1), by_right, preferred_element_type=F32
        )

    def left(value):
        vh, vl = split(value)
        return jnp.dot(
            by_left, jnp.concatenate([vh, vl, vh], axis=0), preferred_element_type=F32
        )

    modes = left(right(plane[...]))
    copies[2].wait()
    modes = modes * inverse[...]
    plane[...] = right(left(modes))
    for r, ref in enumerate(outputs):
        b = lax.rem(c + r, count)
        ref[...] = plane[pl.ds(pl.multiple_of(b * height, height), height), :]


def disc_kernel(d0, d1, d2, d3, owners, blade_a, blade_b, f0, f1, f2, f3, plane, total):
    step = pl.program_id(0)
    height = d0.shape[0]

    @pl.when(step == 0)
    def _():
        for r, ref in enumerate((d0, d1, d2, d3)):
            plane[height * r : height * (r + 1)] = ref[...]
        total[...] = jnp.zeros_like(total)

    per_step = blade_a.shape[0]
    for i in range(0, per_step, 2):
        pair = jnp.concatenate(
            [
                jnp.concatenate([blade_a[i], blade_b[i]], axis=0),
                jnp.concatenate([blade_a[i + 1], blade_b[i + 1]], axis=0),
            ],
            axis=1,
        )
        response = jnp.dot(plane[...], pair, preferred_element_type=F32)
        first = step * per_step + i
        kept = jnp.where(owners[...] == first, response[:, :LANE], total[...])
        total[...] = jnp.where(owners[...] == first + 1, response[:, LANE:], kept)

    @pl.when(step == pl.num_programs(0) - 1)
    def _():
        for r, ref in enumerate((f0, f1, f2, f3)):
            ref[...] = jnp.tanh(total[height * r : height * (r + 1)])


def offset_kernel(
    place, p0, p1, p2, p3, f0, f1, f2, f3, decay, term, inflow, pressure, lead, force, offset
):
    c = place[0]
    first = place[1]
    pieces, forces = (p0, p1, p2, p3), (f0, f1, f2, f3)
    count = len(pieces)
    width = inflow.shape[1] // count
    for r in range(count):
        s = lax.rem(c - r + count, count)
        pressure[s] = pieces[r][...]
        b = lax.rem(c + r, count)
        force[:, pl.ds(pl.multiple_of(b * width, width), width)] = forces[r][...]
    for g, rows in groups(inflow.shape[0]):
        start = pressure[0, rows]
        lead[rows] = start
        state = jnp.where(first == 1, inflow[rows] + start, 0.0)
        for s in range(count):
            p = pressure[s, rows]
            t = term[s, rows]
            if s == 0:
                t = t + force[rows]
            d = decay[s, rows]
            state = d * state + (t + (1.0 - d) * p)
        to_chunks(offset, g, state)


def scan_kernel(scale, offset, entering):
    entering[0] = jnp.zeros_like(entering[0])
    state = offset[0]
    for m in range(1, scale.shape[0]):
        entering[m] = state
        state = scale[m] * state + offset[m]


def march_rows(first, g, rows, entering, pressure, following, decay, term, force, inflow):
    stations = decay.shape[0]
    ahead = pressure[0, rows]
    state = jnp.where(first == 1, inflow[rows], from_chunks(entering, g) - ahead)
    states = [state]
    for s in range(stations):
        here = ahead
        ahead = following[rows] if s == stations - 1 else pressure[s + 1, rows]
        t = term[s, rows]
        if s == 0:
            t = t + force[rows]
        state = decay[s, rows] * state + (t - (ahead - here))
        states.append(state)
    return states


def middle_kernel(
    place, entering, pressure, following, decay, term, force, inflow, damping,
    current, decay_new, scale, disc, x0, x1, x2, x3, source,
):
    first = place[1]
    stations, height, _ = current.shape
    for g, rows in groups(height):
        states = march_rows(
            first, g, rows, entering, pressure, following, decay, term, force, inflow
        )
        product = None
        for s in range(stations):
            value = states[s + 1]
            current[s, rows] = value
            source[s, rows] = SOURCE_GAIN * (value - states[s])
            d = decay_of(value, damping[s, rows])
            decay_new[s, rows] = d
            product = d if product is None else product * d
        to_chunks(scale, g, product)
    outs = (x0, x1, x2, x3)
    send_order(place, pl.program_id(0), source, outs)
    send_edges(current, outs)
    disc[...] = current[0].astype(BF16)


def last_kernel(
    place, entering, pressure, following, decay, term, force, inflow, current
):
    first = place[1]
    for g, rows in groups(current.shape[1]):
        states = march_rows(
            first, g, rows, entering, pressure, following, decay, term, force, inflow
        )
        for s in range(current.shape[0]):
            current[s, rows] = states[s + 1]


def cost(flops, size):
    return pl.CostEstimate(flops=int(flops), bytes_accessed=int(size), transcendentals=0)


def near(shape, dtype=F32):
    return pltpu.VMEM(shape, dtype)


def far(shape, dtype=F32):
    return pltpu.HBM(shape, dtype)


def stay(value):
    return pltpu.with_memory_space_constraint(value, pltpu.HBM)


def call(kernel, outs, args, work, scalars=0, limit=8, scratch=()):
    return pl.pallas_call(
        kernel,
        out_shape=outs,
        in_specs=[SMEM] * scalars + [VMEM] * (len(args) - scalars),
        out_specs=[VMEM] * len(outs),
        scratch_shapes=list(scratch),
        compiler_params=pltpu.CompilerParams(vmem_limit_bytes=limit * MIB),
        cost_estimate=work,
    )(*args)


def by_rows(kernel, height, outs, place, args, work, whole=(), scratch=()):
    part = height // STEPS

    def spec(shape, index):
        if index in whole:
            return pl.BlockSpec(shape, lambda i, p: (0,) * len(shape))
        if shape[-1] == LANE and len(shape) == 3:
            return pl.BlockSpec((shape[0] // STEPS,) + shape[1:], lambda i, p: (i, 0, 0))
        if len(shape) == 3:
            return pl.BlockSpec((shape[0], part, shape[2]), lambda i, p: (0, i, 0))
        return pl.BlockSpec((part, shape[1]), lambda i, p: (i, 0))

    count = len(args)
    return pl.pallas_call(
        kernel,
        grid_spec=pltpu.PrefetchScalarGridSpec(
            num_scalar_prefetch=1,
            grid=(STEPS,),
            in_specs=[spec(a.shape, None) for a in args],
            out_specs=[spec(a.inner_aval.shape, i) for i, a in enumerate(outs)],
            scratch_shapes=list(scratch),
        ),
        out_shape=outs,
        compiler_params=pltpu.CompilerParams(vmem_limit_bytes=12 * MIB),
        cost_estimate=work,
    )(place, *args)


def disc_forces(rows, owners, blades):
    height, width = rows[0].shape
    count = len(rows)
    number, half, _ = blades[0].shape
    per_step = 4
    fixed = lambda shape: pl.BlockSpec(shape, lambda i: (0,) * len(shape))
    table = pl.BlockSpec((per_step, half, LANE), lambda i: (i, 0, 0))
    blades = [stay(b) for b in blades]
    return pl.pallas_call(
        disc_kernel,
        grid=(number // per_step,),
        out_shape=[near((height, LANE))] * count,
        in_specs=[fixed((height, width))] * count + [fixed(owners.shape), table, table],
        out_specs=[fixed((height, LANE))] * count,
        scratch_shapes=[
            pltpu.VMEM((count * height, width), BF16),
            pltpu.VMEM((count * height, LANE), F32),
        ],
        compiler_params=pltpu.CompilerParams(vmem_limit_bytes=16 * MIB),
        cost_estimate=cost(2 * number * width * width * LANE, 5 * MIB),
    )(*rows, stay(owners), *blades)


def local(velocity_guess, damping, inflow, disc_rows, owner, blade):
    stations, height, width = velocity_guess.shape
    march_size = lax.axis_size("march")
    cross_size = lax.axis_size("cross")
    march_index = lax.axis_index("march")
    cross_index = lax.axis_index("cross")
    disc_slab = stations * march_size // 2 // stations
    at_disc = march_index == disc_slab
    first = march_index == 0
    place = jnp.stack(
        [
            cross_index.astype(jnp.int32),
            first.astype(jnp.int32),
            (cross_index == 0).astype(jnp.int32),
            (cross_index == cross_size - 1).astype(jnp.int32),
        ]
    )
    tabled = [stay(jnp.asarray(t)) for t in tables(width)]

    slab = (stations, height, width)
    plane = (height, width)
    edged = (height + EDGE, width)
    chunks = (march_size, height * width // march_size // LANE, LANE)
    sources = [near(plane), near(edged), near(plane), near(edged)]

    def turn(value, steps):
        return lax.ppermute(
            value, "cross", [(i, (i + steps) % cross_size) for i in range(cross_size)]
        )

    def turns(blocks, sign=1):
        return [blocks[0]] + [turn(blocks[r], sign * r) for r in range(1, cross_size)]

    def along_march(value, steps):
        count = march_size
        return lax.ppermute(
            value, "march", [(i, i + steps) for i in range(count) if 0 <= i + steps < count]
        )

    def across_march(value):
        return lax.all_to_all(value, "march", split_axis=0, concat_axis=0, tiled=True)

    half = width // 2
    blades = [
        lax.all_gather(blade[:, half * i : half * (i + 1)], "march", axis=0, tiled=True)
        for i in range(2)
    ]
    blocks = (cross_index - jnp.arange(cross_size, dtype=jnp.int32) + cross_size) % cross_size
    ids = (blocks[:, None] * height + jnp.arange(height, dtype=jnp.int32)[None, :]).reshape(-1)
    owners = jnp.max(
        jnp.where(ids[:, None] == disc_rows[None, :], owner[None, :], -1), axis=1
    )
    owners = jnp.where(at_disc, owners, -1)
    owners = jnp.broadcast_to(owners[:, None], (cross_size * height, LANE))

    step = (stations, height // STEPS, width)
    turned = range(4, 8)
    near_inflow = stay(inflow)
    upstream = along_march(velocity_guess[-1], 1)
    current = stay(velocity_guess)
    disc = velocity_guess[0].astype(BF16)
    rows = turns([disc] * cross_size)
    source = by_rows(
        source_kernel,
        height,
        sources,
        place,
        (current, upstream, near_inflow),
        cost(1e6, 2 * MIB),
        whole=range(4),
        scratch=[pltpu.VMEM(step, F32)],
    )
    guess, damp, *source = lax.optimization_barrier((velocity_guess, damping, *source))
    decay, scale = by_rows(
        decay_kernel,
        height,
        [far(slab), far(chunks)],
        place,
        (stay(guess), stay(damp)),
        cost(4e6, 3 * MIB),
    )
    for sweep_index in range(SWEEPS):
        arrived = turns(source)
        scales = across_march(scale)
        if sweep_index > 0:
            disc, *arrived = lax.optimization_barrier((disc, *arrived))
            rows = turns([disc] * cross_size)
        solved = pl.pallas_call(
            solve_kernel,
            out_shape=[near(plane)] * cross_size,
            in_specs=[SMEM] + [VMEM] * cross_size + [pl.BlockSpec(memory_space=pltpu.HBM)] * 3,
            out_specs=[VMEM] * cross_size,
            scratch_shapes=[pltpu.VMEM((width, width), F32)]
            + [pltpu.VMEM((width, width), BF16)] * 2
            + [pltpu.VMEM((width, width), F32), pltpu.SemaphoreType.DMA((3,))],
            compiler_params=pltpu.CompilerParams(vmem_limit_bytes=20 * MIB),
            cost_estimate=cost(3 * 8 * width**3, 5 * MIB),
        )(place, *arrived, *tabled)
        rows, solved = lax.optimization_barrier((rows, solved))
        pieces = turns(solved)
        forces = turns(disc_forces(rows, owners, blades), -1)
        (term,) = call(
            laplace_kernel,
            [far(slab)],
            (place, current, arrived[1], arrived[-1]),
            cost(4e6, 2 * MIB),
            scalars=1,
        )
        decay, term = stay(decay), stay(term)
        pressure, lead, force, offset = by_rows(
            offset_kernel,
            height,
            [far(slab), near(plane), far(plane), far(chunks)],
            place,
            (*pieces, *forces, decay, term, near_inflow),
            cost(4e6, 5 * MIB),
        )
        following = along_march(lead, -1)
        (entering,) = call(
            scan_kernel,
            [far(chunks)],
            (stay(scales), across_march(offset)),
            cost(1e5, MIB),
        )
        entering = across_march(entering)
        common = (entering, stay(pressure), stay(following), decay, term, stay(force), near_inflow)
        if sweep_index == SWEEPS - 1:
            (current,) = by_rows(
                last_kernel, height, [far(slab)], place, common, cost(4e6, 5 * MIB)
            )
            return (current, pressure)
        current, decay, scale, disc, *source = by_rows(
            middle_kernel,
            height,
            [far(slab), far(slab), far(chunks), near(plane, BF16)] + sources,
            place,
            common + (stay(damping),),
            cost(8e6, 8 * MIB),
            whole=turned,
            scratch=[pltpu.VMEM(step, F32)],
        )
        current = stay(current)


def solution(mesh):
    in_specs = (
        P("march", "cross", None),
        P("march", "cross", None),
        P("cross", None),
        P(),
        P(),
        P("march", None, "cross"),
    )
    out_specs = (P("march", "cross", None), P("march", "cross", None))
    return jax.shard_map(local, mesh=mesh, in_specs=in_specs, out_specs=out_specs, check_vma=False)
```

```python
import ml_dtypes
import numpy as np
import jax
import jax.numpy as jnp
from jax import lax
from jax.experimental import pallas as pl
from jax.experimental.pallas import tpu as pltpu
from jax.sharding import PartitionSpec as P

SWEEPS = 2
SOURCE_GAIN = 0.04
SCREENING = 0.001
VISCOSITY = 0.1
DRAG_RATE = 0.01

F32 = jnp.float32
BF16 = jnp.bfloat16
SUB = 8
LANE = 128
EDGE = 8
STEPS = 4
MIB = 1024 * 1024
VMEM = pl.BlockSpec(memory_space=pltpu.VMEM)
SMEM = pl.BlockSpec(memory_space=pltpu.SMEM)


def tables(length):
    ordinal = np.arange(1, length + 1)
    product = np.outer(ordinal, ordinal) % (2 * (length + 1))
    sine = np.sqrt(2.0 / (length + 1)) * np.sin(np.pi * product / (length + 1))
    high = sine.astype(np.float32).astype(ml_dtypes.bfloat16)
    low = (sine - high.astype(np.float64)).astype(np.float32).astype(ml_dtypes.bfloat16)
    values = 2.0 - 2.0 * np.cos(np.pi * ordinal / (length + 1))
    inverse = 1.0 / (SCREENING + values[:, None] + values[None, :])
    return high, low, inverse.astype(np.float32)


def split(value):
    high = value.astype(BF16)
    return high, (value - high.astype(F32)).astype(BF16)


def groups(rows):
    return [(g, slice(SUB * g, SUB * g + SUB)) for g in range(rows // SUB)]


def to_chunks(ref, g, value):
    for h in range(2):
        for q in range(2):
            at = (2 * h + q) * LANE
            ref[2 * g + h, SUB * q : SUB * q + SUB, :] = value[:, at : at + LANE]


def from_chunks(ref, g):
    parts = []
    for h in range(2):
        for q in range(2):
            parts.append(ref[2 * g + h, SUB * q : SUB * q + SUB, :])
    return jnp.concatenate(parts, axis=1)


def decay_of(value, damping):
    return 1.0 - (damping + DRAG_RATE * jnp.abs(value))


def send_order(place, i, source, outs):
    count, height, _ = source.shape
    at = pl.multiple_of(i * height, height)
    for r, ref in enumerate(outs):
        ref[pl.ds(at, height), :] = source[lax.rem(place[0] + r, count)]


def send_edges(current, outs):
    stations, height, width = current.shape
    i = pl.program_id(0)
    total = outs[1].shape[0]
    empty = jnp.zeros((EDGE - stations, width), F32)

    @pl.when(i == pl.num_programs(0) - 1)
    def _():
        rows = [current[s, height - 1 : height] for s in range(stations)]
        outs[1][total - EDGE : total] = jnp.concatenate(rows + [empty], axis=0)

    @pl.when(i == 0)
    def _():
        rows = [current[s, 0:1] for s in range(stations)]
        outs[-1][total - EDGE : total] = jnp.concatenate(rows + [empty], axis=0)


def source_kernel(place, current, upstream, inflow, x0, x1, x2, x3, source):
    stations, height, _ = current.shape
    for _, rows in groups(height):
        previous = jnp.where(place[1] == 1, inflow[rows], upstream[rows])
        for s in range(stations):
            here = current[s, rows]
            source[s, rows] = SOURCE_GAIN * (here - previous)
            previous = here
    outs = (x0, x1, x2, x3)
    send_order(place, pl.program_id(0), source, outs)
    send_edges(current, outs)


def decay_kernel(place, current, damping, decay, scale):
    for g, rows in groups(current.shape[1]):
        product = None
        for s in range(current.shape[0]):
            d = decay_of(current[s, rows], damping[s, rows])
            decay[s, rows] = d
            product = d if product is None else product * d
        to_chunks(scale, g, product)


def weights_kernel(
    place, current, before, after, decay, inflow, term, weights, base, force_weight
):
    stations, height, width = current.shape
    first = place[1] == 1
    above = jnp.where(place[2] == 1, 0.0, before[height : height + EDGE])
    below = jnp.where(place[3] == 1, 0.0, after[height : height + EDGE])
    lane = lax.broadcasted_iota(jnp.int32, (SUB, width), 1)
    for g, rows in groups(height):
        lo, hi = SUB * g, SUB * g + SUB
        total = jnp.zeros((SUB, width), F32)
        factor = None
        for s in reversed(range(stations)):
            here = current[s, rows]
            if g == 0:
                up = jnp.concatenate([above[s : s + 1], current[s, 0 : SUB - 1]], axis=0)
            else:
                up = current[s, lo - 1 : hi - 1]
            if hi == height:
                down = jnp.concatenate([current[s, lo + 1 : hi], below[s : s + 1]], axis=0)
            else:
                down = current[s, lo + 1 : hi + 1]
            left = jnp.where(lane == 0, 0.0, pltpu.roll(here, 1, 1))
            right = jnp.where(lane == width - 1, 0.0, pltpu.roll(here, width - 1, 1))
            t = VISCOSITY * (up + down + left + right - 4.0 * here)
            term[s, rows] = t
            d = decay[s, rows]
            if factor is None:
                total, weight, factor = t, 1.0 - d, d
            else:
                if s == 0:
                    force_weight[rows] = factor
                total, weight, factor = total + factor * t, factor * (1.0 - d), factor * d
            if s == 0:
                entry = jnp.where(first, factor, 0.0)
                weight = weight + entry
                total = total + entry * inflow[rows]
            weights[s, rows] = weight
        base[rows] = total


def solve_kernel(place, x0, x1, x2, x3, high_far, low_far, inverse_far, *rest):
    *forces, p0, p1, p2, p3, plane, high, low, inverse, arrivals = rest
    c = place[0]
    copies = [
        pltpu.make_async_copy(far_ref, ref, arrivals.at[i])
        for i, (far_ref, ref) in enumerate(
            ((high_far, high), (low_far, low), (inverse_far, inverse))
        )
    ]
    for copy in copies:
        copy.start()
    inputs, outputs = (x0, x1, x2, x3), (p0, p1, p2, p3)
    count = len(inputs)
    height = x0.shape[0]
    for r, ref in enumerate(inputs):
        b = lax.rem(c - r + count, count)
        plane[pl.ds(pl.multiple_of(b * height, height), height), :] = ref[0:height]
    copies[0].wait()
    copies[1].wait()
    sh, sl = high[...], low[...]
    by_left = jnp.concatenate([sh, sh, sl], axis=1)
    by_right = jnp.concatenate([sh, sl, sh], axis=0)

    def right(value):
        vh, vl = split(value)
        return jnp.dot(
            jnp.concatenate([vh, vh, vl], axis=1), by_right, preferred_element_type=F32
        )

    def left(value):
        vh, vl = split(value)
        return jnp.dot(
            by_left, jnp.concatenate([vh, vl, vh], axis=0), preferred_element_type=F32
        )

    modes = left(right(plane[...]))
    copies[2].wait()
    modes = modes * inverse[...]
    plane[...] = right(left(modes))
    for r, ref in enumerate(outputs):
        b = lax.rem(c + r, count)
        ref[0:height] = plane[pl.ds(pl.multiple_of(b * height, height), height), :]
    if forces:
        extra = p0.shape[0] - height
        for r, ref in enumerate(outputs):
            for q in range(height // extra):
                ref[height : height + extra, LANE * q : LANE * (q + 1)] = forces[-r][
                    extra * q : extra * (q + 1)
                ]


def disc_kernel(d0, d1, d2, d3, owners, *rest):
    *blades, f0, f1, f2, f3, plane, total = rest
    step = pl.program_id(0)
    height = d0.shape[0]

    @pl.when(step == 0)
    def _():
        for r, ref in enumerate((d0, d1, d2, d3)):
            plane[height * r : height * (r + 1)] = ref[...]
        total[...] = jnp.zeros_like(total)

    per_step = blades[0].shape[0]
    for i in range(0, per_step, 2):
        pair = jnp.concatenate(
            [
                jnp.concatenate([blade[j] for blade in blades], axis=0)
                for j in (i, i + 1)
            ],
            axis=1,
        )
        response = jnp.dot(plane[...], pair, preferred_element_type=F32)
        first = step * per_step + i
        kept = jnp.where(owners[...] == first, response[:, :LANE], total[...])
        total[...] = jnp.where(owners[...] == first + 1, response[:, LANE:], kept)

    @pl.when(step == pl.num_programs(0) - 1)
    def _():
        for r, ref in enumerate((f0, f1, f2, f3)):
            ref[...] = jnp.tanh(total[height * r : height * (r + 1)])


def offset_kernel(place, *rest):
    c = place[0]
    pieces = rest[:4]
    *forces, weights, base, force_weight, lead, lead_far, force, offset = rest[4:]
    count, height, full = weights.shape
    width = full // count
    for r in range(count):
        b = lax.rem(c + r if forces else c - r + count, count)
        lanes = pl.ds(pl.multiple_of(b * width, width), width)
        if forces:
            force[:, lanes] = forces[r][...]
        else:
            extra = pieces[r].shape[0] - height
            for q in range(height // extra):
                force[extra * q : extra * (q + 1), lanes] = pieces[r][
                    height : height + extra, width * q : width * (q + 1)
                ]

    for r in range(count):
        @pl.when(c == r)
        def _():
            lead[...] = pieces[r][0:height]
            lead_far[...] = pieces[r][0:height]

    for g, rows in groups(height):
        state = base[rows] + force_weight[rows] * force[rows]
        for r in range(count):
            s = lax.rem(c - r + count, count)
            state = state + weights[s, rows] * pieces[r][rows]
        to_chunks(offset, g, state)


def change_kernel(place, p0, p1, p2, p3, term, force, change, pressure):
    c = place[0]
    pieces = (p0, p1, p2, p3)
    count, height, _ = term.shape
    for r in range(count):
        pressure[lax.rem(c - r + count, count)] = pieces[r][...]
    for _, rows in groups(height):
        here = pressure[0, rows]
        for s in range(count):
            value = term[s, rows] + here
            if s == 0:
                value = value + force[rows]
            if s < count - 1:
                here = pressure[s + 1, rows]
                value = value - here
            change[s, rows] = value


def scan_kernel(scale, offset, entering):
    entering[0] = jnp.zeros_like(entering[0])
    state = offset[0]
    for m in range(1, scale.shape[0]):
        entering[m] = state
        state = scale[m] * state + offset[m]


def march_rows(first, g, rows, entering, change, following, decay, lead, inflow):
    stations = decay.shape[0]
    state = jnp.where(first == 1, inflow[rows], from_chunks(entering, g) - lead[rows])
    states = [state]
    for s in range(stations):
        step = change[s, rows]
        if s == stations - 1:
            step = step - following[rows]
        state = decay[s, rows] * state + step
        states.append(state)
    return states


def middle_kernel(
    place, entering, change, following, decay, lead, inflow, damping,
    current, decay_new, scale, disc, x0, x1, x2, x3, source,
):
    first = place[1]
    stations, height, _ = current.shape
    for g, rows in groups(height):
        states = march_rows(first, g, rows, entering, change, following, decay, lead, inflow)
        product = None
        for s in range(stations):
            value = states[s + 1]
            current[s, rows] = value
            source[s, rows] = SOURCE_GAIN * (value - states[s])
            d = decay_of(value, damping[s, rows])
            decay_new[s, rows] = d
            product = d if product is None else product * d
        to_chunks(scale, g, product)
    outs = (x0, x1, x2, x3)
    send_order(place, pl.program_id(0), source, outs)
    send_edges(current, outs)
    disc[...] = current[0].astype(BF16)


def last_kernel(place, entering, change, following, decay, lead, inflow, current):
    first = place[1]
    for g, rows in groups(current.shape[1]):
        states = march_rows(first, g, rows, entering, change, following, decay, lead, inflow)
        for s in range(current.shape[0]):
            current[s, rows] = states[s + 1]


def cost(flops, size):
    return pl.CostEstimate(flops=int(flops), bytes_accessed=int(size), transcendentals=0)


def near(shape, dtype=F32):
    return pltpu.VMEM(shape, dtype)


def far(shape, dtype=F32):
    return pltpu.HBM(shape, dtype)


def stay(value):
    return pltpu.with_memory_space_constraint(value, pltpu.HBM)


def call(kernel, outs, args, work, scalars=0, limit=8, scratch=()):
    return pl.pallas_call(
        kernel,
        out_shape=outs,
        in_specs=[SMEM] * scalars + [VMEM] * (len(args) - scalars),
        out_specs=[VMEM] * len(outs),
        scratch_shapes=list(scratch),
        compiler_params=pltpu.CompilerParams(vmem_limit_bytes=limit * MIB),
        cost_estimate=work,
    )(*args)


def by_rows(kernel, height, outs, place, args, work, whole=(), scratch=()):
    part = height // STEPS

    def spec(shape, index):
        if index in whole:
            return pl.BlockSpec(shape, lambda i, p: (0,) * len(shape))
        if shape[-1] == LANE and len(shape) == 3:
            return pl.BlockSpec((shape[0] // STEPS,) + shape[1:], lambda i, p: (i, 0, 0))
        if len(shape) == 3:
            return pl.BlockSpec((shape[0], part, shape[2]), lambda i, p: (0, i, 0))
        return pl.BlockSpec((part, shape[1]), lambda i, p: (i, 0))

    count = len(args)
    return pl.pallas_call(
        kernel,
        grid_spec=pltpu.PrefetchScalarGridSpec(
            num_scalar_prefetch=1,
            grid=(STEPS,),
            in_specs=[spec(a.shape, None) for a in args],
            out_specs=[spec(a.inner_aval.shape, i) for i, a in enumerate(outs)],
            scratch_shapes=list(scratch),
        ),
        out_shape=outs,
        compiler_params=pltpu.CompilerParams(vmem_limit_bytes=12 * MIB),
        cost_estimate=work,
    )(place, *args)


def disc_forces(rows, owners, blades):
    height, width = rows[0].shape
    count = len(rows)
    number = blades.shape[0]
    per_step, streams = 8, 4
    fixed = lambda shape: pl.BlockSpec(shape, lambda i: (0,) * len(shape))
    table = lambda k: pl.BlockSpec((per_step, width // streams, LANE), lambda i: (i, k, 0))
    return pl.pallas_call(
        disc_kernel,
        grid=(number // per_step,),
        out_shape=[near((height, LANE))] * count,
        in_specs=[fixed((height, width))] * count
        + [fixed(owners.shape)]
        + [table(k) for k in range(streams)],
        out_specs=[fixed((height, LANE))] * count,
        scratch_shapes=[
            pltpu.VMEM((count * height, width), BF16),
            pltpu.VMEM((count * height, LANE), F32),
        ],
        compiler_params=pltpu.CompilerParams(vmem_limit_bytes=16 * MIB),
        cost_estimate=cost(2 * number * width * width * LANE, 5 * MIB),
    )(*rows, stay(owners), *[stay(blades)] * streams)


def local(velocity_guess, damping, inflow, disc_rows, owner, blade):
    stations, height, width = velocity_guess.shape
    march_size = lax.axis_size("march")
    cross_size = lax.axis_size("cross")
    march_index = lax.axis_index("march")
    cross_index = lax.axis_index("cross")
    disc_slab = stations * march_size // 2 // stations
    at_disc = march_index == disc_slab
    first = march_index == 0
    place = jnp.stack(
        [
            cross_index.astype(jnp.int32),
            first.astype(jnp.int32),
            (cross_index == 0).astype(jnp.int32),
            (cross_index == cross_size - 1).astype(jnp.int32),
        ]
    )
    tabled = [stay(jnp.asarray(t)) for t in tables(width)]

    slab = (stations, height, width)
    plane = (height, width)
    edged = (height + EDGE, width)
    chunks = (march_size, height * width // march_size // LANE, LANE)
    sources = [near(plane), near(edged), near(plane), near(edged)]

    def turn(value, steps):
        return lax.ppermute(
            value, "cross", [(i, (i + steps) % cross_size) for i in range(cross_size)]
        )

    def turns(blocks, sign=1):
        return [blocks[0]] + [turn(blocks[r], sign * r) for r in range(1, cross_size)]

    def along_march(value, steps):
        count = march_size
        return lax.ppermute(
            value, "march", [(i, i + steps) for i in range(count) if 0 <= i + steps < count]
        )

    def across_march(value):
        return lax.all_to_all(value, "march", split_axis=0, concat_axis=0, tiled=True)

    blades = lax.all_gather(blade, "march", axis=0, tiled=True)
    blocks = (cross_index - jnp.arange(cross_size, dtype=jnp.int32) + cross_size) % cross_size
    ids = (blocks[:, None] * height + jnp.arange(height, dtype=jnp.int32)[None, :]).reshape(-1)
    owners = jnp.max(
        jnp.where(ids[:, None] == disc_rows[None, :], owner[None, :], -1), axis=1
    )
    owners = jnp.where(at_disc, owners, -1)
    owners = jnp.broadcast_to(owners[:, None], (cross_size * height, LANE))

    step = (stations, height // STEPS, width)
    turned = range(4, 8)
    near_inflow = stay(inflow)
    upstream = along_march(velocity_guess[-1], 1)
    current = stay(velocity_guess)
    disc = velocity_guess[0].astype(BF16)
    rows = turns([disc] * cross_size)
    source = by_rows(
        source_kernel,
        height,
        sources,
        place,
        (current, upstream, near_inflow),
        cost(1e6, 2 * MIB),
        whole=range(4),
        scratch=[pltpu.VMEM(step, F32)],
    )
    guess, damp, *source = lax.optimization_barrier((velocity_guess, damping, *source))
    decay, scale = by_rows(
        decay_kernel,
        height,
        [far(slab), far(chunks)],
        place,
        (stay(guess), stay(damp)),
        cost(4e6, 3 * MIB),
    )
    for sweep_index in range(SWEEPS):
        merged = sweep_index > 0
        final = sweep_index == SWEEPS - 1
        if merged:
            rows = turns([disc] * cross_size)
        arrived = turns(source)
        extra = []
        piece = plane
        if not merged:
            scales = across_march(scale)
        if merged:
            extra = disc_forces(rows, owners, blades)
            piece = (height + height * LANE // width, width)
        solved = pl.pallas_call(
            solve_kernel,
            out_shape=[near(piece)] * cross_size,
            in_specs=[SMEM]
            + [VMEM] * cross_size
            + [pl.BlockSpec(memory_space=pltpu.HBM)] * 3
            + [VMEM] * len(extra),
            out_specs=[VMEM] * cross_size,
            scratch_shapes=[pltpu.VMEM((width, width), F32)]
            + [pltpu.VMEM((width, width), BF16)] * 2
            + [pltpu.VMEM((width, width), F32), pltpu.SemaphoreType.DMA((3,))],
            compiler_params=pltpu.CompilerParams(vmem_limit_bytes=20 * MIB),
            cost_estimate=cost(3 * 8 * width**3, 5 * MIB),
        )(place, *arrived, *tabled, *extra)
        forces = []
        if merged:
            scales = across_march(scale)
        else:
            rows, scales, solved = lax.optimization_barrier((rows, scales, solved))
            forces = turns(disc_forces(rows, owners, blades), -1)
        pieces = turns(solved)
        decay = stay(decay)
        term, weights, base, force_weight = call(
            weights_kernel,
            [far(slab), near(slab), near(plane), near(plane)],
            (place, current, arrived[1], arrived[-1], decay, near_inflow),
            cost(8e6, 4 * MIB),
            scalars=1,
            limit=12,
        )
        lead, lead_far, force, offset = call(
            offset_kernel,
            [near(plane), far(plane), far(plane), far(chunks)],
            (place, *pieces, *forces, weights, base, force_weight),
            cost(2e6, 3 * MIB),
            scalars=1,
            limit=12,
        )
        following = along_march(lead, -1)
        offset, force, *pieces = lax.optimization_barrier((offset, force, *pieces))
        change, pressure = by_rows(
            change_kernel,
            height,
            [far(slab), far(slab)],
            place,
            (*pieces, stay(term), stay(force)),
            cost(4e6, 4 * MIB),
        )
        (entering,) = call(
            scan_kernel, [far(chunks)], (scales, across_march(offset)), cost(1e5, MIB)
        )
        entering = across_march(entering)
        common = (entering, stay(change), stay(following), decay, stay(lead_far), near_inflow)
        if final:
            (current,) = by_rows(
                last_kernel, height, [far(slab)], place, common, cost(4e6, 5 * MIB)
            )
            return (current, pressure)
        current, decay, scale, disc, *source = by_rows(
            middle_kernel,
            height,
            [far(slab), far(slab), far(chunks), near(plane, BF16)] + sources,
            place,
            common + (stay(damping),),
            cost(8e6, 8 * MIB),
            whole=turned,
            scratch=[pltpu.VMEM(step, F32)],
        )
        current = stay(current)


def solution(mesh):
    in_specs = (
        P("march", "cross", None),
        P("march", "cross", None),
        P("cross", None),
        P(),
        P(),
        P("march", None, "cross"),
    )
    out_specs = (P("march", "cross", None), P("march", "cross", None))
    return jax.shard_map(local, mesh=mesh, in_specs=in_specs, out_specs=out_specs, check_vma=False)
```

```python
import ml_dtypes
import numpy as np
import jax
import jax.numpy as jnp
from jax import lax
from jax.experimental import pallas as pl
from jax.experimental.pallas import tpu as pltpu
from jax.sharding import Mesh, PartitionSpec as P

SWEEPS = 2
SOURCE_GAIN = 0.04
SCREENING = 0.001
VISCOSITY = 0.1
DRAG_RATE = 0.01

MARCH = ("chip", "core")
F32 = jnp.float32
BF16 = jnp.bfloat16
SUB = 8
LANE = 128
EDGE = 8
STEPS = 4
MIB = 1024 * 1024
VMEM = pl.BlockSpec(memory_space=pltpu.VMEM)
SMEM = pl.BlockSpec(memory_space=pltpu.SMEM)


def tables(length):
    ordinal = np.arange(1, length + 1)
    product = np.outer(ordinal, ordinal) % (2 * (length + 1))
    sine = np.sqrt(2.0 / (length + 1)) * np.sin(np.pi * product / (length + 1))
    high = sine.astype(np.float32).astype(ml_dtypes.bfloat16)
    low = (sine - high.astype(np.float64)).astype(np.float32).astype(ml_dtypes.bfloat16)
    values = 2.0 - 2.0 * np.cos(np.pi * ordinal / (length + 1))
    inverse = 1.0 / (SCREENING + values[:, None] + values[None, :])
    return high, low, inverse.astype(np.float32)


def split(value):
    high = value.astype(BF16)
    return high, (value - high.astype(F32)).astype(BF16)


def groups(rows):
    return [(g, slice(SUB * g, SUB * g + SUB)) for g in range(rows // SUB)]


def to_chunks(ref, g, value, base=0):
    for h in range(2):
        for q in range(2):
            at = (2 * h + q) * LANE
            ref[2 * g + h, base + SUB * q : base + SUB * q + SUB, :] = value[:, at : at + LANE]


def from_chunks(ref, g):
    parts = []
    for h in range(2):
        for q in range(2):
            parts.append(ref[2 * g + h, SUB * q : SUB * q + SUB, :])
    return jnp.concatenate(parts, axis=1)


def decay_of(value, damping):
    return 1.0 - (damping + DRAG_RATE * jnp.abs(value))


def send_order(place, i, source, outs):
    count, height, _ = source.shape
    at = pl.multiple_of(i * height, height)
    for r, ref in enumerate(outs):
        ref[pl.ds(at, height), :] = source[lax.rem(place[0] + r, count)]


def send_edges(current, outs):
    stations, height, width = current.shape
    i = pl.program_id(0)
    total = outs[1].shape[0]
    empty = jnp.zeros((EDGE - stations, width), F32)

    @pl.when(i == pl.num_programs(0) - 1)
    def _():
        rows = [current[s, height - 1 : height] for s in range(stations)]
        outs[1][total - EDGE : total] = jnp.concatenate(rows + [empty], axis=0)

    @pl.when(i == 0)
    def _():
        rows = [current[s, 0:1] for s in range(stations)]
        outs[-1][total - EDGE : total] = jnp.concatenate(rows + [empty], axis=0)


def source_kernel(place, current, upstream, inflow, x0, x1, x2, x3, source):
    stations, height, _ = current.shape
    for _, rows in groups(height):
        previous = jnp.where(place[1] == 1, inflow[rows], upstream[rows])
        for s in range(stations):
            here = current[s, rows]
            source[s, rows] = SOURCE_GAIN * (here - previous)
            previous = here
    outs = (x0, x1, x2, x3)
    send_order(place, pl.program_id(0), source, outs)
    send_edges(current, outs)


def weights_kernel(
    place, current, before, after, damping, inflow,
    term, decay, weights, base, force_weight, scale,
):
    stations, height, width = current.shape
    first = place[1] == 1
    above = jnp.where(place[2] == 1, 0.0, before[height : height + EDGE])
    below = jnp.where(place[3] == 1, 0.0, after[height : height + EDGE])
    lane = lax.broadcasted_iota(jnp.int32, (SUB, width), 1)
    for g, rows in groups(height):
        lo, hi = SUB * g, SUB * g + SUB
        total = jnp.zeros((SUB, width), F32)
        factor = None
        for s in reversed(range(stations)):
            here = current[s, rows]
            if g == 0:
                up = jnp.concatenate([above[s : s + 1], current[s, 0 : SUB - 1]], axis=0)
            else:
                up = current[s, lo - 1 : hi - 1]
            if hi == height:
                down = jnp.concatenate([current[s, lo + 1 : hi], below[s : s + 1]], axis=0)
            else:
                down = current[s, lo + 1 : hi + 1]
            left = jnp.where(lane == 0, 0.0, pltpu.roll(here, 1, 1))
            right = jnp.where(lane == width - 1, 0.0, pltpu.roll(here, width - 1, 1))
            t = VISCOSITY * (up + down + left + right - 4.0 * here)
            term[s, rows] = t
            d = decay_of(here, damping[s, rows])
            decay[s, rows] = d
            if factor is None:
                total, weight, factor = t, 1.0 - d, d
            else:
                if s == 0:
                    force_weight[rows] = factor
                total, weight, factor = total + factor * t, factor * (1.0 - d), factor * d
            if s == 0:
                entry = jnp.where(first, factor, 0.0)
                weight = weight + entry
                total = total + entry * inflow[rows]
            weights[s, rows] = weight
        base[rows] = total
        scale[rows] = factor


def solve_kernel(
    place, x0, x1, x2, x3, high_far, low_far, inverse_far, p0, p1, p2, p3,
    plane, high, low, inverse, arrivals,
):
    c = place[0]
    copies = [
        pltpu.make_async_copy(far_ref, ref, arrivals.at[i])
        for i, (far_ref, ref) in enumerate(
            ((high_far, high), (low_far, low), (inverse_far, inverse))
        )
    ]
    for copy in copies:
        copy.start()
    inputs, outputs = (x0, x1, x2, x3), (p0, p1, p2, p3)
    count = len(inputs)
    height = x0.shape[0]
    for r, ref in enumerate(inputs):
        b = lax.rem(c - r + count, count)
        plane[pl.ds(pl.multiple_of(b * height, height), height), :] = ref[0:height]
    copies[0].wait()
    copies[1].wait()
    sh, sl = high[...], low[...]
    by_left = jnp.concatenate([sh, sh, sl], axis=1)
    by_right = jnp.concatenate([sh, sl, sh], axis=0)

    def right(value):
        vh, vl = split(value)
        return jnp.dot(
            jnp.concatenate([vh, vh, vl], axis=1), by_right, preferred_element_type=F32
        )

    def left(value):
        vh, vl = split(value)
        return jnp.dot(
            by_left, jnp.concatenate([vh, vl, vh], axis=0), preferred_element_type=F32
        )

    modes = left(right(plane[...]))
    copies[2].wait()
    modes = modes * inverse[...]
    plane[...] = right(left(modes))
    for r, ref in enumerate(outputs):
        b = lax.rem(c + r, count)
        ref[...] = plane[pl.ds(pl.multiple_of(b * height, height), height), :]


def disc_kernel(d0, d1, d2, d3, owners, *rest):
    *blades, forces, plane, total = rest
    step = pl.program_id(0)
    height = d0.shape[0]

    @pl.when(step == 0)
    def _():
        for r, ref in enumerate((d0, d1, d2, d3)):
            plane[height * r : height * (r + 1)] = ref[...]
        total[...] = jnp.zeros_like(total)

    per_step = blades[0].shape[0]
    for i in range(0, per_step, 2):
        pair = jnp.concatenate(
            [
                jnp.concatenate([blade[j] for blade in blades], axis=0)
                for j in (i, i + 1)
            ],
            axis=1,
        )
        response = jnp.dot(plane[...], pair, preferred_element_type=F32)
        first = step * per_step + i
        kept = jnp.where(owners[...] == first, response[:, :LANE], total[...])
        total[...] = jnp.where(owners[...] == first + 1, response[:, LANE:], kept)

    @pl.when(step == pl.num_programs(0) - 1)
    def _():
        forces[...] = jnp.tanh(total[...])


def share_kernel(place, own, other, f0, f1, f2, f3):
    height = f0.shape[0]
    for r, ref in enumerate((f0, f1, f2, f3)):
        rows = slice(height * r, height * (r + 1))
        ref[...] = jnp.where(place[4] == 1, own[rows] + other[rows], 0.0)


def partial_kernel(place, p0, p1, p2, p3, weights, base, lead, lead_far, state):
    c = place[0]
    pieces = (p0, p1, p2, p3)
    count, height, _ = weights.shape
    for r in range(count):
        @pl.when(c == r)
        def _():
            lead[...] = pieces[r][...]
            lead_far[...] = pieces[r][...]

    for _, rows in groups(height):
        total = base[rows]
        for r in range(count):
            s = lax.rem(c - r + count, count)
            total = total + weights[s, rows] * pieces[r][rows]
        state[rows] = total


def offset_kernel(place, f0, f1, f2, f3, state, force_weight, scale, force, chunks):
    c = place[0]
    forces = (f0, f1, f2, f3)
    count = len(forces)
    height, full = state.shape
    width = full // count
    for r in range(count):
        b = lax.rem(c + r, count)
        force[:, pl.ds(pl.multiple_of(b * width, width), width)] = forces[r][...]
    for g, rows in groups(height):
        to_chunks(chunks, g, state[rows] + force_weight[rows] * force[rows])
        to_chunks(chunks, g, scale[rows], chunks.shape[1] // 2)


def change_kernel(place, p0, p1, p2, p3, term, force, change, pressure):
    c = place[0]
    pieces = (p0, p1, p2, p3)
    count, height, _ = term.shape
    for r in range(count):
        pressure[lax.rem(c - r + count, count)] = pieces[r][...]
    for _, rows in groups(height):
        here = pressure[0, rows]
        for s in range(count):
            value = term[s, rows] + here
            if s == 0:
                value = value + force[rows]
            if s < count - 1:
                here = pressure[s + 1, rows]
                value = value - here
            change[s, rows] = value


def scan_kernel(chunks, entering):
    half = entering.shape[1]
    entering[0] = jnp.zeros_like(entering[0])
    state = chunks[0, 0:half]
    for m in range(1, chunks.shape[0]):
        entering[m] = state
        state = chunks[m, half : 2 * half] * state + chunks[m, 0:half]


def march_rows(first, g, rows, entering, change, following, decay, lead, inflow):
    stations = decay.shape[0]
    state = jnp.where(first == 1, inflow[rows], from_chunks(entering, g) - lead[rows])
    states = [state]
    for s in range(stations):
        step = change[s, rows]
        if s == stations - 1:
            step = step - following[rows]
        state = decay[s, rows] * state + step
        states.append(state)
    return states


def middle_kernel(
    place, entering, change, following, decay, lead, inflow,
    current, disc, x0, x1, x2, x3, source,
):
    first = place[1]
    stations, height, _ = current.shape
    for g, rows in groups(height):
        states = march_rows(first, g, rows, entering, change, following, decay, lead, inflow)
        for s in range(stations):
            current[s, rows] = states[s + 1]
            source[s, rows] = SOURCE_GAIN * (states[s + 1] - states[s])
    outs = (x0, x1, x2, x3)
    send_order(place, pl.program_id(0), source, outs)
    send_edges(current, outs)
    disc[...] = current[0].astype(BF16)


def last_kernel(place, entering, change, following, decay, lead, inflow, current):
    first = place[1]
    for g, rows in groups(current.shape[1]):
        states = march_rows(first, g, rows, entering, change, following, decay, lead, inflow)
        for s in range(current.shape[0]):
            current[s, rows] = states[s + 1]


def cost(flops, size):
    return pl.CostEstimate(flops=int(flops), bytes_accessed=int(size), transcendentals=0)


def near(shape, dtype=F32):
    return pltpu.VMEM(shape, dtype)


def far(shape, dtype=F32):
    return pltpu.HBM(shape, dtype)


def stay(value):
    return pltpu.with_memory_space_constraint(value, pltpu.HBM)


def call(kernel, outs, args, work, scalars=0, limit=8, scratch=()):
    return pl.pallas_call(
        kernel,
        out_shape=outs,
        in_specs=[SMEM] * scalars + [VMEM] * (len(args) - scalars),
        out_specs=[VMEM] * len(outs),
        scratch_shapes=list(scratch),
        compiler_params=pltpu.CompilerParams(vmem_limit_bytes=limit * MIB),
        cost_estimate=work,
    )(*args)


def by_rows(kernel, height, outs, place, args, work, whole=(), scratch=()):
    part = height // STEPS

    def spec(shape, index):
        if index in whole:
            return pl.BlockSpec(shape, lambda i, p: (0,) * len(shape))
        if shape[-1] == LANE and len(shape) == 3:
            return pl.BlockSpec((shape[0] // STEPS,) + shape[1:], lambda i, p: (i, 0, 0))
        if len(shape) == 3:
            return pl.BlockSpec((shape[0], part, shape[2]), lambda i, p: (0, i, 0))
        return pl.BlockSpec((part, shape[1]), lambda i, p: (i, 0))

    count = len(args)
    return pl.pallas_call(
        kernel,
        grid_spec=pltpu.PrefetchScalarGridSpec(
            num_scalar_prefetch=1,
            grid=(STEPS,),
            in_specs=[spec(a.shape, None) for a in args],
            out_specs=[spec(a.inner_aval.shape, i) for i, a in enumerate(outs)],
            scratch_shapes=list(scratch),
        ),
        out_shape=outs,
        compiler_params=pltpu.CompilerParams(vmem_limit_bytes=12 * MIB),
        cost_estimate=work,
    )(place, *args)


def disc_forces(rows, owners, blades):
    height, width = rows[0].shape
    count = len(rows)
    number = blades.shape[0]
    per_step, streams = 8, 4
    fixed = lambda shape: pl.BlockSpec(shape, lambda i: (0,) * len(shape))
    table = lambda k: pl.BlockSpec((per_step, width // streams, LANE), lambda i: (i, k, 0))
    return pl.pallas_call(
        disc_kernel,
        grid=(number // per_step,),
        out_shape=near((count * height, LANE)),
        in_specs=[fixed((height, width))] * count
        + [fixed(owners.shape)]
        + [table(k) for k in range(streams)],
        out_specs=fixed((count * height, LANE)),
        scratch_shapes=[
            pltpu.VMEM((count * height, width), BF16),
            pltpu.VMEM((count * height, LANE), F32),
        ],
        compiler_params=pltpu.CompilerParams(vmem_limit_bytes=16 * MIB),
        cost_estimate=cost(1, 1),
    )(*rows, stay(owners), *[stay(blades)] * streams)


def local(velocity_guess, damping, inflow, disc_rows, owner, blade):
    stations, height, width = velocity_guess.shape
    cores = lax.axis_size("core")
    march_size = lax.axis_size("chip") * cores
    cross_size = lax.axis_size("cross")
    chip_index = lax.axis_index("chip")
    core_index = lax.axis_index("core")
    march_index = chip_index * cores + core_index
    cross_index = lax.axis_index("cross")
    disc_slab = stations * march_size // 2 // stations
    at_disc = march_index == disc_slab
    first = march_index == 0
    place = jnp.stack(
        [
            cross_index.astype(jnp.int32),
            first.astype(jnp.int32),
            (cross_index == 0).astype(jnp.int32),
            (cross_index == cross_size - 1).astype(jnp.int32),
            at_disc.astype(jnp.int32),
        ]
    )
    tabled = [stay(jnp.asarray(t)) for t in tables(width)]

    slab = (stations, height, width)
    plane = (height, width)
    edged = (height + EDGE, width)
    chunks = (march_size, height * width // march_size // LANE, LANE)
    sources = [near(plane), near(edged), near(plane), near(edged)]

    def turn(value, steps):
        return lax.ppermute(
            value, "cross", [(i, (i + steps) % cross_size) for i in range(cross_size)]
        )

    def turns(blocks, sign=1):
        return [blocks[0]] + [turn(blocks[r], sign * r) for r in range(1, cross_size)]

    def along_march(value, steps):
        count = march_size
        return lax.ppermute(
            value, MARCH, [(i, i + steps) for i in range(count) if 0 <= i + steps < count]
        )

    def across_march(value):
        return lax.all_to_all(value, MARCH, split_axis=0, concat_axis=0, tiled=True)

    def swap(value):
        return lax.ppermute(value, "core", [(i, (i + 1) % cores) for i in range(cores)])

    def share(value):
        return jnp.where(core_index == disc_slab % cores, value, swap(value))

    blades = lax.all_gather(blade, "chip", axis=0, tiled=True)
    blocks = (cross_index - jnp.arange(cross_size, dtype=jnp.int32) + cross_size) % cross_size
    ids = (blocks[:, None] * height + jnp.arange(height, dtype=jnp.int32)[None, :]).reshape(-1)
    owners = jnp.max(
        jnp.where(ids[:, None] == disc_rows[None, :], owner[None, :], -1), axis=1
    )
    here = (chip_index == disc_slab // cores) & (owners % cores == core_index)
    owners = jnp.where(here & (owners >= 0), owners // cores, -1)
    owners = jnp.broadcast_to(owners[:, None], (cross_size * height, LANE))

    step = (stations, height // STEPS, width)
    turned = range(2, 6)
    near_inflow = stay(inflow)
    upstream = along_march(velocity_guess[-1], 1)
    current = stay(velocity_guess)
    disc = velocity_guess[0].astype(BF16)
    rows = turns([share(disc)] * cross_size)
    source = by_rows(
        source_kernel,
        height,
        sources,
        place,
        (current, upstream, near_inflow),
        cost(1e6, 2 * MIB),
        whole=range(4),
        scratch=[pltpu.VMEM(step, F32)],
    )
    for sweep_index in range(SWEEPS):
        final = sweep_index == SWEEPS - 1
        arrived = turns(source)
        if sweep_index > 0:
            rows = turns([share(disc)] * cross_size)
        solved = pl.pallas_call(
            solve_kernel,
            out_shape=[near(plane)] * cross_size,
            in_specs=[SMEM] + [VMEM] * cross_size + [pl.BlockSpec(memory_space=pltpu.HBM)] * 3,
            out_specs=[VMEM] * cross_size,
            scratch_shapes=[pltpu.VMEM((width, width), F32)]
            + [pltpu.VMEM((width, width), BF16)] * 2
            + [pltpu.VMEM((width, width), F32), pltpu.SemaphoreType.DMA((3,))],
            compiler_params=pltpu.CompilerParams(vmem_limit_bytes=20 * MIB),
            cost_estimate=cost(3 * 8 * width**3, 5 * MIB),
        )(place, *arrived, *tabled)
        rows, solved = lax.optimization_barrier((rows, solved))
        pieces = turns(solved)
        part = disc_forces(rows, owners, blades)
        forces = call(
            share_kernel,
            [near((height, LANE))] * cross_size,
            (place, part, swap(part)),
            cost(1, 1),
            scalars=1,
        )
        forces = turns(forces, -1)
        term, decay, weights, base, force_weight, scale = call(
            weights_kernel,
            [far(slab), far(slab), near(slab), near(plane), near(plane), near(plane)],
            (place, current, arrived[1], arrived[-1], stay(damping), near_inflow),
            cost(1, 1),
            scalars=1,
            limit=12,
        )
        lead, lead_far, state = call(
            partial_kernel,
            [near(plane), far(plane), near(plane)],
            (place, *pieces, weights, base),
            cost(2e6, 2 * MIB),
            scalars=1,
            limit=12,
        )
        force, offset = call(
            offset_kernel,
            [far(plane), far((march_size, 2 * chunks[1], LANE))],
            (place, *forces, state, force_weight, scale),
            cost(2e6, MIB),
            scalars=1,
            limit=12,
        )
        following = along_march(lead, -1)
        offset, force, *pieces = lax.optimization_barrier((offset, force, *pieces))
        change, pressure = by_rows(
            change_kernel,
            height,
            [far(slab), far(slab)],
            place,
            (*pieces, stay(term), stay(force)),
            cost(4e6, 4 * MIB),
        )
        (entering,) = call(
            scan_kernel, [far(chunks)], (across_march(offset),), cost(1e5, MIB)
        )
        entering = across_march(entering)
        common = (
            entering,
            stay(change),
            stay(following),
            stay(decay),
            stay(lead_far),
            near_inflow,
        )
        if final:
            (current,) = by_rows(
                last_kernel, height, [far(slab)], place, common, cost(4e6, 5 * MIB)
            )
            return (current, pressure)
        current, disc, *source = by_rows(
            middle_kernel,
            height,
            [far(slab), near(plane, BF16)] + sources,
            place,
            common,
            cost(6e6, 5 * MIB),
            whole=turned,
            scratch=[pltpu.VMEM(step, F32)],
        )
        current = stay(current)


def solution(mesh):
    march_size, cross_size = (mesh.shape[name] for name in ("march", "cross"))
    devices = mesh.devices.reshape(march_size // 2, 2, cross_size)
    mesh = Mesh(devices, (*MARCH, "cross"))
    in_specs = (
        P(MARCH, "cross", None),
        P(MARCH, "cross", None),
        P("cross", None),
        P(),
        P(),
        P(MARCH, None, "cross"),
    )
    out_specs = (P(MARCH, "cross", None), P(MARCH, "cross", None))
    return jax.shard_map(local, mesh=mesh, in_specs=in_specs, out_specs=out_specs, check_vma=False)
```

```python
import ml_dtypes
import numpy as np
import jax
import jax.numpy as jnp
from jax import lax
from jax.experimental import pallas as pl
from jax.experimental.pallas import tpu as pltpu
from jax.sharding import PartitionSpec as P

SWEEPS = 2
SOURCE_GAIN = 0.04
SCREENING = 0.001
VISCOSITY = 0.1
DRAG_RATE = 0.01

F32 = jnp.float32
BF16 = jnp.bfloat16
SUB = 8
LANE = 128
EDGE = 8
STEPS = 4
MIB = 1024 * 1024
VMEM = pl.BlockSpec(memory_space=pltpu.VMEM)
SMEM = pl.BlockSpec(memory_space=pltpu.SMEM)


def tables(length):
    ordinal = np.arange(1, length + 1)
    product = np.outer(ordinal, ordinal) % (2 * (length + 1))
    sine = np.sqrt(2.0 / (length + 1)) * np.sin(np.pi * product / (length + 1))
    high = sine.astype(np.float32).astype(ml_dtypes.bfloat16)
    low = (sine - high.astype(np.float64)).astype(np.float32).astype(ml_dtypes.bfloat16)
    values = 2.0 - 2.0 * np.cos(np.pi * ordinal / (length + 1))
    inverse = 1.0 / (SCREENING + values[:, None] + values[None, :])
    return high, low, inverse.astype(np.float32)


def split(value):
    high = value.astype(BF16)
    return high, (value - high.astype(F32)).astype(BF16)


def groups(rows):
    return [(g, slice(SUB * g, SUB * g + SUB)) for g in range(rows // SUB)]


def to_chunks(ref, g, value):
    for h in range(2):
        for q in range(2):
            at = (2 * h + q) * LANE
            ref[2 * g + h, SUB * q : SUB * q + SUB, :] = value[:, at : at + LANE]


def from_chunks(ref, g):
    parts = []
    for h in range(2):
        for q in range(2):
            parts.append(ref[2 * g + h, SUB * q : SUB * q + SUB, :])
    return jnp.concatenate(parts, axis=1)


def decay_of(value, damping):
    return 1.0 - (damping + DRAG_RATE * jnp.abs(value))


def send_order(place, i, source, outs):
    count, height, _ = source.shape
    at = pl.multiple_of(i * height, height)
    for r, ref in enumerate(outs):
        ref[pl.ds(at, height), :] = source[lax.rem(place[0] + r, count)]


def send_edges(current, outs):
    stations, height, width = current.shape
    i = pl.program_id(0)
    total = outs[1].shape[0]
    empty = jnp.zeros((EDGE - stations, width), F32)

    @pl.when(i == pl.num_programs(0) - 1)
    def _():
        rows = [current[s, height - 1 : height] for s in range(stations)]
        outs[1][total - EDGE : total] = jnp.concatenate(rows + [empty], axis=0)

    @pl.when(i == 0)
    def _():
        rows = [current[s, 0:1] for s in range(stations)]
        outs[-1][total - EDGE : total] = jnp.concatenate(rows + [empty], axis=0)


def source_kernel(place, current, upstream, inflow, x0, x1, x2, x3, source):
    stations, height, _ = current.shape
    for _, rows in groups(height):
        previous = jnp.where(place[1] == 1, inflow[rows], upstream[rows])
        for s in range(stations):
            here = current[s, rows]
            source[s, rows] = SOURCE_GAIN * (here - previous)
            previous = here
    outs = (x0, x1, x2, x3)
    send_order(place, pl.program_id(0), source, outs)
    send_edges(current, outs)


def decay_kernel(place, current, damping, decay, scale):
    for g, rows in groups(current.shape[1]):
        product = None
        for s in range(current.shape[0]):
            d = decay_of(current[s, rows], damping[s, rows])
            decay[s, rows] = d
            product = d if product is None else product * d
        to_chunks(scale, g, product)


def weights_kernel(
    place, current, before, after, decay, inflow, term, weights, base, force_weight
):
    stations, height, width = current.shape
    first = place[1] == 1
    above = jnp.where(place[2] == 1, 0.0, before[height : height + EDGE])
    below = jnp.where(place[3] == 1, 0.0, after[height : height + EDGE])
    lane = lax.broadcasted_iota(jnp.int32, (SUB, width), 1)
    for g, rows in groups(height):
        lo, hi = SUB * g, SUB * g + SUB
        total = jnp.zeros((SUB, width), F32)
        factor = None
        for s in reversed(range(stations)):
            here = current[s, rows]
            if g == 0:
                up = jnp.concatenate([above[s : s + 1], current[s, 0 : SUB - 1]], axis=0)
            else:
                up = current[s, lo - 1 : hi - 1]
            if hi == height:
                down = jnp.concatenate([current[s, lo + 1 : hi], below[s : s + 1]], axis=0)
            else:
                down = current[s, lo + 1 : hi + 1]
            left = jnp.where(lane == 0, 0.0, pltpu.roll(here, 1, 1))
            right = jnp.where(lane == width - 1, 0.0, pltpu.roll(here, width - 1, 1))
            t = VISCOSITY * (up + down + left + right - 4.0 * here)
            term[s, rows] = t
            d = decay[s, rows]
            if factor is None:
                total, weight, factor = t, 1.0 - d, d
            else:
                if s == 0:
                    force_weight[rows] = factor
                total, weight, factor = total + factor * t, factor * (1.0 - d), factor * d
            if s == 0:
                entry = jnp.where(first, factor, 0.0)
                weight = weight + entry
                total = total + entry * inflow[rows]
            weights[s, rows] = weight
        base[rows] = total


def far_solve_kernel(
    place, x0, x1, x2, x3, high_far, low_far, inverse_far, p0, p1, p2, p3,
    plane, high, low, inverse, arrivals,
):
    copies = [
        pltpu.make_async_copy(far_ref, ref, arrivals.at[i])
        for i, (far_ref, ref) in enumerate(
            ((high_far, high), (low_far, low), (inverse_far, inverse))
        )
    ]
    solve(place, (x0, x1, x2, x3), (high, low, inverse), (), (p0, p1, p2, p3), plane, copies)


def near_solve_kernel(
    place, x0, x1, x2, x3, high, low, inverse, f0, f1, f2, f3, p0, p1, p2, p3, plane
):
    forces = (f0, f1, f2, f3)
    solve(place, (x0, x1, x2, x3), (high, low, inverse), forces, (p0, p1, p2, p3), plane)


def solve(place, inputs, tables_near, forces, outputs, plane, copies=()):
    c = place[0]
    high, low, inverse = tables_near
    for copy in copies:
        copy.start()
    count = len(inputs)
    height = inputs[0].shape[0]
    for r, ref in enumerate(inputs):
        b = lax.rem(c - r + count, count)
        plane[pl.ds(pl.multiple_of(b * height, height), height), :] = ref[0:height]
    for copy in copies[:2]:
        copy.wait()
    sh, sl = high[...], low[...]
    by_left = jnp.concatenate([sh, sh, sl], axis=1)
    by_right = jnp.concatenate([sh, sl, sh], axis=0)

    def right(value):
        vh, vl = split(value)
        return jnp.dot(
            jnp.concatenate([vh, vh, vl], axis=1), by_right, preferred_element_type=F32
        )

    def left(value):
        vh, vl = split(value)
        return jnp.dot(
            by_left, jnp.concatenate([vh, vl, vh], axis=0), preferred_element_type=F32
        )

    modes = left(right(plane[...]))
    for copy in copies[2:]:
        copy.wait()
    modes = modes * inverse[...]
    plane[...] = right(left(modes))
    for r, ref in enumerate(outputs):
        b = lax.rem(c + r, count)
        ref[0:height] = plane[pl.ds(pl.multiple_of(b * height, height), height), :]
    if forces:
        extra = outputs[0].shape[0] - height
        for r, ref in enumerate(outputs):
            for q in range(height // extra):
                ref[height : height + extra, LANE * q : LANE * (q + 1)] = forces[-r][
                    extra * q : extra * (q + 1)
                ]


def disc_kernel(d0, d1, d2, d3, places, place_row, owners, *rest):
    streams, tabled = 4, (len(rest) - 11) // 2
    blades, tables_far = rest[:streams], rest[streams : streams + tabled]
    f0, f1, f2, f3 = rest[streams + tabled : streams + tabled + 4]
    tables_near = rest[streams + tabled + 4 : streams + 2 * tabled + 4]
    picked, total = rest[streams + 2 * tabled + 4 : streams + 2 * tabled + 6]
    step = pl.program_id(0)
    last = pl.num_programs(0) - 1
    height, width = d0.shape
    number = picked.shape[0]
    copies = [
        pltpu.make_async_copy(source, target, rest[-1].at[i])
        for i, (source, target) in enumerate(zip(tables_far, tables_near))
    ]

    @pl.when(step == 0)
    def _():
        for copy in copies:
            copy.start()
        plane = jnp.concatenate([d[...] for d in (d0, d1, d2, d3)], axis=0)
        lane = lax.broadcasted_iota(jnp.int32, (number, LANE), 1)
        chosen = [
            jnp.where(places[...] == lane + LANE * q, 1.0, 0.0).astype(BF16)
            for q in range(width // LANE)
        ]
        rows = jnp.dot(
            jnp.concatenate(chosen, axis=1), plane, preferred_element_type=F32
        )
        picked[...] = rows.astype(BF16)
        total[...] = jnp.zeros_like(total)

    per_step = blades[0].shape[0]
    for i in range(0, per_step, 2):
        pair = jnp.concatenate(
            [
                jnp.concatenate([blade[j] for blade in blades], axis=0)
                for j in (i, i + 1)
            ],
            axis=1,
        )
        response = jnp.dot(picked[...], pair, preferred_element_type=F32)
        first = step * per_step + i
        kept = jnp.where(owners[...] == first, response[:, :LANE], total[...])
        total[...] = jnp.where(owners[...] == first + 1, response[:, LANE:], kept)

    @pl.when(step == last)
    def _():
        rest_of, parts = jnp.tanh(total[...]), []
        for _ in range(3):
            parts.append(rest_of.astype(BF16))
            rest_of = rest_of - parts[-1].astype(F32)
        forces = jnp.concatenate(parts, axis=0)
        at = place_row[0:1]
        for r, ref in enumerate((f0, f1, f2, f3)):
            row = lax.broadcasted_iota(jnp.int32, (height, number), 0) + height * r
            back = jnp.where(row == at, 1.0, 0.0).astype(BF16)
            ref[...] = jnp.dot(
                jnp.concatenate([back] * 3, axis=1), forces, preferred_element_type=F32
            )
        for copy in copies:
            copy.wait()


def offset_kernel(place, *rest):
    c = place[0]
    pieces = rest[:4]
    *forces, weights, base, force_weight, lead, lead_far, force, offset = rest[4:]
    count, height, full = weights.shape
    width = full // count
    for r in range(count):
        b = lax.rem(c + r if forces else c - r + count, count)
        lanes = pl.ds(pl.multiple_of(b * width, width), width)
        if forces:
            force[:, lanes] = forces[r][...]
        else:
            extra = pieces[r].shape[0] - height
            for q in range(height // extra):
                force[extra * q : extra * (q + 1), lanes] = pieces[r][
                    height : height + extra, width * q : width * (q + 1)
                ]

    for r in range(count):
        @pl.when(c == r)
        def _():
            lead[...] = pieces[r][0:height]
            lead_far[...] = pieces[r][0:height]

    for g, rows in groups(height):
        state = base[rows] + force_weight[rows] * force[rows]
        for r in range(count):
            s = lax.rem(c - r + count, count)
            state = state + weights[s, rows] * pieces[r][rows]
        to_chunks(offset, g, state)


def change_kernel(place, p0, p1, p2, p3, term, force, change, pressure):
    c = place[0]
    pieces = (p0, p1, p2, p3)
    count, height, _ = term.shape
    for r in range(count):
        pressure[lax.rem(c - r + count, count)] = pieces[r][...]
    for _, rows in groups(height):
        here = pressure[0, rows]
        for s in range(count):
            value = term[s, rows] + here
            if s == 0:
                value = value + force[rows]
            if s < count - 1:
                here = pressure[s + 1, rows]
                value = value - here
            change[s, rows] = value


def scan_kernel(scale, offset, entering):
    entering[0] = jnp.zeros_like(entering[0])
    state = offset[0]
    for m in range(1, scale.shape[0]):
        entering[m] = state
        state = scale[m] * state + offset[m]


def march_rows(first, g, rows, entering, change, following, decay, lead, inflow):
    stations = decay.shape[0]
    state = jnp.where(first == 1, inflow[rows], from_chunks(entering, g) - lead[rows])
    states = [state]
    for s in range(stations):
        step = change[s, rows]
        if s == stations - 1:
            step = step - following[rows]
        state = decay[s, rows] * state + step
        states.append(state)
    return states


def middle_kernel(
    place, entering, change, following, decay, lead, inflow, damping,
    current, decay_new, scale, disc, x0, x1, x2, x3, source,
):
    first = place[1]
    stations, height, _ = current.shape
    for g, rows in groups(height):
        states = march_rows(first, g, rows, entering, change, following, decay, lead, inflow)
        product = None
        for s in range(stations):
            value = states[s + 1]
            current[s, rows] = value
            source[s, rows] = SOURCE_GAIN * (value - states[s])
            d = decay_of(value, damping[s, rows])
            decay_new[s, rows] = d
            product = d if product is None else product * d
        to_chunks(scale, g, product)
    outs = (x0, x1, x2, x3)
    send_order(place, pl.program_id(0), source, outs)
    send_edges(current, outs)
    disc[...] = current[0].astype(BF16)


def last_kernel(place, entering, change, following, decay, lead, inflow, current):
    first = place[1]
    for g, rows in groups(current.shape[1]):
        states = march_rows(first, g, rows, entering, change, following, decay, lead, inflow)
        for s in range(current.shape[0]):
            current[s, rows] = states[s + 1]


def cost(flops, size):
    return pl.CostEstimate(flops=int(flops), bytes_accessed=int(size), transcendentals=0)


def near(shape, dtype=F32):
    return pltpu.VMEM(shape, dtype)


def far(shape, dtype=F32):
    return pltpu.HBM(shape, dtype)


def stay(value):
    return pltpu.with_memory_space_constraint(value, pltpu.HBM)


def call(kernel, outs, args, work, scalars=0, limit=8, scratch=()):
    return pl.pallas_call(
        kernel,
        out_shape=outs,
        in_specs=[SMEM] * scalars + [VMEM] * (len(args) - scalars),
        out_specs=[VMEM] * len(outs),
        scratch_shapes=list(scratch),
        compiler_params=pltpu.CompilerParams(vmem_limit_bytes=limit * MIB),
        cost_estimate=work,
    )(*args)


def by_rows(kernel, height, outs, place, args, work, whole=(), scratch=()):
    part = height // STEPS

    def spec(shape, index):
        if index in whole:
            return pl.BlockSpec(shape, lambda i, p: (0,) * len(shape))
        if shape[-1] == LANE and len(shape) == 3:
            return pl.BlockSpec((shape[0] // STEPS,) + shape[1:], lambda i, p: (i, 0, 0))
        if len(shape) == 3:
            return pl.BlockSpec((shape[0], part, shape[2]), lambda i, p: (0, i, 0))
        return pl.BlockSpec((part, shape[1]), lambda i, p: (i, 0))

    count = len(args)
    return pl.pallas_call(
        kernel,
        grid_spec=pltpu.PrefetchScalarGridSpec(
            num_scalar_prefetch=1,
            grid=(STEPS,),
            in_specs=[spec(a.shape, None) for a in args],
            out_specs=[spec(a.inner_aval.shape, i) for i, a in enumerate(outs)],
            scratch_shapes=list(scratch),
        ),
        out_shape=outs,
        compiler_params=pltpu.CompilerParams(vmem_limit_bytes=12 * MIB),
        cost_estimate=work,
    )(place, *args)


def disc_forces(rows, where, blades, tabled=()):
    height, width = rows[0].shape
    count = len(rows)
    number = blades.shape[0]
    per_step, streams = 8, 4
    fixed = lambda shape: pl.BlockSpec(shape, lambda i: (0,) * len(shape))
    table = lambda k: pl.BlockSpec((per_step, width // streams, LANE), lambda i: (i, k, 0))
    discs = where[0].shape[0]
    return pl.pallas_call(
        disc_kernel,
        grid=(number // per_step,),
        out_shape=[near((height, LANE))] * count + [near(t.shape, t.dtype) for t in tabled],
        in_specs=[fixed((height, width))] * count
        + [fixed(w.shape) for w in where]
        + [table(k) for k in range(streams)]
        + [pl.BlockSpec(memory_space=pltpu.HBM)] * len(tabled),
        out_specs=[fixed((height, LANE))] * count
        + [pl.BlockSpec(memory_space=pltpu.VMEM)] * len(tabled),
        scratch_shapes=[
            pltpu.VMEM((discs, width), BF16),
            pltpu.VMEM((discs, LANE), F32),
            pltpu.SemaphoreType.DMA((3,)),
        ],
        compiler_params=pltpu.CompilerParams(vmem_limit_bytes=16 * MIB),
        cost_estimate=cost(2 * number * width * width * LANE, 5 * MIB),
    )(*rows, *map(stay, where), *[stay(blades)] * streams, *tabled)


def local(velocity_guess, damping, inflow, disc_rows, owner, blade):
    stations, height, width = velocity_guess.shape
    march_size = lax.axis_size("march")
    cross_size = lax.axis_size("cross")
    march_index = lax.axis_index("march")
    cross_index = lax.axis_index("cross")
    disc_slab = stations * march_size // 2 // stations
    at_disc = march_index == disc_slab
    first = march_index == 0
    place = jnp.stack(
        [
            cross_index.astype(jnp.int32),
            first.astype(jnp.int32),
            (cross_index == 0).astype(jnp.int32),
            (cross_index == cross_size - 1).astype(jnp.int32),
        ]
    )
    tabled = [stay(jnp.asarray(t)) for t in tables(width)]

    slab = (stations, height, width)
    plane = (height, width)
    edged = (height + EDGE, width)
    chunks = (march_size, height * width // march_size // LANE, LANE)
    sources = [near(plane), near(edged), near(plane), near(edged)]

    def turn(value, steps):
        return lax.ppermute(
            value, "cross", [(i, (i + steps) % cross_size) for i in range(cross_size)]
        )

    def turns(blocks, sign=1):
        return [blocks[0]] + [turn(blocks[r], sign * r) for r in range(1, cross_size)]

    def along_march(value, steps):
        count = march_size
        return lax.ppermute(
            value, "march", [(i, i + steps) for i in range(count) if 0 <= i + steps < count]
        )

    def across_march(value):
        return lax.all_to_all(value, "march", split_axis=0, concat_axis=0, tiled=True)

    blades = lax.all_gather(blade, "march", axis=0, tiled=True)
    turn_of = (cross_index - disc_rows // height + cross_size) % cross_size
    places = turn_of * height + disc_rows % height
    count = disc_rows.shape[0]
    where = (
        jnp.broadcast_to(places[:, None], (count, LANE)),
        jnp.broadcast_to(places[None, :], (SUB, count)),
        jnp.broadcast_to(jnp.where(at_disc, owner, -1)[:, None], (count, LANE)),
    )

    step = (stations, height // STEPS, width)
    turned = range(4, 8)
    near_inflow = stay(inflow)
    upstream = along_march(velocity_guess[-1], 1)
    upstream, *where = lax.optimization_barrier((upstream, *where))
    current = stay(velocity_guess)
    disc = velocity_guess[0].astype(BF16)
    rows = turns([disc] * cross_size)
    source = by_rows(
        source_kernel,
        height,
        sources,
        place,
        (current, upstream, near_inflow),
        cost(1e6, 2 * MIB),
        whole=range(4),
        scratch=[pltpu.VMEM(step, F32)],
    )
    guess, damp, *source = lax.optimization_barrier((velocity_guess, damping, *source))
    decay, scale = by_rows(
        decay_kernel,
        height,
        [far(slab), far(chunks)],
        place,
        (stay(guess), stay(damp)),
        cost(4e6, 3 * MIB),
    )
    for sweep_index in range(SWEEPS):
        merged = sweep_index > 0
        final = sweep_index == SWEEPS - 1
        if merged:
            rows = turns([disc] * cross_size)
        arrived = turns(source)
        solve_cost = cost(3 * 8 * width**3, 5 * MIB)
        if merged:
            made = disc_forces(rows, where, blades, tabled)
            forces, near_tables = made[:cross_size], made[cross_size:]
            solved = call(
                near_solve_kernel,
                [near((height + height * LANE // width, width))] * cross_size,
                (place, *arrived, *near_tables, *forces),
                solve_cost,
                scalars=1,
                limit=16,
                scratch=[pltpu.VMEM((width, width), F32)],
            )
            scales = across_march(scale)
            forces = []
        else:
            scales = across_march(scale)
            solved = pl.pallas_call(
                far_solve_kernel,
                out_shape=[near(plane)] * cross_size,
                in_specs=[SMEM] + [VMEM] * cross_size + [pl.BlockSpec(memory_space=pltpu.HBM)] * 3,
                out_specs=[VMEM] * cross_size,
                scratch_shapes=[pltpu.VMEM((width, width), F32)]
                + [pltpu.VMEM((width, width), BF16)] * 2
                + [pltpu.VMEM((width, width), F32), pltpu.SemaphoreType.DMA((3,))],
                compiler_params=pltpu.CompilerParams(vmem_limit_bytes=20 * MIB),
                cost_estimate=solve_cost,
            )(place, *arrived, *tabled)
            rows, scales, solved = lax.optimization_barrier((rows, scales, solved))
        pieces = turns(solved)
        decay = stay(decay)
        term, weights, base, force_weight = call(
            weights_kernel,
            [far(slab), near(slab), near(plane), near(plane)],
            (place, current, arrived[1], arrived[-1], decay, near_inflow),
            cost(8e6, 4 * MIB),
            scalars=1,
            limit=12,
        )
        if not merged:
            rows, base = lax.optimization_barrier((rows, base))
            forces = turns(disc_forces(rows, where, blades), -1)
        lead, lead_far, force, offset = call(
            offset_kernel,
            [near(plane), far(plane), far(plane), far(chunks)],
            (place, *pieces, *forces, weights, base, force_weight),
            cost(2e6, 3 * MIB),
            scalars=1,
            limit=12,
        )
        following = along_march(lead, -1)
        offset, force, *pieces = lax.optimization_barrier((offset, force, *pieces))
        change, pressure = by_rows(
            change_kernel,
            height,
            [far(slab), far(slab)],
            place,
            (*pieces, stay(term), stay(force)),
            cost(4e6, 4 * MIB),
        )
        (entering,) = call(
            scan_kernel, [far(chunks)], (scales, across_march(offset)), cost(1e5, MIB)
        )
        entering = across_march(entering)
        common = (entering, stay(change), stay(following), decay, stay(lead_far), near_inflow)
        if final:
            (current,) = by_rows(
                last_kernel, height, [far(slab)], place, common, cost(4e6, 5 * MIB)
            )
            return (current, pressure)
        current, decay, scale, disc, *source = by_rows(
            middle_kernel,
            height,
            [far(slab), far(slab), far(chunks), near(plane, BF16)] + sources,
            place,
            common + (stay(damping),),
            cost(8e6, 8 * MIB),
            whole=turned,
            scratch=[pltpu.VMEM(step, F32)],
        )
        current = stay(current)


def solution(mesh):
    in_specs = (
        P("march", "cross", None),
        P("march", "cross", None),
        P("cross", None),
        P(),
        P(),
        P("march", None, "cross"),
    )
    out_specs = (P("march", "cross", None), P("march", "cross", None))
    return jax.shard_map(local, mesh=mesh, in_specs=in_specs, out_specs=out_specs, check_vma=False)
```

```python
import ml_dtypes
import numpy as np
import jax
import jax.numpy as jnp
from jax import lax
from jax.experimental import pallas as pl
from jax.experimental.pallas import tpu as pltpu
from jax.sharding import PartitionSpec as P

SWEEPS = 2
SOURCE_GAIN = 0.04
SCREENING = 0.001
VISCOSITY = 0.1
DRAG_RATE = 0.01

F32 = jnp.float32
BF16 = jnp.bfloat16
SUB = 8
LANE = 128
EDGE = 8
STEPS = 4
MIB = 1024 * 1024
VMEM = pl.BlockSpec(memory_space=pltpu.VMEM)
SMEM = pl.BlockSpec(memory_space=pltpu.SMEM)


def tables(length):
    ordinal = np.arange(1, length + 1)
    product = np.outer(ordinal, ordinal) % (2 * (length + 1))
    sine = np.sqrt(2.0 / (length + 1)) * np.sin(np.pi * product / (length + 1))
    high = sine.astype(np.float32).astype(ml_dtypes.bfloat16)
    low = (sine - high.astype(np.float64)).astype(np.float32).astype(ml_dtypes.bfloat16)
    values = 2.0 - 2.0 * np.cos(np.pi * ordinal / (length + 1))
    inverse = 1.0 / (SCREENING + values[:, None] + values[None, :])
    return high, low, inverse.astype(np.float32)


def split(value):
    high = value.astype(BF16)
    return high, (value - high.astype(F32)).astype(BF16)


def groups(rows):
    return [(g, slice(SUB * g, SUB * g + SUB)) for g in range(rows // SUB)]


def to_chunks(ref, g, value):
    for h in range(2):
        for q in range(2):
            at = (2 * h + q) * LANE
            ref[2 * g + h, SUB * q : SUB * q + SUB, :] = value[:, at : at + LANE]


def from_chunks(ref, g):
    parts = []
    for h in range(2):
        for q in range(2):
            parts.append(ref[2 * g + h, SUB * q : SUB * q + SUB, :])
    return jnp.concatenate(parts, axis=1)


def decay_of(value, damping):
    return 1.0 - (damping + DRAG_RATE * jnp.abs(value))


def send_order(place, source, outs, i=None):
    count, height, _ = source.shape
    rows = slice(0, height) if i is None else pl.ds(pl.multiple_of(i * height, height), height)
    for r, ref in enumerate(outs):
        ref[rows, :] = source[lax.rem(place[0] + r, count)]


def send_edges(current, outs, first=True, last=True):
    stations, height, width = current.shape
    total = outs[1].shape[0]
    empty = jnp.zeros((EDGE - stations, width), F32)

    @pl.when(last)
    def _():
        rows = [current[s, height - 1 : height] for s in range(stations)]
        outs[1][total - EDGE : total] = jnp.concatenate(rows + [empty], axis=0)

    @pl.when(first)
    def _():
        rows = [current[s, 0:1] for s in range(stations)]
        outs[-1][total - EDGE : total] = jnp.concatenate(rows + [empty], axis=0)


def source_kernel(place, current, upstream, inflow, x0, x1, x2, x3, source):
    stations, height, _ = current.shape
    for _, rows in groups(height):
        previous = jnp.where(place[1] == 1, inflow[rows], upstream[rows])
        for s in range(stations):
            here = current[s, rows]
            source[s, rows] = SOURCE_GAIN * (here - previous)
            previous = here
    outs = (x0, x1, x2, x3)
    i = pl.program_id(0)
    send_order(place, source, outs, i)
    send_edges(current, outs, i == 0, i == pl.num_programs(0) - 1)


def decay_kernel(place, current, damping, decay, scale):
    for g, rows in groups(current.shape[1]):
        product = None
        for s in range(current.shape[0]):
            d = decay_of(current[s, rows], damping[s, rows])
            decay[s, rows] = d
            product = d if product is None else product * d
        to_chunks(scale, g, product)


def weights_kernel(
    place, current, before, after, decay, inflow, term, weights, base, force_weight
):
    stations, height, width = current.shape
    first = place[1] == 1
    above = jnp.where(place[2] == 1, 0.0, before[height : height + EDGE])
    below = jnp.where(place[3] == 1, 0.0, after[height : height + EDGE])
    lane = lax.broadcasted_iota(jnp.int32, (SUB, width), 1)
    for g, rows in groups(height):
        lo, hi = SUB * g, SUB * g + SUB
        total = jnp.zeros((SUB, width), F32)
        factor = None
        for s in reversed(range(stations)):
            here = current[s, rows]
            if g == 0:
                up = jnp.concatenate([above[s : s + 1], current[s, 0 : SUB - 1]], axis=0)
            else:
                up = current[s, lo - 1 : hi - 1]
            if hi == height:
                down = jnp.concatenate([current[s, lo + 1 : hi], below[s : s + 1]], axis=0)
            else:
                down = current[s, lo + 1 : hi + 1]
            left = jnp.where(lane == 0, 0.0, pltpu.roll(here, 1, 1))
            right = jnp.where(lane == width - 1, 0.0, pltpu.roll(here, width - 1, 1))
            t = VISCOSITY * (up + down + left + right - 4.0 * here)
            term[s, rows] = t
            d = decay[s, rows]
            if factor is None:
                total, weight, factor = t, 1.0 - d, d
            else:
                if s == 0:
                    force_weight[rows] = factor
                total, weight, factor = total + factor * t, factor * (1.0 - d), factor * d
            if s == 0:
                entry = jnp.where(first, factor, 0.0)
                weight = weight + entry
                total = total + entry * inflow[rows]
            weights[s, rows] = weight
        base[rows] = total


def far_solve_kernel(
    place, x0, x1, x2, x3, high_far, low_far, inverse_far, p0, p1, p2, p3,
    plane, high, low, inverse, arrivals,
):
    copies = [
        pltpu.make_async_copy(far_ref, ref, arrivals.at[i])
        for i, (far_ref, ref) in enumerate(
            ((high_far, high), (low_far, low), (inverse_far, inverse))
        )
    ]
    solve(place, (x0, x1, x2, x3), (high, low, inverse), (), (p0, p1, p2, p3), plane, copies)


def near_solve_kernel(
    place, x0, x1, x2, x3, high, low, inverse, f0, f1, f2, f3, p0, p1, p2, p3, plane
):
    forces = (f0, f1, f2, f3)
    solve(place, (x0, x1, x2, x3), (high, low, inverse), forces, (p0, p1, p2, p3), plane)


def solve(place, inputs, tables_near, forces, outputs, plane, copies=()):
    c = place[0]
    high, low, inverse = tables_near
    for copy in copies:
        copy.start()
    count = len(inputs)
    height = inputs[0].shape[0]
    for r, ref in enumerate(inputs):
        b = lax.rem(c - r + count, count)
        plane[pl.ds(pl.multiple_of(b * height, height), height), :] = ref[0:height]
    for copy in copies[:2]:
        copy.wait()
    sh, sl = high[...], low[...]
    by_left = jnp.concatenate([sh, sh, sl], axis=1)
    by_right = jnp.concatenate([sh, sl, sh], axis=0)

    def right(value):
        vh, vl = split(value)
        return jnp.dot(
            jnp.concatenate([vh, vh, vl], axis=1), by_right, preferred_element_type=F32
        )

    def left(value):
        vh, vl = split(value)
        return jnp.dot(
            by_left, jnp.concatenate([vh, vl, vh], axis=0), preferred_element_type=F32
        )

    modes = left(right(plane[...]))
    for copy in copies[2:]:
        copy.wait()
    modes = modes * inverse[...]
    plane[...] = right(left(modes))
    for r, ref in enumerate(outputs):
        b = lax.rem(c + r, count)
        ref[0:height] = plane[pl.ds(pl.multiple_of(b * height, height), height), :]
    if forces:
        extra = outputs[0].shape[0] - height
        for r, ref in enumerate(outputs):
            for q in range(height // extra):
                ref[height : height + extra, LANE * q : LANE * (q + 1)] = forces[-r][
                    extra * q : extra * (q + 1)
                ]


def disc_kernel(d0, d1, d2, d3, places, place_row, owners, *rest):
    streams, tabled = 4, (len(rest) - 11) // 2
    blades, tables_far = rest[:streams], rest[streams : streams + tabled]
    f0, f1, f2, f3 = rest[streams + tabled : streams + tabled + 4]
    tables_near = rest[streams + tabled + 4 : streams + 2 * tabled + 4]
    picked, total = rest[streams + 2 * tabled + 4 : streams + 2 * tabled + 6]
    step = pl.program_id(0)
    last = pl.num_programs(0) - 1
    height, width = d0.shape
    number = picked.shape[0]
    copies = [
        pltpu.make_async_copy(source, target, rest[-1].at[i])
        for i, (source, target) in enumerate(zip(tables_far, tables_near))
    ]

    @pl.when(step == 0)
    def _():
        for copy in copies:
            copy.start()
        plane = jnp.concatenate([d[...] for d in (d0, d1, d2, d3)], axis=0)
        lane = lax.broadcasted_iota(jnp.int32, (number, LANE), 1)
        chosen = [
            jnp.where(places[...] == lane + LANE * q, 1.0, 0.0).astype(BF16)
            for q in range(width // LANE)
        ]
        rows = jnp.dot(
            jnp.concatenate(chosen, axis=1), plane, preferred_element_type=F32
        )
        picked[...] = rows.astype(BF16)
        total[...] = jnp.zeros_like(total)

    per_step = blades[0].shape[0]
    for i in range(0, per_step, 2):
        pair = jnp.concatenate(
            [
                jnp.concatenate([blade[j] for blade in blades], axis=0)
                for j in (i, i + 1)
            ],
            axis=1,
        )
        response = jnp.dot(picked[...], pair, preferred_element_type=F32)
        first = step * per_step + i
        kept = jnp.where(owners[...] == first, response[:, :LANE], total[...])
        total[...] = jnp.where(owners[...] == first + 1, response[:, LANE:], kept)

    @pl.when(step == last)
    def _():
        rest_of, parts = jnp.tanh(total[...]), []
        for _ in range(3):
            parts.append(rest_of.astype(BF16))
            rest_of = rest_of - parts[-1].astype(F32)
        forces = jnp.concatenate(parts, axis=0)
        at = place_row[0:1]
        for r, ref in enumerate((f0, f1, f2, f3)):
            row = lax.broadcasted_iota(jnp.int32, (height, number), 0) + height * r
            back = jnp.where(row == at, 1.0, 0.0).astype(BF16)
            ref[...] = jnp.dot(
                jnp.concatenate([back] * 3, axis=1), forces, preferred_element_type=F32
            )
        for copy in copies:
            copy.wait()


def offset_kernel(place, *rest):
    c = place[0]
    pieces = rest[:4]
    *forces, weights, base, force_weight, lead, force, offset = rest[4:]
    count, height, full = weights.shape
    width = full // count
    for r in range(count):
        b = lax.rem(c + r if forces else c - r + count, count)
        lanes = pl.ds(pl.multiple_of(b * width, width), width)
        if forces:
            force[:, lanes] = forces[r][...]
        else:
            extra = pieces[r].shape[0] - height
            for q in range(height // extra):
                force[extra * q : extra * (q + 1), lanes] = pieces[r][
                    height : height + extra, width * q : width * (q + 1)
                ]

    for r in range(count):
        @pl.when(c == r)
        def _():
            lead[...] = pieces[r][0:height]

    for g, rows in groups(height):
        state = base[rows] + force_weight[rows] * force[rows]
        for r in range(count):
            s = lax.rem(c - r + count, count)
            state = state + weights[s, rows] * pieces[r][rows]
        to_chunks(offset, g, state)


def change_kernel(
    place, p0, p1, p2, p3, term, force, decay, inflow,
    change, pressure, decay_near, entry,
):
    c = place[0]
    pieces = (p0, p1, p2, p3)
    count, height, _ = term.shape
    for r in range(count):
        pressure[lax.rem(c - r + count, count)] = pieces[r][...]
    for _, rows in groups(height):
        here = pressure[0, rows]
        entry[rows] = jnp.where(place[1] == 1, inflow[rows], -here)
        for s in range(count):
            value = term[s, rows] + here
            if s == 0:
                value = value + force[rows]
            if s < count - 1:
                here = pressure[s + 1, rows]
                value = value - here
            change[s, rows] = value
            decay_near[s, rows] = decay[s, rows]


def scan_kernel(scale, offset, entering):
    entering[0] = jnp.zeros_like(entering[0])
    state = offset[0]
    for m in range(1, scale.shape[0]):
        entering[m] = state
        state = scale[m] * state + offset[m]


def march_rows(g, rows, entering, change, following, decay, entry):
    stations = decay.shape[0]
    state = from_chunks(entering, g) + entry[rows]
    states = [state]
    for s in range(stations):
        step = change[s, rows]
        if s == stations - 1:
            step = step - following[rows]
        state = decay[s, rows] * state + step
        states.append(state)
    return states


def middle_kernel(
    place, entering, change, following, decay, entry, current, disc, x0, x1, x2, x3, source
):
    stations, height, _ = current.shape
    for g, rows in groups(height):
        states = march_rows(g, rows, entering, change, following, decay, entry)
        for s in range(stations):
            current[s, rows] = states[s + 1]
            source[s, rows] = SOURCE_GAIN * (states[s + 1] - states[s])
    outs = (x0, x1, x2, x3)
    send_order(place, source, outs)
    send_edges(current, outs)
    disc[...] = current[0].astype(BF16)


def last_kernel(entering, change, following, decay, entry, current):
    for g, rows in groups(current.shape[1]):
        states = march_rows(g, rows, entering, change, following, decay, entry)
        for s in range(current.shape[0]):
            current[s, rows] = states[s + 1]


def cost(flops, size):
    return pl.CostEstimate(flops=int(flops), bytes_accessed=int(size), transcendentals=0)


def near(shape, dtype=F32):
    return pltpu.VMEM(shape, dtype)


def far(shape, dtype=F32):
    return pltpu.HBM(shape, dtype)


def stay(value):
    return pltpu.with_memory_space_constraint(value, pltpu.HBM)


def call(kernel, outs, args, work, scalars=0, limit=8, scratch=()):
    return pl.pallas_call(
        kernel,
        out_shape=outs,
        in_specs=[SMEM] * scalars + [VMEM] * (len(args) - scalars),
        out_specs=[VMEM] * len(outs),
        scratch_shapes=list(scratch),
        compiler_params=pltpu.CompilerParams(vmem_limit_bytes=limit * MIB),
        cost_estimate=work,
    )(*args)


def by_rows(kernel, height, outs, place, args, work, whole=(), scratch=()):
    part = height // STEPS

    def spec(shape, index):
        if index in whole:
            return pl.BlockSpec(shape, lambda i, p: (0,) * len(shape))
        if shape[-1] == LANE and len(shape) == 3:
            return pl.BlockSpec((shape[0] // STEPS,) + shape[1:], lambda i, p: (i, 0, 0))
        if len(shape) == 3:
            return pl.BlockSpec((shape[0], part, shape[2]), lambda i, p: (0, i, 0))
        return pl.BlockSpec((part, shape[1]), lambda i, p: (i, 0))

    count = len(args)
    return pl.pallas_call(
        kernel,
        grid_spec=pltpu.PrefetchScalarGridSpec(
            num_scalar_prefetch=1,
            grid=(STEPS,),
            in_specs=[spec(a.shape, None) for a in args],
            out_specs=[spec(a.inner_aval.shape, i) for i, a in enumerate(outs)],
            scratch_shapes=list(scratch),
        ),
        out_shape=outs,
        compiler_params=pltpu.CompilerParams(vmem_limit_bytes=12 * MIB),
        cost_estimate=work,
    )(place, *args)


def disc_forces(rows, where, blades, tabled=()):
    height, width = rows[0].shape
    count = len(rows)
    number = blades.shape[0]
    per_step, streams = 8, 4
    fixed = lambda shape: pl.BlockSpec(shape, lambda i: (0,) * len(shape))
    table = lambda k: pl.BlockSpec((per_step, width // streams, LANE), lambda i: (i, k, 0))
    discs = where[0].shape[0]
    return pl.pallas_call(
        disc_kernel,
        grid=(number // per_step,),
        out_shape=[near((height, LANE))] * count + [near(t.shape, t.dtype) for t in tabled],
        in_specs=[fixed((height, width))] * count
        + [fixed(w.shape) for w in where]
        + [table(k) for k in range(streams)]
        + [pl.BlockSpec(memory_space=pltpu.HBM)] * len(tabled),
        out_specs=[fixed((height, LANE))] * count
        + [pl.BlockSpec(memory_space=pltpu.VMEM)] * len(tabled),
        scratch_shapes=[
            pltpu.VMEM((discs, width), BF16),
            pltpu.VMEM((discs, LANE), F32),
            pltpu.SemaphoreType.DMA((3,)),
        ],
        compiler_params=pltpu.CompilerParams(vmem_limit_bytes=16 * MIB),
        cost_estimate=cost(2 * number * width * width * LANE, 5 * MIB),
    )(*rows, *map(stay, where), *[stay(blades)] * streams, *tabled)


def local(velocity_guess, damping, inflow, disc_rows, owner, blade):
    stations, height, width = velocity_guess.shape
    march_size = lax.axis_size("march")
    cross_size = lax.axis_size("cross")
    march_index = lax.axis_index("march")
    cross_index = lax.axis_index("cross")
    disc_slab = stations * march_size // 2 // stations
    at_disc = march_index == disc_slab
    first = march_index == 0
    place = jnp.stack(
        [
            cross_index.astype(jnp.int32),
            first.astype(jnp.int32),
            (cross_index == 0).astype(jnp.int32),
            (cross_index == cross_size - 1).astype(jnp.int32),
        ]
    )
    tabled = [stay(jnp.asarray(t)) for t in tables(width)]

    slab = (stations, height, width)
    plane = (height, width)
    edged = (height + EDGE, width)
    chunks = (march_size, height * width // march_size // LANE, LANE)
    sources = [near(plane), near(edged), near(plane), near(edged)]

    def turn(value, steps):
        return lax.ppermute(
            value, "cross", [(i, (i + steps) % cross_size) for i in range(cross_size)]
        )

    def turns(blocks, sign=1):
        return [blocks[0]] + [turn(blocks[r], sign * r) for r in range(1, cross_size)]

    def along_march(value, steps):
        count = march_size
        return lax.ppermute(
            value, "march", [(i, i + steps) for i in range(count) if 0 <= i + steps < count]
        )

    def across_march(value):
        return lax.all_to_all(value, "march", split_axis=0, concat_axis=0, tiled=True)

    blades = lax.all_gather(blade, "march", axis=0, tiled=True)
    turn_of = (cross_index - disc_rows // height + cross_size) % cross_size
    places = turn_of * height + disc_rows % height
    count = disc_rows.shape[0]
    where = (
        jnp.broadcast_to(places[:, None], (count, LANE)),
        jnp.broadcast_to(places[None, :], (SUB, count)),
        jnp.broadcast_to(jnp.where(at_disc, owner, -1)[:, None], (count, LANE)),
    )

    step = (stations, height // STEPS, width)
    near_inflow = stay(inflow)
    upstream = along_march(velocity_guess[-1], 1)
    upstream, *where = lax.optimization_barrier((upstream, *where))
    current = stay(velocity_guess)
    disc = velocity_guess[0].astype(BF16)
    rows = turns([disc] * cross_size)
    source = by_rows(
        source_kernel,
        height,
        sources,
        place,
        (current, upstream, near_inflow),
        cost(1e6, 2 * MIB),
        whole=range(4),
        scratch=[pltpu.VMEM(step, F32)],
    )
    for sweep_index in range(SWEEPS):
        merged = sweep_index > 0
        final = sweep_index == SWEEPS - 1
        if merged:
            rows = turns([disc] * cross_size)
        guess, damp, *source = lax.optimization_barrier((current, damping, *source))
        arrived = turns(source)
        decay, scale = by_rows(
            decay_kernel,
            height,
            [far(slab), far(chunks)],
            place,
            (guess if merged else stay(guess), stay(damp)),
            cost(4e6, 3 * MIB),
        )
        solve_cost = cost(3 * 8 * width**3, 5 * MIB)
        if merged:
            scale, *arrived = lax.optimization_barrier((scale, *arrived))
            made = disc_forces(rows, where, blades, tabled)
            forces, near_tables = made[:cross_size], made[cross_size:]
            solved = call(
                near_solve_kernel,
                [near((height + height * LANE // width, width))] * cross_size,
                (place, *arrived, *near_tables, *forces),
                solve_cost,
                scalars=1,
                limit=16,
                scratch=[pltpu.VMEM((width, width), F32)],
            )
            scales = across_march(scale)
            forces = []
        else:
            scales = across_march(scale)
            solved = pl.pallas_call(
                far_solve_kernel,
                out_shape=[near(plane)] * cross_size,
                in_specs=[SMEM] + [VMEM] * cross_size + [pl.BlockSpec(memory_space=pltpu.HBM)] * 3,
                out_specs=[VMEM] * cross_size,
                scratch_shapes=[pltpu.VMEM((width, width), F32)]
                + [pltpu.VMEM((width, width), BF16)] * 2
                + [pltpu.VMEM((width, width), F32), pltpu.SemaphoreType.DMA((3,))],
                compiler_params=pltpu.CompilerParams(vmem_limit_bytes=20 * MIB),
                cost_estimate=solve_cost,
            )(place, *arrived, *tabled)
            rows, scales, solved = lax.optimization_barrier((rows, scales, solved))
            forces = turns(disc_forces(rows, where, blades), -1)
        pieces = turns(solved)
        decay = stay(decay)
        term, weights, base, force_weight = call(
            weights_kernel,
            [far(slab), near(slab), near(plane), near(plane)],
            (place, current, arrived[1], arrived[-1], decay, near_inflow),
            cost(8e6, 4 * MIB),
            scalars=1,
            limit=12,
        )
        lead, force, offset = call(
            offset_kernel,
            [near(plane), far(plane), far(chunks)],
            (place, *pieces, *forces, weights, base, force_weight),
            cost(2e6, 3 * MIB),
            scalars=1,
            limit=12,
        )
        following = along_march(lead, -1)
        offset, force, *pieces = lax.optimization_barrier((offset, force, *pieces))
        change, pressure, decay, entry = by_rows(
            change_kernel,
            height,
            [near(slab), far(slab), near(slab), near(plane)],
            place,
            (*pieces, stay(term), stay(force), decay, near_inflow),
            cost(4e6, 4 * MIB),
        )
        (entering,) = call(
            scan_kernel, [far(chunks)], (scales, across_march(offset)), cost(1e5, MIB)
        )
        entering = across_march(entering)
        common = (entering, change, following, decay, entry)
        if final:
            (current,) = call(
                last_kernel, [far(slab)], common, cost(4e6, 5 * MIB), limit=12
            )
            return (current, pressure)
        current, disc, *source = call(
            middle_kernel,
            [near(slab), near(plane, BF16)] + sources,
            (place, *common),
            cost(6e6, 5 * MIB),
            scalars=1,
            limit=12,
            scratch=[pltpu.VMEM(slab, F32)],
        )


def solution(mesh):
    in_specs = (
        P("march", "cross", None),
        P("march", "cross", None),
        P("cross", None),
        P(),
        P(),
        P("march", None, "cross"),
    )
    out_specs = (P("march", "cross", None), P("march", "cross", None))
    return jax.shard_map(local, mesh=mesh, in_specs=in_specs, out_specs=out_specs, check_vma=False)
```

```python
import ml_dtypes
import numpy as np
import jax
import jax.numpy as jnp
from jax import lax
from jax.experimental import pallas as pl
from jax.experimental.pallas import tpu as pltpu
from jax.sharding import PartitionSpec as P

SWEEPS = 2
SOURCE_GAIN = 0.04
SCREENING = 0.001
VISCOSITY = 0.1
DRAG_RATE = 0.01

F32 = jnp.float32
BF16 = jnp.bfloat16
SUB = 8
LANE = 128
EDGE = 8
STEPS = 4
MIB = 1024 * 1024
VMEM = pl.BlockSpec(memory_space=pltpu.VMEM)
SMEM = pl.BlockSpec(memory_space=pltpu.SMEM)


def tables(length):
    ordinal = np.arange(1, length + 1)
    product = np.outer(ordinal, ordinal) % (2 * (length + 1))
    sine = np.sqrt(2.0 / (length + 1)) * np.sin(np.pi * product / (length + 1))
    high = sine.astype(np.float32).astype(ml_dtypes.bfloat16)
    low = (sine - high.astype(np.float64)).astype(np.float32).astype(ml_dtypes.bfloat16)
    values = 2.0 - 2.0 * np.cos(np.pi * ordinal / (length + 1))
    inverse = 1.0 / (SCREENING + values[:, None] + values[None, :])
    return high, low, inverse.astype(np.float32)


def split(value):
    high = value.astype(BF16)
    return high, (value - high.astype(F32)).astype(BF16)


def groups(rows):
    return [(g, slice(SUB * g, SUB * g + SUB)) for g in range(rows // SUB)]


def to_chunks(ref, g, value):
    for h in range(2):
        for q in range(2):
            at = (2 * h + q) * LANE
            ref[2 * g + h, SUB * q : SUB * q + SUB, :] = value[:, at : at + LANE]


def from_chunks(ref, g):
    parts = []
    for h in range(2):
        for q in range(2):
            parts.append(ref[2 * g + h, SUB * q : SUB * q + SUB, :])
    return jnp.concatenate(parts, axis=1)


def decay_of(value, damping):
    return 1.0 - (damping + DRAG_RATE * jnp.abs(value))


def send_order(place, source, outs, i=None):
    count, height, _ = source.shape
    rows = slice(0, height) if i is None else pl.ds(pl.multiple_of(i * height, height), height)
    for r, ref in enumerate(outs):
        ref[rows, :] = source[lax.rem(place[0] + r, count)]


def send_edges(current, outs, first=True, last=True):
    stations, height, width = current.shape
    total = outs[1].shape[0]
    empty = jnp.zeros((EDGE - stations, width), F32)

    @pl.when(last)
    def _():
        rows = [current[s, height - 1 : height] for s in range(stations)]
        outs[1][total - EDGE : total] = jnp.concatenate(rows + [empty], axis=0)

    @pl.when(first)
    def _():
        rows = [current[s, 0:1] for s in range(stations)]
        outs[-1][total - EDGE : total] = jnp.concatenate(rows + [empty], axis=0)


def source_kernel(place, current, upstream, inflow, x0, x1, x2, x3, source):
    stations, height, _ = current.shape
    for _, rows in groups(height):
        previous = jnp.where(place[1] == 1, inflow[rows], upstream[rows])
        for s in range(stations):
            here = current[s, rows]
            source[s, rows] = SOURCE_GAIN * (here - previous)
            previous = here
    outs = (x0, x1, x2, x3)
    i = pl.program_id(0)
    send_order(place, source, outs, i)
    send_edges(current, outs, i == 0, i == pl.num_programs(0) - 1)


def decay_kernel(place, current, damping, decay, scale, *copy):
    for g, rows in groups(current.shape[1]):
        product = None
        for s in range(current.shape[0]):
            here = current[s, rows]
            for ref in copy:
                ref[s, rows] = here
            d = decay_of(here, damping[s, rows])
            decay[s, rows] = d
            product = d if product is None else product * d
        to_chunks(scale, g, product)


def weights_kernel(
    place, current, before, after, decay, inflow, term, weights, base, force_weight
):
    stations, height, width = current.shape
    first = place[1] == 1
    above = jnp.where(place[2] == 1, 0.0, before[height : height + EDGE])
    below = jnp.where(place[3] == 1, 0.0, after[height : height + EDGE])
    lane = lax.broadcasted_iota(jnp.int32, (SUB, width), 1)
    for g, rows in groups(height):
        lo, hi = SUB * g, SUB * g + SUB
        total = jnp.zeros((SUB, width), F32)
        factor = None
        for s in reversed(range(stations)):
            here = current[s, rows]
            if g == 0:
                up = jnp.concatenate([above[s : s + 1], current[s, 0 : SUB - 1]], axis=0)
            else:
                up = current[s, lo - 1 : hi - 1]
            if hi == height:
                down = jnp.concatenate([current[s, lo + 1 : hi], below[s : s + 1]], axis=0)
            else:
                down = current[s, lo + 1 : hi + 1]
            left = jnp.where(lane == 0, 0.0, pltpu.roll(here, 1, 1))
            right = jnp.where(lane == width - 1, 0.0, pltpu.roll(here, width - 1, 1))
            t = VISCOSITY * (up + down + left + right - 4.0 * here)
            term[s, rows] = t
            d = decay[s, rows]
            if factor is None:
                total, weight, factor = t, 1.0 - d, d
            else:
                if s == 0:
                    force_weight[rows] = factor
                total, weight, factor = total + factor * t, factor * (1.0 - d), factor * d
            if s == 0:
                entry = jnp.where(first, factor, 0.0)
                weight = weight + entry
                total = total + entry * inflow[rows]
            weights[s, rows] = weight
        base[rows] = total


def far_solve_kernel(
    place, x0, x1, x2, x3, high_far, low_far, inverse_far, p0, p1, p2, p3,
    plane, high, low, inverse, arrivals,
):
    copies = [
        pltpu.make_async_copy(far_ref, ref, arrivals.at[i])
        for i, (far_ref, ref) in enumerate(
            ((high_far, high), (low_far, low), (inverse_far, inverse))
        )
    ]
    solve(place, (x0, x1, x2, x3), (high, low, inverse), (), (p0, p1, p2, p3), plane, copies)


def near_solve_kernel(
    place, x0, x1, x2, x3, high, low, inverse, f0, f1, f2, f3, p0, p1, p2, p3, plane
):
    forces = (f0, f1, f2, f3)
    solve(place, (x0, x1, x2, x3), (high, low, inverse), forces, (p0, p1, p2, p3), plane)


def solve(place, inputs, tables_near, forces, outputs, plane, copies=()):
    c = place[0]
    high, low, inverse = tables_near
    for copy in copies:
        copy.start()
    count = len(inputs)
    height = inputs[0].shape[0]
    for r, ref in enumerate(inputs):
        b = lax.rem(c - r + count, count)
        plane[pl.ds(pl.multiple_of(b * height, height), height), :] = ref[0:height]
    for copy in copies[:2]:
        copy.wait()
    sh, sl = high[...], low[...]
    by_left = jnp.concatenate([sh, sh, sl], axis=1)
    by_right = jnp.concatenate([sh, sl, sh], axis=0)

    def right(value):
        vh, vl = split(value)
        return jnp.dot(
            jnp.concatenate([vh, vh, vl], axis=1), by_right, preferred_element_type=F32
        )

    def left(value):
        vh, vl = split(value)
        return jnp.dot(
            by_left, jnp.concatenate([vh, vl, vh], axis=0), preferred_element_type=F32
        )

    modes = left(right(plane[...]))
    for copy in copies[2:]:
        copy.wait()
    modes = modes * inverse[...]
    plane[...] = right(left(modes))
    for r, ref in enumerate(outputs):
        b = lax.rem(c + r, count)
        ref[0:height] = plane[pl.ds(pl.multiple_of(b * height, height), height), :]
    if forces:
        extra = outputs[0].shape[0] - height
        for r, ref in enumerate(outputs):
            for q in range(height // extra):
                ref[height : height + extra, LANE * q : LANE * (q + 1)] = forces[-r][
                    extra * q : extra * (q + 1)
                ]


def disc_kernel(d0, d1, d2, d3, *rest):
    tabled = (len(rest) - 14) // 2
    where_far, blades_far, tables_far = rest[:3], rest[3], rest[4 : 4 + tabled]
    f0, f1, f2, f3 = rest[4 + tabled : 8 + tabled]
    tables_near = rest[8 + tabled : 8 + 2 * tabled]
    *where, blades, total, sems = rest[8 + 2 * tabled :]
    places, place_row, owners = where
    height, width = d0.shape
    number = places.shape[0]
    pairs = blades.shape[0] // 2
    sources = list(where_far) + list(tables_far)
    targets = where + list(tables_near)
    copies = [
        pltpu.make_async_copy(source, target, sems.at[pairs + i])
        for i, (source, target) in enumerate(zip(sources, targets))
    ]
    fetches = [
        pltpu.make_async_copy(
            blades_far.at[pl.ds(2 * i, 2)], blades.at[pl.ds(2 * i, 2)], sems.at[i]
        )
        for i in range(pairs)
    ]
    for copy in copies[:3] + fetches + copies[3:]:
        copy.start()
    plane = jnp.concatenate([d[...] for d in (d0, d1, d2, d3)], axis=0)
    for copy in copies[:3]:
        copy.wait()
    lane = lax.broadcasted_iota(jnp.int32, (number, LANE), 1)
    chosen = [
        jnp.where(places[...] == lane + LANE * q, 1.0, 0.0).astype(BF16)
        for q in range(width // LANE)
    ]
    picked = jnp.dot(
        jnp.concatenate(chosen, axis=1), plane, preferred_element_type=F32
    ).astype(BF16)
    total[...] = jnp.zeros_like(total)
    for i in range(pairs):
        fetches[i].wait()
        pair = jnp.concatenate([blades[2 * i], blades[2 * i + 1]], axis=1)
        response = jnp.dot(picked, pair, preferred_element_type=F32)
        kept = jnp.where(owners[...] == 2 * i, response[:, :LANE], total[...])
        total[...] = jnp.where(owners[...] == 2 * i + 1, response[:, LANE:], kept)

    rest_of, parts = jnp.tanh(total[...]), []
    for _ in range(3):
        parts.append(rest_of.astype(BF16))
        rest_of = rest_of - parts[-1].astype(F32)
    forces = jnp.concatenate(parts, axis=0)
    at = place_row[0:1]
    for r, ref in enumerate((f0, f1, f2, f3)):
        row = lax.broadcasted_iota(jnp.int32, (height, number), 0) + height * r
        back = jnp.where(row == at, 1.0, 0.0).astype(BF16)
        ref[...] = jnp.dot(
            jnp.concatenate([back] * 3, axis=1), forces, preferred_element_type=F32
        )
    for copy in copies[3:]:
        copy.wait()


def offset_kernel(place, *rest):
    c = place[0]
    pieces = rest[:4]
    *forces, weights, base, force_weight, lead, force, offset = rest[4:]
    count, height, full = weights.shape
    width = full // count
    for r in range(count):
        b = lax.rem(c + r if forces else c - r + count, count)
        lanes = pl.ds(pl.multiple_of(b * width, width), width)
        if forces:
            force[:, lanes] = forces[r][...]
        else:
            extra = pieces[r].shape[0] - height
            for q in range(height // extra):
                force[extra * q : extra * (q + 1), lanes] = pieces[r][
                    height : height + extra, width * q : width * (q + 1)
                ]

    for r in range(count):
        @pl.when(c == r)
        def _():
            lead[...] = pieces[r][0:height]

    for g, rows in groups(height):
        state = base[rows] + force_weight[rows] * force[rows]
        for r in range(count):
            s = lax.rem(c - r + count, count)
            state = state + weights[s, rows] * pieces[r][rows]
        to_chunks(offset, g, state)


def change_kernel(
    place, p0, p1, p2, p3, term, force, decay, inflow,
    change, pressure, decay_near, entry,
):
    c = place[0]
    pieces = (p0, p1, p2, p3)
    count, height, _ = term.shape
    for r in range(count):
        pressure[lax.rem(c - r + count, count)] = pieces[r][...]
    for _, rows in groups(height):
        here = pressure[0, rows]
        entry[rows] = jnp.where(place[1] == 1, inflow[rows], -here)
        for s in range(count):
            value = term[s, rows] + here
            if s == 0:
                value = value + force[rows]
            if s < count - 1:
                here = pressure[s + 1, rows]
                value = value - here
            change[s, rows] = value
            decay_near[s, rows] = decay[s, rows]


def scan_kernel(scale, offset, entering):
    entering[0] = jnp.zeros_like(entering[0])
    state = offset[0]
    for m in range(1, scale.shape[0]):
        entering[m] = state
        state = scale[m] * state + offset[m]


def march_rows(g, rows, entering, change, following, decay, entry):
    stations = decay.shape[0]
    state = from_chunks(entering, g) + entry[rows]
    states = [state]
    for s in range(stations):
        step = change[s, rows]
        if s == stations - 1:
            step = step - following[rows]
        state = decay[s, rows] * state + step
        states.append(state)
    return states


def middle_kernel(
    place, entering, change, following, decay, entry, current, disc, x0, x1, x2, x3, source
):
    stations, height, _ = current.shape
    for g, rows in groups(height):
        states = march_rows(g, rows, entering, change, following, decay, entry)
        for s in range(stations):
            current[s, rows] = states[s + 1]
            source[s, rows] = SOURCE_GAIN * (states[s + 1] - states[s])
    outs = (x0, x1, x2, x3)
    send_order(place, source, outs)
    send_edges(current, outs)
    disc[...] = current[0].astype(BF16)


def last_kernel(entering, change, following, decay, entry, current):
    for g, rows in groups(current.shape[1]):
        states = march_rows(g, rows, entering, change, following, decay, entry)
        for s in range(current.shape[0]):
            current[s, rows] = states[s + 1]


def cost(flops, size):
    return pl.CostEstimate(flops=int(flops), bytes_accessed=int(size), transcendentals=0)


def near(shape, dtype=F32):
    return pltpu.VMEM(shape, dtype)


def far(shape, dtype=F32):
    return pltpu.HBM(shape, dtype)


def stay(value):
    return pltpu.with_memory_space_constraint(value, pltpu.HBM)


def call(kernel, outs, args, work, scalars=0, limit=8, scratch=()):
    return pl.pallas_call(
        kernel,
        out_shape=outs,
        in_specs=[SMEM] * scalars + [VMEM] * (len(args) - scalars),
        out_specs=[VMEM] * len(outs),
        scratch_shapes=list(scratch),
        compiler_params=pltpu.CompilerParams(vmem_limit_bytes=limit * MIB),
        cost_estimate=work,
    )(*args)


def by_rows(kernel, height, outs, place, args, work, whole=(), scratch=()):
    part = height // STEPS

    def spec(shape, index):
        if index in whole:
            return pl.BlockSpec(shape, lambda i, p: (0,) * len(shape))
        if shape[-1] == LANE and len(shape) == 3:
            return pl.BlockSpec((shape[0] // STEPS,) + shape[1:], lambda i, p: (i, 0, 0))
        if len(shape) == 3:
            return pl.BlockSpec((shape[0], part, shape[2]), lambda i, p: (0, i, 0))
        return pl.BlockSpec((part, shape[1]), lambda i, p: (i, 0))

    count = len(args)
    return pl.pallas_call(
        kernel,
        grid_spec=pltpu.PrefetchScalarGridSpec(
            num_scalar_prefetch=1,
            grid=(STEPS,),
            in_specs=[spec(a.shape, None) for a in args],
            out_specs=[spec(a.inner_aval.shape, i) for i, a in enumerate(outs)],
            scratch_shapes=list(scratch),
        ),
        out_shape=outs,
        compiler_params=pltpu.CompilerParams(vmem_limit_bytes=12 * MIB),
        cost_estimate=work,
    )(place, *args)


def disc_forces(rows, where, blades, tabled=()):
    height = rows[0].shape[0]
    count = len(rows)
    number = blades.shape[0]
    brought = [*where, blades, *tabled]
    return pl.pallas_call(
        disc_kernel,
        out_shape=[near((height, LANE))] * count + [near(t.shape, t.dtype) for t in tabled],
        in_specs=[VMEM] * count + [pl.BlockSpec(memory_space=pltpu.HBM)] * len(brought),
        out_specs=[VMEM] * (count + len(tabled)),
        scratch_shapes=[pltpu.VMEM(a.shape, a.dtype) for a in (*where, blades)]
        + [
            pltpu.VMEM((where[0].shape[0], LANE), F32),
            pltpu.SemaphoreType.DMA((number // 2 + 3 + len(tabled),)),
        ],
        compiler_params=pltpu.CompilerParams(vmem_limit_bytes=16 * MIB),
        cost_estimate=cost(2 * number * blade_work(blades), 5 * MIB),
    )(*rows, *map(stay, brought))


def blade_work(blades):
    return blades.shape[1] ** 2 * blades.shape[2]


def local(velocity_guess, damping, inflow, disc_rows, owner, blade):
    stations, height, width = velocity_guess.shape
    march_size = lax.axis_size("march")
    cross_size = lax.axis_size("cross")
    march_index = lax.axis_index("march")
    cross_index = lax.axis_index("cross")
    disc_slab = stations * march_size // 2 // stations
    at_disc = march_index == disc_slab
    first = march_index == 0
    place = jnp.stack(
        [
            cross_index.astype(jnp.int32),
            first.astype(jnp.int32),
            (cross_index == 0).astype(jnp.int32),
            (cross_index == cross_size - 1).astype(jnp.int32),
        ]
    )
    tabled = [stay(jnp.asarray(t)) for t in tables(width)]

    slab = (stations, height, width)
    plane = (height, width)
    edged = (height + EDGE, width)
    chunks = (march_size, height * width // march_size // LANE, LANE)
    sources = [near(plane), near(edged), near(plane), near(edged)]

    def turn(value, steps):
        return lax.ppermute(
            value, "cross", [(i, (i + steps) % cross_size) for i in range(cross_size)]
        )

    def turns(blocks, sign=1):
        return [blocks[0]] + [turn(blocks[r], sign * r) for r in range(1, cross_size)]

    def along_march(value, steps):
        count = march_size
        return lax.ppermute(
            value, "march", [(i, i + steps) for i in range(count) if 0 <= i + steps < count]
        )

    def across_march(value):
        return lax.all_to_all(value, "march", split_axis=0, concat_axis=0, tiled=True)

    blades = lax.all_gather(blade, "march", axis=0, tiled=True)
    turn_of = (cross_index - disc_rows // height + cross_size) % cross_size
    places = turn_of * height + disc_rows % height
    count = disc_rows.shape[0]
    where = (
        jnp.broadcast_to(places[:, None], (count, LANE)),
        jnp.broadcast_to(places[None, :], (SUB, count)),
        jnp.broadcast_to(jnp.where(at_disc, owner, -1)[:, None], (count, LANE)),
    )

    step = (stations, height // STEPS, width)
    near_inflow = stay(inflow)
    upstream = along_march(velocity_guess[-1], 1)
    current = stay(velocity_guess)
    disc = velocity_guess[0].astype(BF16)
    rows = turns([disc] * cross_size)
    source = by_rows(
        source_kernel,
        height,
        sources,
        place,
        (current, upstream, near_inflow),
        cost(1e6, 2 * MIB),
        whole=range(4),
        scratch=[pltpu.VMEM(step, F32)],
    )
    for sweep_index in range(SWEEPS):
        merged = sweep_index > 0
        final = sweep_index == SWEEPS - 1
        if merged:
            rows = turns([disc] * cross_size)
        guess, damp, *source = lax.optimization_barrier((current, damping, *source))
        arrived = turns(source)
        decay, scale, *kept = by_rows(
            decay_kernel,
            height,
            [far(slab), far(chunks)] + [far(slab)] * merged,
            place,
            (guess if merged else stay(guess), stay(damp)),
            cost(4e6, 3 * MIB),
        )
        solve_cost = cost(3 * 8 * width**3, 5 * MIB)
        if merged:
            scale, *arrived = lax.optimization_barrier((scale, *arrived))
            made = disc_forces(rows, where, blades, tabled)
            forces, near_tables = made[:cross_size], made[cross_size:]
            solved = call(
                near_solve_kernel,
                [near((height + height * LANE // width, width))] * cross_size,
                (place, *arrived, *near_tables, *forces),
                solve_cost,
                scalars=1,
                limit=16,
                scratch=[pltpu.VMEM((width, width), F32)],
            )
            scales = across_march(scale)
            forces = []
        else:
            scales = across_march(scale)
            solved = pl.pallas_call(
                far_solve_kernel,
                out_shape=[near(plane)] * cross_size,
                in_specs=[SMEM] + [VMEM] * cross_size + [pl.BlockSpec(memory_space=pltpu.HBM)] * 3,
                out_specs=[VMEM] * cross_size,
                scratch_shapes=[pltpu.VMEM((width, width), F32)]
                + [pltpu.VMEM((width, width), BF16)] * 2
                + [pltpu.VMEM((width, width), F32), pltpu.SemaphoreType.DMA((3,))],
                compiler_params=pltpu.CompilerParams(vmem_limit_bytes=20 * MIB),
                cost_estimate=solve_cost,
            )(place, *arrived, *tabled)
            rows, scales, solved, where = lax.optimization_barrier((rows, scales, solved, where))
            forces = turns(disc_forces(rows, where, blades), -1)
        pieces = turns(solved)
        decay = stay(decay)
        if merged:
            current = stay(kept[0])
        term, weights, base, force_weight = call(
            weights_kernel,
            [far(slab), near(slab), near(plane), near(plane)],
            (place, current, arrived[1], arrived[-1], decay, near_inflow),
            cost(8e6, 4 * MIB),
            scalars=1,
            limit=12,
        )
        lead, force, offset = call(
            offset_kernel,
            [near(plane), far(plane), far(chunks)],
            (place, *pieces, *forces, weights, base, force_weight),
            cost(2e6, 3 * MIB),
            scalars=1,
            limit=12,
        )
        following = along_march(lead, -1)
        offset, force, *pieces = lax.optimization_barrier((offset, force, *pieces))
        change, pressure, decay, entry = by_rows(
            change_kernel,
            height,
            [near(slab), far(slab), near(slab), near(plane)],
            place,
            (*pieces, stay(term), stay(force), decay, near_inflow),
            cost(4e6, 4 * MIB),
        )
        offset = across_march(offset)
        if not merged:
            offset, change = lax.optimization_barrier((offset, change))
        (entering,) = call(scan_kernel, [far(chunks)], (scales, offset), cost(1e5, MIB))
        entering = across_march(entering)
        common = (entering, change, following, decay, entry)
        if final:
            (current,) = call(
                last_kernel, [far(slab)], common, cost(4e6, 5 * MIB), limit=12
            )
            return (current, pressure)
        current, disc, *source = call(
            middle_kernel,
            [near(slab), near(plane, BF16)] + sources,
            (place, *common),
            cost(6e6, 5 * MIB),
            scalars=1,
            limit=12,
            scratch=[pltpu.VMEM(slab, F32)],
        )


def solution(mesh):
    in_specs = (
        P("march", "cross", None),
        P("march", "cross", None),
        P("cross", None),
        P(),
        P(),
        P("march", None, "cross"),
    )
    out_specs = (P("march", "cross", None), P("march", "cross", None))
    return jax.shard_map(local, mesh=mesh, in_specs=in_specs, out_specs=out_specs, check_vma=False)
```

```python
import ml_dtypes
import numpy as np
import jax
import jax.numpy as jnp
from jax import lax
from jax.experimental import pallas as pl
from jax.experimental.pallas import tpu as pltpu
from jax.sharding import PartitionSpec as P

SWEEPS = 2
SOURCE_GAIN = 0.04
SCREENING = 0.001
VISCOSITY = 0.1
DRAG_RATE = 0.01

F32 = jnp.float32
BF16 = jnp.bfloat16
SUB = 8
LANE = 128
EDGE = 8
STEPS = 4
MIB = 1024 * 1024
VMEM = pl.BlockSpec(memory_space=pltpu.VMEM)
SMEM = pl.BlockSpec(memory_space=pltpu.SMEM)


def tables(length):
    ordinal = np.arange(1, length + 1)
    product = np.outer(ordinal, ordinal) % (2 * (length + 1))
    sine = np.sqrt(2.0 / (length + 1)) * np.sin(np.pi * product / (length + 1))
    high = sine.astype(np.float32).astype(ml_dtypes.bfloat16)
    low = (sine - high.astype(np.float64)).astype(np.float32).astype(ml_dtypes.bfloat16)
    values = 2.0 - 2.0 * np.cos(np.pi * ordinal / (length + 1))
    inverse = 1.0 / (SCREENING + values[:, None] + values[None, :])
    return high, low, inverse.astype(np.float32)


def split(value):
    high = value.astype(BF16)
    return high, (value - high.astype(F32)).astype(BF16)


def groups(rows):
    return [(g, slice(SUB * g, SUB * g + SUB)) for g in range(rows // SUB)]


def to_chunks(ref, g, value):
    for h in range(2):
        for q in range(2):
            at = (2 * h + q) * LANE
            ref[2 * g + h, SUB * q : SUB * q + SUB, :] = value[:, at : at + LANE]


def from_chunks(ref, g):
    parts = []
    for h in range(2):
        for q in range(2):
            parts.append(ref[2 * g + h, SUB * q : SUB * q + SUB, :])
    return jnp.concatenate(parts, axis=1)


def decay_of(value, damping):
    return 1.0 - (damping + DRAG_RATE * jnp.abs(value))


def send_order(place, source, outs, i=None):
    count, height, _ = source.shape
    rows = slice(0, height) if i is None else pl.ds(pl.multiple_of(i * height, height), height)
    for r, ref in enumerate(outs):
        ref[rows, :] = source[lax.rem(place[0] + r, count)]


def send_edges(current, outs, first=True, last=True):
    stations, height, width = current.shape
    total = outs[1].shape[0]
    empty = jnp.zeros((EDGE - stations, width), F32)

    @pl.when(last)
    def _():
        rows = [current[s, height - 1 : height] for s in range(stations)]
        outs[1][total - EDGE : total] = jnp.concatenate(rows + [empty], axis=0)

    @pl.when(first)
    def _():
        rows = [current[s, 0:1] for s in range(stations)]
        outs[-1][total - EDGE : total] = jnp.concatenate(rows + [empty], axis=0)


def source_kernel(place, current, upstream, inflow, x0, x1, x2, x3, source):
    stations, height, _ = current.shape
    for _, rows in groups(height):
        previous = jnp.where(place[1] == 1, inflow[rows], upstream[rows])
        for s in range(stations):
            here = current[s, rows]
            source[s, rows] = SOURCE_GAIN * (here - previous)
            previous = here
    outs = (x0, x1, x2, x3)
    i = pl.program_id(0)
    send_order(place, source, outs, i)
    send_edges(current, outs, i == 0, i == pl.num_programs(0) - 1)


def decay_kernel(place, current, damping, decay, scale, *copy):
    for g, rows in groups(current.shape[1]):
        product = None
        for s in range(current.shape[0]):
            here = current[s, rows]
            for ref in copy:
                ref[s, rows] = here
            d = decay_of(here, damping[s, rows])
            decay[s, rows] = d
            product = d if product is None else product * d
        to_chunks(scale, g, product)


def weights_kernel(
    place, current, before, after, decay, inflow, term, weights, base, force_weight
):
    stations, height, width = current.shape
    first = place[1] == 1
    above = jnp.where(place[2] == 1, 0.0, before[height : height + EDGE])
    below = jnp.where(place[3] == 1, 0.0, after[height : height + EDGE])
    lane = lax.broadcasted_iota(jnp.int32, (SUB, width), 1)
    for g, rows in groups(height):
        lo, hi = SUB * g, SUB * g + SUB
        total = jnp.zeros((SUB, width), F32)
        factor = None
        for s in reversed(range(stations)):
            here = current[s, rows]
            if g == 0:
                up = jnp.concatenate([above[s : s + 1], current[s, 0 : SUB - 1]], axis=0)
            else:
                up = current[s, lo - 1 : hi - 1]
            if hi == height:
                down = jnp.concatenate([current[s, lo + 1 : hi], below[s : s + 1]], axis=0)
            else:
                down = current[s, lo + 1 : hi + 1]
            left = jnp.where(lane == 0, 0.0, pltpu.roll(here, 1, 1))
            right = jnp.where(lane == width - 1, 0.0, pltpu.roll(here, width - 1, 1))
            t = VISCOSITY * (up + down + left + right - 4.0 * here)
            term[s, rows] = t
            d = decay[s, rows]
            if factor is None:
                total, weight, factor = t, 1.0 - d, d
            else:
                if s == 0:
                    force_weight[rows] = factor
                total, weight, factor = total + factor * t, factor * (1.0 - d), factor * d
            if s == 0:
                entry = jnp.where(first, factor, 0.0)
                weight = weight + entry
                total = total + entry * inflow[rows]
            weights[s, rows] = weight
        base[rows] = total


def far_solve_kernel(
    place, x0, x1, x2, x3, high_far, low_far, inverse_far, p0, p1, p2, p3,
    plane, high, low, inverse, arrivals,
):
    copies = [
        pltpu.make_async_copy(far_ref, ref, arrivals.at[i])
        for i, (far_ref, ref) in enumerate(
            ((high_far, high), (low_far, low), (inverse_far, inverse))
        )
    ]
    solve(place, (x0, x1, x2, x3), (high, low, inverse), (), (p0, p1, p2, p3), plane, copies)


def near_solve_kernel(
    place, x0, x1, x2, x3, high, low, inverse, f0, f1, f2, f3, p0, p1, p2, p3, plane
):
    forces = (f0, f1, f2, f3)
    solve(place, (x0, x1, x2, x3), (high, low, inverse), forces, (p0, p1, p2, p3), plane)


def solve(place, inputs, tables_near, forces, outputs, plane, copies=()):
    c = place[0]
    high, low, inverse = tables_near
    for copy in copies:
        copy.start()
    count = len(inputs)
    height = inputs[0].shape[0]
    for r, ref in enumerate(inputs):
        b = lax.rem(c - r + count, count)
        plane[pl.ds(pl.multiple_of(b * height, height), height), :] = ref[0:height]
    for copy in copies[:2]:
        copy.wait()
    sh, sl = high[...], low[...]
    by_left = jnp.concatenate([sh, sh, sl], axis=1)
    by_right = jnp.concatenate([sh, sl, sh], axis=0)

    def right(value):
        vh, vl = split(value)
        return jnp.dot(
            jnp.concatenate([vh, vh, vl], axis=1), by_right, preferred_element_type=F32
        )

    def left(value):
        vh, vl = split(value)
        return jnp.dot(
            by_left, jnp.concatenate([vh, vl, vh], axis=0), preferred_element_type=F32
        )

    modes = left(right(plane[...]))
    for copy in copies[2:]:
        copy.wait()
    modes = modes * inverse[...]
    plane[...] = right(left(modes))
    for r, ref in enumerate(outputs):
        b = lax.rem(c + r, count)
        ref[0:height] = plane[pl.ds(pl.multiple_of(b * height, height), height), :]
    if forces:
        extra = outputs[0].shape[0] - height
        for r, ref in enumerate(outputs):
            for q in range(height // extra):
                ref[height : height + extra, LANE * q : LANE * (q + 1)] = forces[-r][
                    extra * q : extra * (q + 1)
                ]


def disc_kernel(d0, d1, d2, d3, places, place_row, owners, *rest):
    streams, tabled = 4, (len(rest) - 11) // 2
    blades, tables_far = rest[:streams], rest[streams : streams + tabled]
    f0, f1, f2, f3 = rest[streams + tabled : streams + tabled + 4]
    tables_near = rest[streams + tabled + 4 : streams + 2 * tabled + 4]
    picked, total = rest[streams + 2 * tabled + 4 : streams + 2 * tabled + 6]
    step = pl.program_id(0)
    last = pl.num_programs(0) - 1
    height, width = d0.shape
    number = picked.shape[0]
    copies = [
        pltpu.make_async_copy(source, target, rest[-1].at[i])
        for i, (source, target) in enumerate(zip(tables_far, tables_near))
    ]

    @pl.when(step == 0)
    def _():
        for copy in copies:
            copy.start()
        plane = jnp.concatenate([d[...] for d in (d0, d1, d2, d3)], axis=0)
        lane = lax.broadcasted_iota(jnp.int32, (number, LANE), 1)
        chosen = [
            jnp.where(places[...] == lane + LANE * q, 1.0, 0.0).astype(BF16)
            for q in range(width // LANE)
        ]
        rows = jnp.dot(
            jnp.concatenate(chosen, axis=1), plane, preferred_element_type=F32
        )
        picked[...] = rows.astype(BF16)
        total[...] = jnp.zeros_like(total)

    per_step = blades[0].shape[0]
    for i in range(0, per_step, 2):
        pair = jnp.concatenate(
            [
                jnp.concatenate([blade[j] for blade in blades], axis=0)
                for j in (i, i + 1)
            ],
            axis=1,
        )
        response = jnp.dot(picked[...], pair, preferred_element_type=F32)
        first = step * per_step + i
        kept = jnp.where(owners[...] == first, response[:, :LANE], total[...])
        total[...] = jnp.where(owners[...] == first + 1, response[:, LANE:], kept)

    @pl.when(step == last)
    def _():
        rest_of, parts = jnp.tanh(total[...]), []
        for _ in range(3):
            parts.append(rest_of.astype(BF16))
            rest_of = rest_of - parts[-1].astype(F32)
        forces = jnp.concatenate(parts, axis=0)
        at = place_row[0:1]
        for r, ref in enumerate((f0, f1, f2, f3)):
            row = lax.broadcasted_iota(jnp.int32, (height, number), 0) + height * r
            back = jnp.where(row == at, 1.0, 0.0).astype(BF16)
            ref[...] = jnp.dot(
                jnp.concatenate([back] * 3, axis=1), forces, preferred_element_type=F32
            )
        for copy in copies:
            copy.wait()


def offset_kernel(place, *rest):
    c = place[0]
    pieces = rest[:4]
    *forces, weights, base, force_weight, lead, force, offset = rest[4:]
    count, height, full = weights.shape
    width = full // count
    for r in range(count):
        b = lax.rem(c + r if forces else c - r + count, count)
        lanes = pl.ds(pl.multiple_of(b * width, width), width)
        if forces:
            force[:, lanes] = forces[r][...]
        else:
            extra = pieces[r].shape[0] - height
            for q in range(height // extra):
                force[extra * q : extra * (q + 1), lanes] = pieces[r][
                    height : height + extra, width * q : width * (q + 1)
                ]

    for r in range(count):
        @pl.when(c == r)
        def _():
            lead[...] = pieces[r][0:height]

    for g, rows in groups(height):
        state = base[rows] + force_weight[rows] * force[rows]
        for r in range(count):
            s = lax.rem(c - r + count, count)
            state = state + weights[s, rows] * pieces[r][rows]
        to_chunks(offset, g, state)


def change_kernel(
    place, p0, p1, p2, p3, term, force, decay, inflow,
    change, decay_near, pressure,
):
    c = place[0]
    pieces = (p0, p1, p2, p3)
    count, height, _ = term.shape
    for r in range(count):
        pressure[lax.rem(c - r + count, count)] = pieces[r][0:height]
    for _, rows in groups(height):
        here = pressure[0, rows]
        entry = jnp.where(place[1] == 1, inflow[rows], -here)
        if change.shape[0] > count:
            change[count, rows] = entry
        for s in range(count):
            value = term[s, rows] + here
            if s == 0:
                value = value + force[rows]
            if s < count - 1:
                here = pressure[s + 1, rows]
                value = value - here
            d = decay[s, rows]
            decay_near[s, rows] = d
            if s == 0 and change.shape[0] == count:
                value = value + d * entry
            change[s, rows] = value


def scan_kernel(scale, offset, entering):
    entering[0] = jnp.zeros_like(entering[0])
    state = offset[0]
    for m in range(1, scale.shape[0]):
        entering[m] = state
        state = scale[m] * state + offset[m]


def march_rows(g, rows, entering, change, following, decay):
    stations = decay.shape[0]
    state = from_chunks(entering, g)
    if change.shape[0] > stations:
        state = state + change[stations, rows]
    states = [state]
    for s in range(stations):
        step = change[s, rows]
        if s == stations - 1:
            step = step - following[rows]
        state = decay[s, rows] * state + step
        states.append(state)
    return states


def middle_kernel(
    place, entering, change, following, decay, current, disc, x0, x1, x2, x3, source
):
    stations, height, _ = current.shape
    for g, rows in groups(height):
        states = march_rows(g, rows, entering, change, following, decay)
        for s in range(stations):
            current[s, rows] = states[s + 1]
            source[s, rows] = SOURCE_GAIN * (states[s + 1] - states[s])
    outs = (x0, x1, x2, x3)
    send_order(place, source, outs)
    send_edges(current, outs)
    disc[...] = current[0].astype(BF16)


def last_kernel(entering, change, following, decay, current):
    for g, rows in groups(current.shape[1]):
        states = march_rows(g, rows, entering, change, following, decay)
        for s in range(current.shape[0]):
            current[s, rows] = states[s + 1]


def cost(flops, size):
    return pl.CostEstimate(flops=int(flops), bytes_accessed=int(size), transcendentals=0)


def near(shape, dtype=F32):
    return pltpu.VMEM(shape, dtype)


def far(shape, dtype=F32):
    return pltpu.HBM(shape, dtype)


def stay(value):
    return pltpu.with_memory_space_constraint(value, pltpu.HBM)


def call(kernel, outs, args, work, scalars=0, limit=8, scratch=()):
    return pl.pallas_call(
        kernel,
        out_shape=outs,
        in_specs=[SMEM] * scalars + [VMEM] * (len(args) - scalars),
        out_specs=[VMEM] * len(outs),
        scratch_shapes=list(scratch),
        compiler_params=pltpu.CompilerParams(vmem_limit_bytes=limit * MIB),
        cost_estimate=work,
    )(*args)


def by_rows(kernel, height, outs, place, args, work, whole=(), scratch=()):
    part = height // STEPS

    def spec(shape, index):
        if index in whole:
            return pl.BlockSpec(shape, lambda i, p: (0,) * len(shape))
        if shape[-1] == LANE and len(shape) == 3:
            return pl.BlockSpec((shape[0] // STEPS,) + shape[1:], lambda i, p: (i, 0, 0))
        if len(shape) == 3:
            return pl.BlockSpec((shape[0], part, shape[2]), lambda i, p: (0, i, 0))
        return pl.BlockSpec((part, shape[1]), lambda i, p: (i, 0))

    count = len(args)
    return pl.pallas_call(
        kernel,
        grid_spec=pltpu.PrefetchScalarGridSpec(
            num_scalar_prefetch=1,
            grid=(STEPS,),
            in_specs=[spec(a.shape, None) for a in args],
            out_specs=[spec(a.inner_aval.shape, i) for i, a in enumerate(outs)],
            scratch_shapes=list(scratch),
        ),
        out_shape=outs,
        compiler_params=pltpu.CompilerParams(vmem_limit_bytes=12 * MIB),
        cost_estimate=work,
    )(place, *args)


def disc_forces(rows, where, blades, tabled=()):
    height, width = rows[0].shape
    count = len(rows)
    number = blades.shape[0]
    per_step, streams = 8, 4
    fixed = lambda shape: pl.BlockSpec(shape, lambda i: (0,) * len(shape))
    table = lambda k: pl.BlockSpec((per_step, width // streams, LANE), lambda i: (i, k, 0))
    discs = where[0].shape[0]
    return pl.pallas_call(
        disc_kernel,
        grid=(number // per_step,),
        out_shape=[near((height, LANE))] * count + [near(t.shape, t.dtype) for t in tabled],
        in_specs=[fixed((height, width))] * count
        + [fixed(w.shape) for w in where]
        + [table(k) for k in range(streams)]
        + [pl.BlockSpec(memory_space=pltpu.HBM)] * len(tabled),
        out_specs=[fixed((height, LANE))] * count
        + [pl.BlockSpec(memory_space=pltpu.VMEM)] * len(tabled),
        scratch_shapes=[
            pltpu.VMEM((discs, width), BF16),
            pltpu.VMEM((discs, LANE), F32),
            pltpu.SemaphoreType.DMA((3,)),
        ],
        compiler_params=pltpu.CompilerParams(vmem_limit_bytes=16 * MIB),
        cost_estimate=cost(2 * number * width * width * LANE, 5 * MIB),
    )(*rows, *map(stay, where), *[stay(blades)] * streams, *tabled)


def local(velocity_guess, damping, inflow, disc_rows, owner, blade):
    stations, height, width = velocity_guess.shape
    march_size = lax.axis_size("march")
    cross_size = lax.axis_size("cross")
    march_index = lax.axis_index("march")
    cross_index = lax.axis_index("cross")
    disc_slab = stations * march_size // 2 // stations
    at_disc = march_index == disc_slab
    first = march_index == 0
    place = jnp.stack(
        [
            cross_index.astype(jnp.int32),
            first.astype(jnp.int32),
            (cross_index == 0).astype(jnp.int32),
            (cross_index == cross_size - 1).astype(jnp.int32),
        ]
    )
    tabled = [stay(jnp.asarray(t)) for t in tables(width)]

    slab = (stations, height, width)
    plane = (height, width)
    edged = (height + EDGE, width)
    chunks = (march_size, height * width // march_size // LANE, LANE)
    sources = [near(plane), near(edged), near(plane), near(edged)]

    def turn(value, steps):
        return lax.ppermute(
            value, "cross", [(i, (i + steps) % cross_size) for i in range(cross_size)]
        )

    def turns(blocks, sign=1):
        return [blocks[0]] + [turn(blocks[r], sign * r) for r in range(1, cross_size)]

    def along_march(value, steps):
        count = march_size
        return lax.ppermute(
            value, "march", [(i, i + steps) for i in range(count) if 0 <= i + steps < count]
        )

    def across_march(value):
        return lax.all_to_all(value, "march", split_axis=0, concat_axis=0, tiled=True)

    blades = lax.all_gather(blade, "march", axis=0, tiled=True)
    turn_of = (cross_index - disc_rows // height + cross_size) % cross_size
    places = turn_of * height + disc_rows % height
    count = disc_rows.shape[0]
    where = (
        jnp.broadcast_to(places[:, None], (count, LANE)),
        jnp.broadcast_to(places[None, :], (SUB, count)),
        jnp.broadcast_to(jnp.where(at_disc, owner, -1)[:, None], (count, LANE)),
    )

    step = (stations, height // STEPS, width)
    near_inflow = stay(inflow)
    upstream = along_march(velocity_guess[-1], 1)
    current = stay(velocity_guess)
    disc = velocity_guess[0].astype(BF16)
    rows = turns([disc] * cross_size)
    source = by_rows(
        source_kernel,
        height,
        sources,
        place,
        (current, upstream, near_inflow),
        cost(1e6, 2 * MIB),
        whole=range(4),
        scratch=[pltpu.VMEM(step, F32)],
    )
    for sweep_index in range(SWEEPS):
        merged = sweep_index > 0
        final = sweep_index == SWEEPS - 1
        if merged:
            rows = turns([disc] * cross_size)
        guess, damp, *source = lax.optimization_barrier((current, damping, *source))
        arrived = turns(source)
        decay, scale, *kept = by_rows(
            decay_kernel,
            height,
            [far(slab), far(chunks)] + [far(slab)] * merged,
            place,
            (guess if merged else stay(guess), stay(damp)),
            cost(4e6, 3 * MIB),
        )
        solve_cost = cost(3 * 8 * width**3, 5 * MIB)
        if merged:
            scale, *arrived = lax.optimization_barrier((scale, *arrived))
            made = disc_forces(rows, where, blades, tabled)
            forces, near_tables = made[:cross_size], made[cross_size:]
            solved = call(
                near_solve_kernel,
                [near((height + height * LANE // width, width))] * cross_size,
                (place, *arrived, *near_tables, *forces),
                solve_cost,
                scalars=1,
                limit=16,
                scratch=[pltpu.VMEM((width, width), F32)],
            )
            scales = across_march(scale)
            forces = []
        else:
            scales = across_march(scale)
            solved = pl.pallas_call(
                far_solve_kernel,
                out_shape=[near(plane)] * cross_size,
                in_specs=[SMEM] + [VMEM] * cross_size + [pl.BlockSpec(memory_space=pltpu.HBM)] * 3,
                out_specs=[VMEM] * cross_size,
                scratch_shapes=[pltpu.VMEM((width, width), F32)]
                + [pltpu.VMEM((width, width), BF16)] * 2
                + [pltpu.VMEM((width, width), F32), pltpu.SemaphoreType.DMA((3,))],
                compiler_params=pltpu.CompilerParams(vmem_limit_bytes=20 * MIB),
                cost_estimate=solve_cost,
            )(place, *arrived, *tabled)
            rows, scales, solved, where = lax.optimization_barrier((rows, scales, solved, where))
            forces = turns(disc_forces(rows, where, blades), -1)
        pieces = turns(solved)
        decay = stay(decay)
        if merged:
            current = stay(kept[0])
        term, weights, base, force_weight = call(
            weights_kernel,
            [far(slab), near(slab), near(plane), near(plane)],
            (place, current, arrived[1], arrived[-1], decay, near_inflow),
            cost(8e6, 4 * MIB),
            scalars=1,
            limit=12,
        )
        lead, force, offset = call(
            offset_kernel,
            [near(plane), far(plane), far(chunks)],
            (place, *pieces, *forces, weights, base, force_weight),
            cost(2e6, 3 * MIB),
            scalars=1,
            limit=12,
        )
        following = along_march(lead, -1)
        offset, force, *pieces = lax.optimization_barrier((offset, force, *pieces))
        change, decay, *pressure = call(
            change_kernel,
            [near((stations + (not final), *plane)), near(slab)] + [far(slab)] * final,
            (place, *pieces, stay(term), stay(force), decay, near_inflow),
            cost(4e6, 4 * MIB),
            scalars=1,
            limit=12,
            scratch=[] if final else [pltpu.VMEM(slab, F32)],
        )
        offset = across_march(offset)
        (entering,) = call(scan_kernel, [far(chunks)], (scales, offset), cost(1e5, MIB))
        entering = across_march(entering)
        common = (entering, change, following, decay)
        if final:
            (current,) = call(
                last_kernel, [far(slab)], common, cost(4e6, 5 * MIB), limit=12
            )
            return (current, pressure[0])
        current, disc, *source = call(
            middle_kernel,
            [near(slab), near(plane, BF16)] + sources,
            (place, *common),
            cost(6e6, 5 * MIB),
            scalars=1,
            limit=12,
            scratch=[pltpu.VMEM(slab, F32)],
        )


def solution(mesh):
    in_specs = (
        P("march", "cross", None),
        P("march", "cross", None),
        P("cross", None),
        P(),
        P(),
        P("march", None, "cross"),
    )
    out_specs = (P("march", "cross", None), P("march", "cross", None))
    return jax.shard_map(local, mesh=mesh, in_specs=in_specs, out_specs=out_specs, check_vma=False)
```

```python
import ml_dtypes
import numpy as np
import jax
import jax.numpy as jnp
from jax import lax
from jax.experimental import pallas as pl
from jax.experimental.pallas import tpu as pltpu
from jax.sharding import PartitionSpec as P

SWEEPS = 2
SOURCE_GAIN = 0.04
SCREENING = 0.001
VISCOSITY = 0.1
DRAG_RATE = 0.01

F32 = jnp.float32
BF16 = jnp.bfloat16
SUB = 8
LANE = 128
EDGE = 8
STEPS = 4
MIB = 1024 * 1024
VMEM = pl.BlockSpec(memory_space=pltpu.VMEM)
SMEM = pl.BlockSpec(memory_space=pltpu.SMEM)


def tables(length):
    ordinal = np.arange(1, length + 1)
    product = np.outer(ordinal, ordinal) % (2 * (length + 1))
    sine = np.sqrt(2.0 / (length + 1)) * np.sin(np.pi * product / (length + 1))
    high = sine.astype(np.float32).astype(ml_dtypes.bfloat16)
    low = (sine - high.astype(np.float64)).astype(np.float32).astype(ml_dtypes.bfloat16)
    values = 2.0 - 2.0 * np.cos(np.pi * ordinal / (length + 1))
    inverse = 1.0 / (SCREENING + values[:, None] + values[None, :])
    return high, low, inverse.astype(np.float32)


def split(value):
    high = value.astype(BF16)
    return high, (value - high.astype(F32)).astype(BF16)


def groups(rows):
    return [(g, slice(SUB * g, SUB * g + SUB)) for g in range(rows // SUB)]


def to_chunks(ref, g, value):
    for h in range(2):
        for q in range(2):
            at = (2 * h + q) * LANE
            ref[2 * g + h, SUB * q : SUB * q + SUB, :] = value[:, at : at + LANE]


def from_chunks(ref, g):
    parts = []
    for h in range(2):
        for q in range(2):
            parts.append(ref[2 * g + h, SUB * q : SUB * q + SUB, :])
    return jnp.concatenate(parts, axis=1)


def far_first(blocks):
    return (blocks[0], blocks[2], blocks[1], blocks[3])


def decay_of(value, damping):
    return 1.0 - (damping + DRAG_RATE * jnp.abs(value))


def send_order(place, source, outs, i=None):
    count, height, _ = source.shape
    rows = slice(0, height) if i is None else pl.ds(pl.multiple_of(i * height, height), height)
    for r, ref in enumerate(outs):
        ref[rows, :] = source[lax.rem(place[0] + r, count)]
        if 1 < r < count - 1:
            ref[ref.shape[0] - EDGE :, :] = jnp.zeros((EDGE, ref.shape[1]), F32)


def send_edges(current, outs, first=True, last=True):
    stations, height, width = current.shape
    total = outs[1].shape[0]
    empty = jnp.zeros((EDGE - stations, width), F32)

    @pl.when(last)
    def _():
        rows = [current[s, height - 1 : height] for s in range(stations)]
        outs[1][total - EDGE : total] = jnp.concatenate(rows + [empty], axis=0)

    @pl.when(first)
    def _():
        rows = [current[s, 0:1] for s in range(stations)]
        outs[-1][total - EDGE : total] = jnp.concatenate(rows + [empty], axis=0)


def source_kernel(place, current, upstream, inflow, x0, x1, x2, x3, source):
    stations, height, _ = current.shape
    for _, rows in groups(height):
        previous = jnp.where(place[1] == 1, inflow[rows], upstream[rows])
        for s in range(stations):
            here = current[s, rows]
            source[s, rows] = SOURCE_GAIN * (here - previous)
            previous = here
    outs = (x0, x1, x2, x3)
    i = pl.program_id(0)
    send_order(place, source, outs, i)
    send_edges(current, outs, i == 0, i == pl.num_programs(0) - 1)


def decay_kernel(place, current, damping, decay, scale, *copy):
    for g, rows in groups(current.shape[1]):
        product = None
        for s in range(current.shape[0]):
            here = current[s, rows]
            for ref in copy:
                ref[s, rows] = here
            d = decay_of(here, damping[s, rows])
            decay[s, rows] = d
            product = d if product is None else product * d
        to_chunks(scale, g, product)


def weights_kernel(
    place, current, before, after, decay, inflow, term, weights, base, force_weight
):
    stations, height, width = current.shape
    first = place[1] == 1
    above = jnp.where(place[2] == 1, 0.0, before[height : height + EDGE])
    below = jnp.where(place[3] == 1, 0.0, after[height : height + EDGE])
    lane = lax.broadcasted_iota(jnp.int32, (SUB, width), 1)
    for g, rows in groups(height):
        lo, hi = SUB * g, SUB * g + SUB
        total = jnp.zeros((SUB, width), F32)
        factor = None
        for s in reversed(range(stations)):
            here = current[s, rows]
            if g == 0:
                up = jnp.concatenate([above[s : s + 1], current[s, 0 : SUB - 1]], axis=0)
            else:
                up = current[s, lo - 1 : hi - 1]
            if hi == height:
                down = jnp.concatenate([current[s, lo + 1 : hi], below[s : s + 1]], axis=0)
            else:
                down = current[s, lo + 1 : hi + 1]
            left = jnp.where(lane == 0, 0.0, pltpu.roll(here, 1, 1))
            right = jnp.where(lane == width - 1, 0.0, pltpu.roll(here, width - 1, 1))
            t = VISCOSITY * (up + down + left + right - 4.0 * here)
            term[s, rows] = t
            d = decay[s, rows]
            if factor is None:
                total, weight, factor = t, 1.0 - d, d
            else:
                if s == 0:
                    force_weight[rows] = factor
                total, weight, factor = total + factor * t, factor * (1.0 - d), factor * d
            if s == 0:
                entry = jnp.where(first, factor, 0.0)
                weight = weight + entry
                total = total + entry * inflow[rows]
            weights[s, rows] = weight
        base[rows] = total


def far_solve_kernel(
    place, x0, x2, x1, x3, high_far, low_far, inverse_far, p0, p1, p2, p3,
    plane, high, low, inverse, arrivals,
):
    copies = [
        pltpu.make_async_copy(far_ref, ref, arrivals.at[i])
        for i, (far_ref, ref) in enumerate(
            ((high_far, high), (low_far, low), (inverse_far, inverse))
        )
    ]
    solve(place, (x0, x1, x2, x3), (high, low, inverse), (), (p0, p1, p2, p3), plane, copies)


def near_solve_kernel(
    place, x0, x2, x1, x3, high, low, inverse, f0, f1, f2, f3, p0, p1, p2, p3, plane
):
    forces = (f0, f1, f2, f3)
    solve(place, (x0, x1, x2, x3), (high, low, inverse), forces, (p0, p1, p2, p3), plane)


def solve(place, inputs, tables_near, forces, outputs, plane, copies=()):
    c = place[0]
    high, low, inverse = tables_near
    for copy in copies:
        copy.start()
    count = len(inputs)
    height = inputs[0].shape[0]
    for r, ref in enumerate(inputs):
        b = lax.rem(c - r + count, count)
        plane[pl.ds(pl.multiple_of(b * height, height), height), :] = ref[0:height]
    for copy in copies[:2]:
        copy.wait()
    sh, sl = high[...], low[...]
    by_left = jnp.concatenate([sh, sh, sl], axis=1)
    by_right = jnp.concatenate([sh, sl, sh], axis=0)

    def right(value):
        vh, vl = split(value)
        return jnp.dot(
            jnp.concatenate([vh, vh, vl], axis=1), by_right, preferred_element_type=F32
        )

    def left(value):
        vh, vl = split(value)
        return jnp.dot(
            by_left, jnp.concatenate([vh, vl, vh], axis=0), preferred_element_type=F32
        )

    modes = left(right(plane[...]))
    for copy in copies[2:]:
        copy.wait()
    modes = modes * inverse[...]
    plane[...] = right(left(modes))
    for r, ref in enumerate(outputs):
        b = lax.rem(c + r, count)
        ref[0:height] = plane[pl.ds(pl.multiple_of(b * height, height), height), :]
    if forces:
        extra = outputs[0].shape[0] - height
        for r, ref in enumerate(outputs):
            for q in range(height // extra):
                ref[height : height + extra, LANE * q : LANE * (q + 1)] = forces[-r][
                    extra * q : extra * (q + 1)
                ]


def disc_kernel(d0, d1, d2, d3, places, place_row, owners, *rest):
    streams, tabled = 4, (len(rest) - 11) // 2
    blades, tables_far = rest[:streams], rest[streams : streams + tabled]
    f0, f1, f2, f3 = rest[streams + tabled : streams + tabled + 4]
    tables_near = rest[streams + tabled + 4 : streams + 2 * tabled + 4]
    picked, total = rest[streams + 2 * tabled + 4 : streams + 2 * tabled + 6]
    step = pl.program_id(0)
    last = pl.num_programs(0) - 1
    height, width = d0.shape
    number = picked.shape[0]
    copies = [
        pltpu.make_async_copy(source, target, rest[-1].at[i])
        for i, (source, target) in enumerate(zip(tables_far, tables_near))
    ]

    @pl.when(step == 0)
    def _():
        for copy in copies:
            copy.start()
        plane = jnp.concatenate([d[...] for d in (d0, d1, d2, d3)], axis=0)
        lane = lax.broadcasted_iota(jnp.int32, (number, LANE), 1)
        chosen = [
            jnp.where(places[...] == lane + LANE * q, 1.0, 0.0).astype(BF16)
            for q in range(width // LANE)
        ]
        rows = jnp.dot(
            jnp.concatenate(chosen, axis=1), plane, preferred_element_type=F32
        )
        picked[...] = rows.astype(BF16)
        total[...] = jnp.zeros_like(total)

    per_step = blades[0].shape[0]
    for i in range(0, per_step, 2):
        pair = jnp.concatenate(
            [
                jnp.concatenate([blade[j] for blade in blades], axis=0)
                for j in (i, i + 1)
            ],
            axis=1,
        )
        response = jnp.dot(picked[...], pair, preferred_element_type=F32)
        first = step * per_step + i
        kept = jnp.where(owners[...] == first, response[:, :LANE], total[...])
        total[...] = jnp.where(owners[...] == first + 1, response[:, LANE:], kept)

    @pl.when(step == last)
    def _():
        rest_of, parts = jnp.tanh(total[...]), []
        for _ in range(3):
            parts.append(rest_of.astype(BF16))
            rest_of = rest_of - parts[-1].astype(F32)
        forces = jnp.concatenate(parts, axis=0)
        at = place_row[0:1]
        for r, ref in enumerate((f0, f1, f2, f3)):
            row = lax.broadcasted_iota(jnp.int32, (height, number), 0) + height * r
            back = jnp.where(row == at, 1.0, 0.0).astype(BF16)
            ref[...] = jnp.dot(
                jnp.concatenate([back] * 3, axis=1), forces, preferred_element_type=F32
            )
        for copy in copies:
            copy.wait()


def offset_kernel(place, *rest):
    c = place[0]
    pieces = far_first(rest[:4])
    *forces, weights, base, force_weight, lead, force, offset = rest[4:]
    count, height, full = weights.shape
    width = full // count
    for r in range(count):
        b = lax.rem(c + r if forces else c - r + count, count)
        lanes = pl.ds(pl.multiple_of(b * width, width), width)
        if forces:
            force[:, lanes] = forces[r][...]
        else:
            extra = pieces[r].shape[0] - height
            for q in range(height // extra):
                force[extra * q : extra * (q + 1), lanes] = pieces[r][
                    height : height + extra, width * q : width * (q + 1)
                ]

    for r in range(count):
        @pl.when(c == r)
        def _():
            lead[...] = pieces[r][0:height]

    for g, rows in groups(height):
        state = base[rows] + force_weight[rows] * force[rows]
        for r in range(count):
            s = lax.rem(c - r + count, count)
            state = state + weights[s, rows] * pieces[r][rows]
        to_chunks(offset, g, state)


def change_kernel(
    place, p0, p1, p2, p3, term, force, decay, inflow,
    change, decay_near, pressure,
):
    c = place[0]
    pieces = (p0, p1, p2, p3)
    count, height, _ = term.shape
    for r in range(count):
        pressure[lax.rem(c - r + count, count)] = pieces[r][0:height]
    for _, rows in groups(height):
        here = pressure[0, rows]
        entry = jnp.where(place[1] == 1, inflow[rows], -here)
        if change.shape[0] > count:
            change[count, rows] = entry
        for s in range(count):
            value = term[s, rows] + here
            if s == 0:
                value = value + force[rows]
            if s < count - 1:
                here = pressure[s + 1, rows]
                value = value - here
            d = decay[s, rows]
            decay_near[s, rows] = d
            if s == 0 and change.shape[0] == count:
                value = value + d * entry
            change[s, rows] = value


def scan_kernel(scale, offset, entering):
    entering[0] = jnp.zeros_like(entering[0])
    state = offset[0]
    for m in range(1, scale.shape[0]):
        entering[m] = state
        state = scale[m] * state + offset[m]


def march_rows(g, rows, entering, change, following, decay):
    stations = decay.shape[0]
    state = from_chunks(entering, g)
    if change.shape[0] > stations:
        state = state + change[stations, rows]
    states = [state]
    for s in range(stations):
        step = change[s, rows]
        if s == stations - 1:
            step = step - following[rows]
        state = decay[s, rows] * state + step
        states.append(state)
    return states


def middle_kernel(
    place, entering, change, following, decay, current, disc, x0, x1, x2, x3, source
):
    stations, height, _ = current.shape
    for g, rows in groups(height):
        states = march_rows(g, rows, entering, change, following, decay)
        for s in range(stations):
            current[s, rows] = states[s + 1]
            source[s, rows] = SOURCE_GAIN * (states[s + 1] - states[s])
    outs = (x0, x1, x2, x3)
    send_order(place, source, outs)
    send_edges(current, outs)
    disc[...] = current[0].astype(BF16)


def last_kernel(entering, change, following, decay, current):
    for g, rows in groups(current.shape[1]):
        states = march_rows(g, rows, entering, change, following, decay)
        for s in range(current.shape[0]):
            current[s, rows] = states[s + 1]


def cost(flops, size):
    return pl.CostEstimate(flops=int(flops), bytes_accessed=int(size), transcendentals=0)


def near(shape, dtype=F32):
    return pltpu.VMEM(shape, dtype)


def far(shape, dtype=F32):
    return pltpu.HBM(shape, dtype)


def stay(value):
    return pltpu.with_memory_space_constraint(value, pltpu.HBM)


def call(kernel, outs, args, work, scalars=0, limit=8, scratch=()):
    return pl.pallas_call(
        kernel,
        out_shape=outs,
        in_specs=[SMEM] * scalars + [VMEM] * (len(args) - scalars),
        out_specs=[VMEM] * len(outs),
        scratch_shapes=list(scratch),
        compiler_params=pltpu.CompilerParams(vmem_limit_bytes=limit * MIB),
        cost_estimate=work,
    )(*args)


def by_rows(kernel, height, outs, place, args, work, whole=(), scratch=()):
    part = height // STEPS

    def spec(shape, index):
        if index in whole:
            return pl.BlockSpec(shape, lambda i, p: (0,) * len(shape))
        if shape[-1] == LANE and len(shape) == 3:
            return pl.BlockSpec((shape[0] // STEPS,) + shape[1:], lambda i, p: (i, 0, 0))
        if len(shape) == 3:
            return pl.BlockSpec((shape[0], part, shape[2]), lambda i, p: (0, i, 0))
        return pl.BlockSpec((part, shape[1]), lambda i, p: (i, 0))

    count = len(args)
    return pl.pallas_call(
        kernel,
        grid_spec=pltpu.PrefetchScalarGridSpec(
            num_scalar_prefetch=1,
            grid=(STEPS,),
            in_specs=[spec(a.shape, None) for a in args],
            out_specs=[spec(a.inner_aval.shape, i) for i, a in enumerate(outs)],
            scratch_shapes=list(scratch),
        ),
        out_shape=outs,
        compiler_params=pltpu.CompilerParams(vmem_limit_bytes=12 * MIB),
        cost_estimate=work,
    )(place, *args)


def disc_forces(rows, where, blades, tabled=()):
    height, width = rows[0].shape
    count = len(rows)
    number = blades.shape[0]
    per_step, streams = 8, 4
    fixed = lambda shape: pl.BlockSpec(shape, lambda i: (0,) * len(shape))
    table = lambda k: pl.BlockSpec((per_step, width // streams, LANE), lambda i: (i, k, 0))
    discs = where[0].shape[0]
    return pl.pallas_call(
        disc_kernel,
        grid=(number // per_step,),
        out_shape=[near((height, LANE))] * count + [near(t.shape, t.dtype) for t in tabled],
        in_specs=[fixed((height, width))] * count
        + [fixed(w.shape) for w in where]
        + [table(k) for k in range(streams)]
        + [pl.BlockSpec(memory_space=pltpu.HBM)] * len(tabled),
        out_specs=[fixed((height, LANE))] * count
        + [pl.BlockSpec(memory_space=pltpu.VMEM)] * len(tabled),
        scratch_shapes=[
            pltpu.VMEM((discs, width), BF16),
            pltpu.VMEM((discs, LANE), F32),
            pltpu.SemaphoreType.DMA((3,)),
        ],
        compiler_params=pltpu.CompilerParams(vmem_limit_bytes=16 * MIB),
        cost_estimate=cost(2 * number * width * width * LANE, 5 * MIB),
    )(*rows, *map(stay, where), *[stay(blades)] * streams, *tabled)


def local(velocity_guess, damping, inflow, disc_rows, owner, blade):
    stations, height, width = velocity_guess.shape
    march_size = lax.axis_size("march")
    cross_size = lax.axis_size("cross")
    march_index = lax.axis_index("march")
    cross_index = lax.axis_index("cross")
    disc_slab = stations * march_size // 2 // stations
    at_disc = march_index == disc_slab
    first = march_index == 0
    place = jnp.stack(
        [
            cross_index.astype(jnp.int32),
            first.astype(jnp.int32),
            (cross_index == 0).astype(jnp.int32),
            (cross_index == cross_size - 1).astype(jnp.int32),
        ]
    )
    tabled = [stay(jnp.asarray(t)) for t in tables(width)]

    slab = (stations, height, width)
    plane = (height, width)
    edged = (height + EDGE, width)
    chunks = (march_size, height * width // march_size // LANE, LANE)
    sources = [near(plane)] + [near(edged)] * (cross_size - 1)

    def turn(value, steps):
        return lax.ppermute(
            value, "cross", [(i, (i + steps) % cross_size) for i in range(cross_size)]
        )

    def turns(blocks, sign=1):
        return [blocks[0]] + [turn(blocks[r], sign * r) for r in range(1, cross_size)]

    def along_march(value, steps):
        count = march_size
        return lax.ppermute(
            value, "march", [(i, i + steps) for i in range(count) if 0 <= i + steps < count]
        )

    def across_march(value):
        return lax.all_to_all(value, "march", split_axis=0, concat_axis=0, tiled=True)

    blades = lax.all_gather(blade, "march", axis=0, tiled=True)
    turn_of = (cross_index - disc_rows // height + cross_size) % cross_size
    places = turn_of * height + disc_rows % height
    count = disc_rows.shape[0]
    where = (
        jnp.broadcast_to(places[:, None], (count, LANE)),
        jnp.broadcast_to(places[None, :], (SUB, count)),
        jnp.broadcast_to(jnp.where(at_disc, owner, -1)[:, None], (count, LANE)),
    )

    step = (stations, height // STEPS, width)
    near_inflow = stay(inflow)
    upstream = along_march(velocity_guess[-1], 1)
    current = stay(velocity_guess)
    disc = velocity_guess[0].astype(BF16)
    rows = turns([disc] * cross_size)
    source = by_rows(
        source_kernel,
        height,
        sources,
        place,
        (current, upstream, near_inflow),
        cost(1e6, 2 * MIB),
        whole=range(4),
        scratch=[pltpu.VMEM(step, F32)],
    )
    for sweep_index in range(SWEEPS):
        merged = sweep_index > 0
        final = sweep_index == SWEEPS - 1
        if merged:
            rows = turns([disc] * cross_size)
        guess, damp, *source = lax.optimization_barrier((current, damping, *source))
        arrived = turns(source)
        decay, scale, *kept = by_rows(
            decay_kernel,
            height,
            [far(slab), far(chunks)] + [far(slab)] * merged,
            place,
            (guess if merged else stay(guess), stay(damp)),
            cost(4e6, 3 * MIB),
        )
        solve_cost = cost(3 * 8 * width**3, 5 * MIB)
        if merged:
            scale, *arrived = lax.optimization_barrier((scale, *far_first(arrived)))
            arrived = far_first(arrived)
            made = disc_forces(rows, where, blades, tabled)
            forces, near_tables = made[:cross_size], made[cross_size:]
            solved = call(
                near_solve_kernel,
                [near((height + height * LANE // width, width))] * cross_size,
                (place, *far_first(arrived), *near_tables, *forces),
                solve_cost,
                scalars=1,
                limit=16,
                scratch=[pltpu.VMEM((width, width), F32)],
            )
            scales = across_march(scale)
            forces = []
        else:
            scales = across_march(scale)
            solved = pl.pallas_call(
                far_solve_kernel,
                out_shape=[near(plane)] * cross_size,
                in_specs=[SMEM] + [VMEM] * cross_size + [pl.BlockSpec(memory_space=pltpu.HBM)] * 3,
                out_specs=[VMEM] * cross_size,
                scratch_shapes=[pltpu.VMEM((width, width), F32)]
                + [pltpu.VMEM((width, width), BF16)] * 2
                + [pltpu.VMEM((width, width), F32), pltpu.SemaphoreType.DMA((3,))],
                compiler_params=pltpu.CompilerParams(vmem_limit_bytes=20 * MIB),
                cost_estimate=solve_cost,
            )(place, *far_first(arrived), *tabled)
            rows, scales, solved, where = lax.optimization_barrier((rows, scales, solved, where))
            forces = turns(disc_forces(rows, where, blades), -1)
        pieces = turns(solved)
        decay = stay(decay)
        if merged:
            current = stay(kept[0])
        term, weights, base, force_weight = call(
            weights_kernel,
            [far(slab), near(slab), near(plane), near(plane)],
            (place, current, arrived[1], arrived[-1], decay, near_inflow),
            cost(8e6, 4 * MIB),
            scalars=1,
            limit=12,
        )
        lead, force, offset = call(
            offset_kernel,
            [near(plane), far(plane), far(chunks)],
            (place, *far_first(pieces), *forces, weights, base, force_weight),
            cost(2e6, 3 * MIB),
            scalars=1,
            limit=12,
        )
        following = along_march(lead, -1)
        offset, force, *pieces = lax.optimization_barrier((offset, force, *pieces))
        change, decay, *pressure = call(
            change_kernel,
            [near((stations + (not final), *plane)), near(slab)] + [far(slab)] * final,
            (place, *pieces, stay(term), stay(force), decay, near_inflow),
            cost(4e6, 4 * MIB),
            scalars=1,
            limit=12,
            scratch=[] if final else [pltpu.VMEM(slab, F32)],
        )
        offset = across_march(offset)
        (entering,) = call(scan_kernel, [far(chunks)], (scales, offset), cost(1e5, MIB))
        entering = across_march(entering)
        common = (entering, change, following, decay)
        if final:
            (current,) = call(
                last_kernel, [far(slab)], common, cost(4e6, 5 * MIB), limit=12
            )
            return (current, pressure[0])
        current, disc, *source = call(
            middle_kernel,
            [near(slab), near(plane, BF16)] + sources,
            (place, *common),
            cost(6e6, 5 * MIB),
            scalars=1,
            limit=12,
            scratch=[pltpu.VMEM(slab, F32)],
        )


def solution(mesh):
    in_specs = (
        P("march", "cross", None),
        P("march", "cross", None),
        P("cross", None),
        P(),
        P(),
        P("march", None, "cross"),
    )
    out_specs = (P("march", "cross", None), P("march", "cross", None))
    return jax.shard_map(local, mesh=mesh, in_specs=in_specs, out_specs=out_specs, check_vma=False)
```

```python
import ml_dtypes
import numpy as np
import jax
import jax.numpy as jnp
from jax import lax
from jax.experimental import pallas as pl
from jax.experimental.pallas import tpu as pltpu
from jax.sharding import PartitionSpec as P

SWEEPS = 2
SOURCE_GAIN = 0.04
SCREENING = 0.001
VISCOSITY = 0.1
DRAG_RATE = 0.01

F32 = jnp.float32
BF16 = jnp.bfloat16
SUB = 8
LANE = 128
EDGE = 8
STEPS = 4
MIB = 1024 * 1024
VMEM = pl.BlockSpec(memory_space=pltpu.VMEM)
SMEM = pl.BlockSpec(memory_space=pltpu.SMEM)


def tables(length):
    ordinal = np.arange(1, length + 1)
    product = np.outer(ordinal, ordinal) % (2 * (length + 1))
    sine = np.sqrt(2.0 / (length + 1)) * np.sin(np.pi * product / (length + 1))
    high = sine.astype(np.float32).astype(ml_dtypes.bfloat16)
    low = (sine - high.astype(np.float64)).astype(np.float32).astype(ml_dtypes.bfloat16)
    values = 2.0 - 2.0 * np.cos(np.pi * ordinal / (length + 1))
    inverse = 1.0 / (SCREENING + values[:, None] + values[None, :])
    return high, low, inverse.astype(np.float32)


def split(value):
    high = value.astype(BF16)
    return high, (value - high.astype(F32)).astype(BF16)


def groups(rows):
    return [(g, slice(SUB * g, SUB * g + SUB)) for g in range(rows // SUB)]


def to_chunks(ref, g, value):
    for h in range(2):
        for q in range(2):
            at = (2 * h + q) * LANE
            ref[2 * g + h, SUB * q : SUB * q + SUB, :] = value[:, at : at + LANE]


def from_chunks(ref, g):
    parts = []
    for h in range(2):
        for q in range(2):
            parts.append(ref[2 * g + h, SUB * q : SUB * q + SUB, :])
    return jnp.concatenate(parts, axis=1)


def decay_of(value, damping):
    return 1.0 - (damping + DRAG_RATE * jnp.abs(value))


def send_order(place, source, outs, i=None):
    count, height, _ = source.shape
    rows = slice(0, height) if i is None else pl.ds(pl.multiple_of(i * height, height), height)
    for r, ref in enumerate(outs):
        ref[rows, :] = source[lax.rem(place[0] + r, count)]


def send_edges(current, outs, first=True, last=True):
    stations, height, width = current.shape
    total = outs[1].shape[0]
    empty = jnp.zeros((EDGE - stations, width), F32)

    @pl.when(last)
    def _():
        rows = [current[s, height - 1 : height] for s in range(stations)]
        outs[1][total - EDGE : total] = jnp.concatenate(rows + [empty], axis=0)

    @pl.when(first)
    def _():
        rows = [current[s, 0:1] for s in range(stations)]
        outs[-1][total - EDGE : total] = jnp.concatenate(rows + [empty], axis=0)


def source_kernel(place, current, upstream, inflow, x0, x1, x2, x3, source):
    stations, height, _ = current.shape
    for _, rows in groups(height):
        previous = jnp.where(place[1] == 1, inflow[rows], upstream[rows])
        for s in range(stations):
            here = current[s, rows]
            source[s, rows] = SOURCE_GAIN * (here - previous)
            previous = here
    outs = (x0, x1, x2, x3)
    i = pl.program_id(0)
    send_order(place, source, outs, i)
    send_edges(current, outs, i == 0, i == pl.num_programs(0) - 1)


def decay_kernel(place, current, damping, decay, scale, *copy):
    for g, rows in groups(current.shape[1]):
        product = None
        for s in range(current.shape[0]):
            here = current[s, rows]
            for ref in copy:
                ref[s, rows] = here
            d = decay_of(here, damping[s, rows])
            decay[s, rows] = d
            product = d if product is None else product * d
        to_chunks(scale, g, product)


def weights_kernel(
    place, current, before, after, decay, inflow, term, weights, base, force_weight
):
    stations, height, width = current.shape
    first = place[1] == 1
    above = jnp.where(place[2] == 1, 0.0, before[height : height + EDGE])
    below = jnp.where(place[3] == 1, 0.0, after[height : height + EDGE])
    lane = lax.broadcasted_iota(jnp.int32, (SUB, width), 1)
    for g, rows in groups(height):
        lo, hi = SUB * g, SUB * g + SUB
        total = jnp.zeros((SUB, width), F32)
        factor = None
        for s in reversed(range(stations)):
            here = current[s, rows]
            if g == 0:
                up = jnp.concatenate([above[s : s + 1], current[s, 0 : SUB - 1]], axis=0)
            else:
                up = current[s, lo - 1 : hi - 1]
            if hi == height:
                down = jnp.concatenate([current[s, lo + 1 : hi], below[s : s + 1]], axis=0)
            else:
                down = current[s, lo + 1 : hi + 1]
            left = jnp.where(lane == 0, 0.0, pltpu.roll(here, 1, 1))
            right = jnp.where(lane == width - 1, 0.0, pltpu.roll(here, width - 1, 1))
            t = VISCOSITY * (up + down + left + right - 4.0 * here)
            term[s, rows] = t
            d = decay[s, rows]
            if factor is None:
                total, weight, factor = t, 1.0 - d, d
            else:
                if s == 0:
                    force_weight[rows] = factor
                total, weight, factor = total + factor * t, factor * (1.0 - d), factor * d
            if s == 0:
                entry = jnp.where(first, factor, 0.0)
                weight = weight + entry
                total = total + entry * inflow[rows]
            weights[s, rows] = weight
        base[rows] = total


def far_solve_kernel(
    place, x0, x1, x2, x3, high_far, low_far, inverse_far, p0, p1, p2, p3,
    plane, high, low, inverse, arrivals,
):
    copies = [
        pltpu.make_async_copy(far_ref, ref, arrivals.at[i])
        for i, (far_ref, ref) in enumerate(
            ((high_far, high), (low_far, low), (inverse_far, inverse))
        )
    ]
    solve(place, (x0, x1, x2, x3), (high, low, inverse), (), (p0, p1, p2, p3), plane, copies)


def near_solve_kernel(
    place, x0, x1, x2, x3, high, low, inverse, p0, p1, p2, p3, plane
):
    solve(place, (x0, x1, x2, x3), (high, low, inverse), (), (p0, p1, p2, p3), plane)


def solve(place, inputs, tables_near, forces, outputs, plane, copies=()):
    c = place[0]
    high, low, inverse = tables_near
    for copy in copies:
        copy.start()
    count = len(inputs)
    height = inputs[0].shape[0]
    for r, ref in enumerate(inputs):
        b = lax.rem(c - r + count, count)
        plane[pl.ds(pl.multiple_of(b * height, height), height), :] = ref[0:height]
    for copy in copies[:2]:
        copy.wait()
    sh, sl = high[...], low[...]
    by_left = jnp.concatenate([sh, sh, sl], axis=1)
    by_right = jnp.concatenate([sh, sl, sh], axis=0)

    def right(value):
        vh, vl = split(value)
        return jnp.dot(
            jnp.concatenate([vh, vh, vl], axis=1), by_right, preferred_element_type=F32
        )

    def left(value):
        vh, vl = split(value)
        return jnp.dot(
            by_left, jnp.concatenate([vh, vl, vh], axis=0), preferred_element_type=F32
        )

    modes = left(right(plane[...]))
    for copy in copies[2:]:
        copy.wait()
    modes = modes * inverse[...]
    plane[...] = right(left(modes))
    for r, ref in enumerate(outputs):
        b = lax.rem(c + r, count)
        ref[0:height] = plane[pl.ds(pl.multiple_of(b * height, height), height), :]
    if forces:
        extra = outputs[0].shape[0] - height
        for r, ref in enumerate(outputs):
            for q in range(height // extra):
                ref[height : height + extra, LANE * q : LANE * (q + 1)] = forces[-r][
                    extra * q : extra * (q + 1)
                ]


def disc_kernel(d0, d1, d2, d3, places, place_row, owners, *rest):
    streams, tabled = 4, (len(rest) - 11) // 2
    blades, tables_far = rest[:streams], rest[streams : streams + tabled]
    f0, f1, f2, f3 = rest[streams + tabled : streams + tabled + 4]
    tables_near = rest[streams + tabled + 4 : streams + 2 * tabled + 4]
    picked, total = rest[streams + 2 * tabled + 4 : streams + 2 * tabled + 6]
    step = pl.program_id(0)
    last = pl.num_programs(0) - 1
    height, width = d0.shape
    number = picked.shape[0]
    copies = [
        pltpu.make_async_copy(source, target, rest[-1].at[i])
        for i, (source, target) in enumerate(zip(tables_far, tables_near))
    ]

    @pl.when(step == 0)
    def _():
        for copy in copies:
            copy.start()
        plane = jnp.concatenate([d[...] for d in (d0, d1, d2, d3)], axis=0)
        lane = lax.broadcasted_iota(jnp.int32, (number, LANE), 1)
        chosen = [
            jnp.where(places[...] == lane + LANE * q, 1.0, 0.0).astype(BF16)
            for q in range(width // LANE)
        ]
        rows = jnp.dot(
            jnp.concatenate(chosen, axis=1), plane, preferred_element_type=F32
        )
        picked[...] = rows.astype(BF16)
        total[...] = jnp.zeros_like(total)

    per_step = blades[0].shape[0]
    for i in range(0, per_step, 2):
        pair = jnp.concatenate(
            [
                jnp.concatenate([blade[j] for blade in blades], axis=0)
                for j in (i, i + 1)
            ],
            axis=1,
        )
        response = jnp.dot(picked[...], pair, preferred_element_type=F32)
        first = step * per_step + i
        kept = jnp.where(owners[...] == first, response[:, :LANE], total[...])
        total[...] = jnp.where(owners[...] == first + 1, response[:, LANE:], kept)

    @pl.when(step == last)
    def _():
        rest_of, parts = jnp.tanh(total[...]), []
        for _ in range(3):
            parts.append(rest_of.astype(BF16))
            rest_of = rest_of - parts[-1].astype(F32)
        forces = jnp.concatenate(parts, axis=0)
        at = place_row[0:1]
        for r, ref in enumerate((f0, f1, f2, f3)):
            row = lax.broadcasted_iota(jnp.int32, (height, number), 0) + height * r
            back = jnp.where(row == at, 1.0, 0.0).astype(BF16)
            ref[...] = jnp.dot(
                jnp.concatenate([back] * 3, axis=1), forces, preferred_element_type=F32
            )
        for copy in copies:
            copy.wait()


def offset_kernel(place, *rest):
    c = place[0]
    pieces = rest[:4]
    *forces, weights, base, force_weight, lead, force, offset = rest[4:]
    count, height, full = weights.shape
    width = full // count
    for r in range(count):
        b = lax.rem(c + r if forces else c - r + count, count)
        lanes = pl.ds(pl.multiple_of(b * width, width), width)
        if forces:
            force[:, lanes] = forces[r][...]
        else:
            extra = pieces[r].shape[0] - height
            for q in range(height // extra):
                force[extra * q : extra * (q + 1), lanes] = pieces[r][
                    height : height + extra, width * q : width * (q + 1)
                ]

    for r in range(count):
        @pl.when(c == r)
        def _():
            lead[...] = pieces[r][0:height]

    for g, rows in groups(height):
        state = base[rows] + force_weight[rows] * force[rows]
        for r in range(count):
            s = lax.rem(c - r + count, count)
            state = state + weights[s, rows] * pieces[r][rows]
        to_chunks(offset, g, state)


def change_kernel(
    place, p0, p1, p2, p3, term, force, decay, inflow,
    change, decay_near, pressure,
):
    c = place[0]
    pieces = (p0, p1, p2, p3)
    count, height, _ = term.shape
    for r in range(count):
        pressure[lax.rem(c - r + count, count)] = pieces[r][0:height]
    for _, rows in groups(height):
        here = pressure[0, rows]
        entry = jnp.where(place[1] == 1, inflow[rows], -here)
        if change.shape[0] > count:
            change[count, rows] = entry
        for s in range(count):
            value = term[s, rows] + here
            if s == 0:
                value = value + force[rows]
            if s < count - 1:
                here = pressure[s + 1, rows]
                value = value - here
            d = decay[s, rows]
            decay_near[s, rows] = d
            if s == 0 and change.shape[0] == count:
                value = value + d * entry
            change[s, rows] = value


def scan_kernel(scale, offset, entering):
    entering[0] = jnp.zeros_like(entering[0])
    state = offset[0]
    for m in range(1, scale.shape[0]):
        entering[m] = state
        state = scale[m] * state + offset[m]


def march_rows(g, rows, entering, change, following, decay):
    stations = decay.shape[0]
    state = from_chunks(entering, g)
    if change.shape[0] > stations:
        state = state + change[stations, rows]
    states = [state]
    for s in range(stations):
        step = change[s, rows]
        if s == stations - 1:
            step = step - following[rows]
        state = decay[s, rows] * state + step
        states.append(state)
    return states


def middle_kernel(
    place, entering, change, following, decay, current, disc, x0, x1, x2, x3, source
):
    stations, height, _ = current.shape
    for g, rows in groups(height):
        states = march_rows(g, rows, entering, change, following, decay)
        for s in range(stations):
            current[s, rows] = states[s + 1]
            source[s, rows] = SOURCE_GAIN * (states[s + 1] - states[s])
    outs = (x0, x1, x2, x3)
    send_order(place, source, outs)
    send_edges(current, outs)
    disc[...] = current[0].astype(BF16)


def last_kernel(entering, change, following, decay, current):
    for g, rows in groups(current.shape[1]):
        states = march_rows(g, rows, entering, change, following, decay)
        for s in range(current.shape[0]):
            current[s, rows] = states[s + 1]


def cost(flops, size):
    return pl.CostEstimate(flops=int(flops), bytes_accessed=int(size), transcendentals=0)


def near(shape, dtype=F32):
    return pltpu.VMEM(shape, dtype)


def far(shape, dtype=F32):
    return pltpu.HBM(shape, dtype)


def stay(value):
    return pltpu.with_memory_space_constraint(value, pltpu.HBM)


def call(kernel, outs, args, work, scalars=0, limit=8, scratch=()):
    return pl.pallas_call(
        kernel,
        out_shape=outs,
        in_specs=[SMEM] * scalars + [VMEM] * (len(args) - scalars),
        out_specs=[VMEM] * len(outs),
        scratch_shapes=list(scratch),
        compiler_params=pltpu.CompilerParams(vmem_limit_bytes=limit * MIB),
        cost_estimate=work,
    )(*args)


def by_rows(kernel, height, outs, place, args, work, whole=(), scratch=()):
    part = height // STEPS

    def spec(shape, index):
        if index in whole:
            return pl.BlockSpec(shape, lambda i, p: (0,) * len(shape))
        if shape[-1] == LANE and len(shape) == 3:
            return pl.BlockSpec((shape[0] // STEPS,) + shape[1:], lambda i, p: (i, 0, 0))
        if len(shape) == 3:
            return pl.BlockSpec((shape[0], part, shape[2]), lambda i, p: (0, i, 0))
        return pl.BlockSpec((part, shape[1]), lambda i, p: (i, 0))

    count = len(args)
    return pl.pallas_call(
        kernel,
        grid_spec=pltpu.PrefetchScalarGridSpec(
            num_scalar_prefetch=1,
            grid=(STEPS,),
            in_specs=[spec(a.shape, None) for a in args],
            out_specs=[spec(a.inner_aval.shape, i) for i, a in enumerate(outs)],
            scratch_shapes=list(scratch),
        ),
        out_shape=outs,
        compiler_params=pltpu.CompilerParams(vmem_limit_bytes=12 * MIB),
        cost_estimate=work,
    )(place, *args)


def disc_forces(rows, where, blades, tabled=()):
    height, width = rows[0].shape
    count = len(rows)
    number = blades.shape[0]
    per_step, streams = 8, 4
    fixed = lambda shape: pl.BlockSpec(shape, lambda i: (0,) * len(shape))
    table = lambda k: pl.BlockSpec((per_step, width // streams, LANE), lambda i: (i, k, 0))
    discs = where[0].shape[0]
    return pl.pallas_call(
        disc_kernel,
        grid=(number // per_step,),
        out_shape=[near((height, LANE))] * count + [near(t.shape, t.dtype) for t in tabled],
        in_specs=[fixed((height, width))] * count
        + [fixed(w.shape) for w in where]
        + [table(k) for k in range(streams)]
        + [pl.BlockSpec(memory_space=pltpu.HBM)] * len(tabled),
        out_specs=[fixed((height, LANE))] * count
        + [pl.BlockSpec(memory_space=pltpu.VMEM)] * len(tabled),
        scratch_shapes=[
            pltpu.VMEM((discs, width), BF16),
            pltpu.VMEM((discs, LANE), F32),
            pltpu.SemaphoreType.DMA((3,)),
        ],
        compiler_params=pltpu.CompilerParams(vmem_limit_bytes=16 * MIB),
        cost_estimate=cost(2 * number * width * width * LANE, 5 * MIB),
    )(*rows, *map(stay, where), *[stay(blades)] * streams, *tabled)


def local(velocity_guess, damping, inflow, disc_rows, owner, blade):
    stations, height, width = velocity_guess.shape
    march_size = lax.axis_size("march")
    cross_size = lax.axis_size("cross")
    march_index = lax.axis_index("march")
    cross_index = lax.axis_index("cross")
    disc_slab = stations * march_size // 2 // stations
    at_disc = march_index == disc_slab
    first = march_index == 0
    place = jnp.stack(
        [
            cross_index.astype(jnp.int32),
            first.astype(jnp.int32),
            (cross_index == 0).astype(jnp.int32),
            (cross_index == cross_size - 1).astype(jnp.int32),
        ]
    )
    tabled = [stay(jnp.asarray(t)) for t in tables(width)]

    slab = (stations, height, width)
    plane = (height, width)
    edged = (height + EDGE, width)
    chunks = (march_size, height * width // march_size // LANE, LANE)
    sources = [near(plane), near(edged), near(plane), near(edged)]

    def turn(value, steps):
        return lax.ppermute(
            value, "cross", [(i, (i + steps) % cross_size) for i in range(cross_size)]
        )

    def turns(blocks, sign=1):
        return [blocks[0]] + [turn(blocks[r], sign * r) for r in range(1, cross_size)]

    def along_march(value, steps):
        count = march_size
        return lax.ppermute(
            value, "march", [(i, i + steps) for i in range(count) if 0 <= i + steps < count]
        )

    def across_march(value):
        return lax.all_to_all(value, "march", split_axis=0, concat_axis=0, tiled=True)

    blades = lax.all_gather(blade, "march", axis=0, tiled=True)
    turn_of = (cross_index - disc_rows // height + cross_size) % cross_size
    places = turn_of * height + disc_rows % height
    count = disc_rows.shape[0]
    where = (
        jnp.broadcast_to(places[:, None], (count, LANE)),
        jnp.broadcast_to(places[None, :], (SUB, count)),
        jnp.broadcast_to(jnp.where(at_disc, owner, -1)[:, None], (count, LANE)),
    )

    step = (stations, height // STEPS, width)
    near_inflow = stay(inflow)
    upstream = along_march(velocity_guess[-1], 1)
    current = stay(velocity_guess)
    disc = velocity_guess[0].astype(BF16)
    rows = turns([disc] * cross_size)
    source = by_rows(
        source_kernel,
        height,
        sources,
        place,
        (current, upstream, near_inflow),
        cost(1e6, 2 * MIB),
        whole=range(4),
        scratch=[pltpu.VMEM(step, F32)],
    )
    for sweep_index in range(SWEEPS):
        merged = sweep_index > 0
        final = sweep_index == SWEEPS - 1
        if merged:
            rows = turns([disc] * cross_size)
        guess, damp, *source = lax.optimization_barrier((current, damping, *source))
        arrived = turns(source)
        decay, scale, *kept = by_rows(
            decay_kernel,
            height,
            [far(slab), far(chunks)] + [far(slab)] * merged,
            place,
            (guess if merged else stay(guess), stay(damp)),
            cost(4e6, 3 * MIB),
        )
        solve_cost = cost(3 * 8 * width**3, 5 * MIB)
        if merged:
            scale, *arrived = lax.optimization_barrier((scale, *arrived))
            made = disc_forces(rows, where, blades, tabled)
            forces, near_tables = made[:cross_size], made[cross_size:]
            solved = call(
                near_solve_kernel,
                [near(plane)] * cross_size,
                (place, *arrived, *near_tables),
                solve_cost,
                scalars=1,
                limit=16,
                scratch=[pltpu.VMEM((width, width), F32)],
            )
            scales = across_march(scale)
            forces, solved = lax.optimization_barrier((turns(forces, -1), solved))
        else:
            scales = across_march(scale)
            solved = pl.pallas_call(
                far_solve_kernel,
                out_shape=[near(plane)] * cross_size,
                in_specs=[SMEM] + [VMEM] * cross_size + [pl.BlockSpec(memory_space=pltpu.HBM)] * 3,
                out_specs=[VMEM] * cross_size,
                scratch_shapes=[pltpu.VMEM((width, width), F32)]
                + [pltpu.VMEM((width, width), BF16)] * 2
                + [pltpu.VMEM((width, width), F32), pltpu.SemaphoreType.DMA((3,))],
                compiler_params=pltpu.CompilerParams(vmem_limit_bytes=20 * MIB),
                cost_estimate=solve_cost,
            )(place, *arrived, *tabled)
            rows, scales, solved, where = lax.optimization_barrier((rows, scales, solved, where))
            forces = turns(disc_forces(rows, where, blades), -1)
        pieces = turns(solved)
        decay = stay(decay)
        if merged:
            current = stay(kept[0])
        term, weights, base, force_weight = call(
            weights_kernel,
            [far(slab), near(slab), near(plane), near(plane)],
            (place, current, arrived[1], arrived[-1], decay, near_inflow),
            cost(8e6, 4 * MIB),
            scalars=1,
            limit=12,
        )
        lead, force, offset = call(
            offset_kernel,
            [near(plane), far(plane), far(chunks)],
            (place, *pieces, *forces, weights, base, force_weight),
            cost(2e6, 3 * MIB),
            scalars=1,
            limit=12,
        )
        following = along_march(lead, -1)
        offset, force, *pieces = lax.optimization_barrier((offset, force, *pieces))
        change, decay, *pressure = call(
            change_kernel,
            [near((stations + (not final), *plane)), near(slab)] + [far(slab)] * final,
            (place, *pieces, stay(term), stay(force), decay, near_inflow),
            cost(4e6, 4 * MIB),
            scalars=1,
            limit=12,
            scratch=[] if final else [pltpu.VMEM(slab, F32)],
        )
        offset = across_march(offset)
        (entering,) = call(scan_kernel, [far(chunks)], (scales, offset), cost(1e5, MIB))
        entering = across_march(entering)
        common = (entering, change, following, decay)
        if final:
            (current,) = call(
                last_kernel, [far(slab)], common, cost(4e6, 5 * MIB), limit=12
            )
            return (current, pressure[0])
        current, disc, *source = call(
            middle_kernel,
            [near(slab), near(plane, BF16)] + sources,
            (place, *common),
            cost(6e6, 5 * MIB),
            scalars=1,
            limit=12,
            scratch=[pltpu.VMEM(slab, F32)],
        )


def solution(mesh):
    in_specs = (
        P("march", "cross", None),
        P("march", "cross", None),
        P("cross", None),
        P(),
        P(),
        P("march", None, "cross"),
    )
    out_specs = (P("march", "cross", None), P("march", "cross", None))
    return jax.shard_map(local, mesh=mesh, in_specs=in_specs, out_specs=out_specs, check_vma=False)
```

```python
import ml_dtypes
import numpy as np
import jax
import jax.numpy as jnp
from jax import lax
from jax.experimental import pallas as pl
from jax.experimental.pallas import tpu as pltpu
from jax.sharding import PartitionSpec as P

SWEEPS = 2
SOURCE_GAIN = 0.04
SCREENING = 0.001
VISCOSITY = 0.1
DRAG_RATE = 0.01

F32 = jnp.float32
BF16 = jnp.bfloat16
SUB = 8
LANE = 128
EDGE = 8
STEPS = 4
MIB = 1024 * 1024
VMEM = pl.BlockSpec(memory_space=pltpu.VMEM)
SMEM = pl.BlockSpec(memory_space=pltpu.SMEM)


def tables(length):
    ordinal = np.arange(1, length + 1)
    product = np.outer(ordinal, ordinal) % (2 * (length + 1))
    sine = np.sqrt(2.0 / (length + 1)) * np.sin(np.pi * product / (length + 1))
    high = sine.astype(np.float32).astype(ml_dtypes.bfloat16)
    low = (sine - high.astype(np.float64)).astype(np.float32).astype(ml_dtypes.bfloat16)
    values = 2.0 - 2.0 * np.cos(np.pi * ordinal / (length + 1))
    inverse = 1.0 / (SCREENING + values[:, None] + values[None, :])
    return high, low, inverse.astype(np.float32)


def split(value):
    high = value.astype(BF16)
    return high, (value - high.astype(F32)).astype(BF16)


def groups(rows):
    return [(g, slice(SUB * g, SUB * g + SUB)) for g in range(rows // SUB)]


def to_chunks(ref, g, value):
    for h in range(2):
        for q in range(2):
            at = (2 * h + q) * LANE
            ref[2 * g + h, SUB * q : SUB * q + SUB, :] = value[:, at : at + LANE]


def from_chunks(ref, g):
    parts = []
    for h in range(2):
        for q in range(2):
            parts.append(ref[2 * g + h, SUB * q : SUB * q + SUB, :])
    return jnp.concatenate(parts, axis=1)


def decay_of(value, damping):
    return 1.0 - (damping + DRAG_RATE * jnp.abs(value))


def send_order(place, source, outs, i=None):
    count, height, _ = source.shape
    rows = slice(0, height) if i is None else pl.ds(pl.multiple_of(i * height, height), height)
    for r, ref in enumerate(outs):
        ref[rows, :] = source[lax.rem(place[0] + r, count)]


def send_edges(current, outs, first=True, last=True):
    stations, height, width = current.shape
    total = outs[1].shape[0]
    empty = jnp.zeros((EDGE - stations, width), F32)

    @pl.when(last)
    def _():
        rows = [current[s, height - 1 : height] for s in range(stations)]
        outs[1][total - EDGE : total] = jnp.concatenate(rows + [empty], axis=0)

    @pl.when(first)
    def _():
        rows = [current[s, 0:1] for s in range(stations)]
        outs[-1][total - EDGE : total] = jnp.concatenate(rows + [empty], axis=0)


def source_kernel(place, current, upstream, inflow, x0, x1, x2, x3, source):
    stations, height, _ = current.shape
    for _, rows in groups(height):
        previous = jnp.where(place[1] == 1, inflow[rows], upstream[rows])
        for s in range(stations):
            here = current[s, rows]
            source[s, rows] = SOURCE_GAIN * (here - previous)
            previous = here
    outs = (x0, x1, x2, x3)
    i = pl.program_id(0)
    send_order(place, source, outs, i)
    send_edges(current, outs, i == 0, i == pl.num_programs(0) - 1)


def decay_kernel(place, current, damping, decay, scale, *copy):
    for g, rows in groups(current.shape[1]):
        product = None
        for s in range(current.shape[0]):
            here = current[s, rows]
            for ref in copy:
                ref[s, rows] = here
            d = decay_of(here, damping[s, rows])
            decay[s, rows] = d
            product = d if product is None else product * d
        to_chunks(scale, g, product)


def weights_kernel(
    place, current, before, after, decay, inflow, term, weights, base, force_weight
):
    stations, height, width = current.shape
    first = place[1] == 1
    above = jnp.where(place[2] == 1, 0.0, before[height : height + EDGE])
    below = jnp.where(place[3] == 1, 0.0, after[height : height + EDGE])
    lane = lax.broadcasted_iota(jnp.int32, (SUB, width), 1)
    for g, rows in groups(height):
        lo, hi = SUB * g, SUB * g + SUB
        total = jnp.zeros((SUB, width), F32)
        factor = None
        for s in reversed(range(stations)):
            here = current[s, rows]
            if g == 0:
                up = jnp.concatenate([above[s : s + 1], current[s, 0 : SUB - 1]], axis=0)
            else:
                up = current[s, lo - 1 : hi - 1]
            if hi == height:
                down = jnp.concatenate([current[s, lo + 1 : hi], below[s : s + 1]], axis=0)
            else:
                down = current[s, lo + 1 : hi + 1]
            left = jnp.where(lane == 0, 0.0, pltpu.roll(here, 1, 1))
            right = jnp.where(lane == width - 1, 0.0, pltpu.roll(here, width - 1, 1))
            t = VISCOSITY * (up + down + left + right - 4.0 * here)
            term[s, rows] = t
            d = decay[s, rows]
            if factor is None:
                total, weight, factor = t, 1.0 - d, d
            else:
                if s == 0:
                    force_weight[rows] = factor
                total, weight, factor = total + factor * t, factor * (1.0 - d), factor * d
            if s == 0:
                entry = jnp.where(first, factor, 0.0)
                weight = weight + entry
                total = total + entry * inflow[rows]
            weights[s, rows] = weight
        base[rows] = total


def far_solve_kernel(
    place, x0, x1, x2, x3, high_far, low_far, inverse_far, p0, p1, p2, p3,
    plane, high, low, inverse, arrivals,
):
    copies = [
        pltpu.make_async_copy(far_ref, ref, arrivals.at[i])
        for i, (far_ref, ref) in enumerate(
            ((high_far, high), (low_far, low), (inverse_far, inverse))
        )
    ]
    solve(place, (x0, x1, x2, x3), (high, low, inverse), (), (p0, p1, p2, p3), plane, copies)


def near_solve_kernel(
    place, x0, x1, x2, x3, high, low, inverse, p0, p1, p2, p3, plane
):
    solve(place, (x0, x1, x2, x3), (high, low, inverse), (), (p0, p1, p2, p3), plane)


def solve(place, inputs, tables_near, forces, outputs, plane, copies=()):
    c = place[0]
    high, low, inverse = tables_near
    for copy in copies:
        copy.start()
    count = len(inputs)
    height = inputs[0].shape[0]
    for r, ref in enumerate(inputs):
        b = lax.rem(c - r + count, count)
        plane[pl.ds(pl.multiple_of(b * height, height), height), :] = ref[0:height]
    for copy in copies[:2]:
        copy.wait()
    sh, sl = high[...], low[...]
    by_left = jnp.concatenate([sh, sh, sl], axis=1)
    by_right = jnp.concatenate([sh, sl, sh], axis=0)

    def right(value):
        vh, vl = split(value)
        return jnp.dot(
            jnp.concatenate([vh, vh, vl], axis=1), by_right, preferred_element_type=F32
        )

    def left(value):
        vh, vl = split(value)
        return jnp.dot(
            by_left, jnp.concatenate([vh, vl, vh], axis=0), preferred_element_type=F32
        )

    modes = left(right(plane[...]))
    for copy in copies[2:]:
        copy.wait()
    modes = modes * inverse[...]
    plane[...] = right(left(modes))
    for r, ref in enumerate(outputs):
        b = lax.rem(c + r, count)
        ref[0:height] = plane[pl.ds(pl.multiple_of(b * height, height), height), :]
    if forces:
        extra = outputs[0].shape[0] - height
        for r, ref in enumerate(outputs):
            for q in range(height // extra):
                ref[height : height + extra, LANE * q : LANE * (q + 1)] = forces[-r][
                    extra * q : extra * (q + 1)
                ]


def disc_kernel(d0, d1, d2, d3, places, place_row, owners, *rest):
    streams, tabled = 4, (len(rest) - 11) // 2
    blades, tables_far = rest[:streams], rest[streams : streams + tabled]
    f0, f1, f2, f3 = rest[streams + tabled : streams + tabled + 4]
    tables_near = rest[streams + tabled + 4 : streams + 2 * tabled + 4]
    picked, total = rest[streams + 2 * tabled + 4 : streams + 2 * tabled + 6]
    step = pl.program_id(0)
    last = pl.num_programs(0) - 1
    height, width = d0.shape
    number = picked.shape[0]
    copies = [
        pltpu.make_async_copy(source, target, rest[-1].at[i])
        for i, (source, target) in enumerate(zip(tables_far, tables_near))
    ]

    @pl.when(step == 0)
    def _():
        for copy in copies:
            copy.start()
        plane = jnp.concatenate([d[...] for d in (d0, d1, d2, d3)], axis=0)
        lane = lax.broadcasted_iota(jnp.int32, (number, LANE), 1)
        chosen = [
            jnp.where(places[...] == lane + LANE * q, 1.0, 0.0).astype(BF16)
            for q in range(width // LANE)
        ]
        rows = jnp.dot(
            jnp.concatenate(chosen, axis=1), plane, preferred_element_type=F32
        )
        picked[...] = rows.astype(BF16)
        total[...] = jnp.zeros_like(total)

    per_step = blades[0].shape[0]
    for i in range(0, per_step, 2):
        pair = jnp.concatenate(
            [
                jnp.concatenate([blade[j] for blade in blades], axis=0)
                for j in (i, i + 1)
            ],
            axis=1,
        )
        response = jnp.dot(picked[...], pair, preferred_element_type=F32)
        first = step * per_step + i
        kept = jnp.where(owners[...] == first, response[:, :LANE], total[...])
        total[...] = jnp.where(owners[...] == first + 1, response[:, LANE:], kept)

    @pl.when(step == last)
    def _():
        rest_of, parts = jnp.tanh(total[...]), []
        for _ in range(3):
            parts.append(rest_of.astype(BF16))
            rest_of = rest_of - parts[-1].astype(F32)
        forces = jnp.concatenate(parts, axis=0)
        at = place_row[0:1]
        for r, ref in enumerate((f0, f1, f2, f3)):
            row = lax.broadcasted_iota(jnp.int32, (height, number), 0) + height * r
            back = jnp.where(row == at, 1.0, 0.0).astype(BF16)
            ref[...] = jnp.dot(
                jnp.concatenate([back] * 3, axis=1), forces, preferred_element_type=F32
            )
        for copy in copies:
            copy.wait()


def offset_kernel(place, *rest):
    c = place[0]
    pieces = rest[:4]
    *forces, weights, base, force_weight, lead, force, offset = rest[4:]
    count, height, full = weights.shape
    width = full // count
    for r in range(count):
        b = lax.rem(c + r if forces else c - r + count, count)
        lanes = pl.ds(pl.multiple_of(b * width, width), width)
        if forces:
            force[:, lanes] = forces[r][...]
        else:
            extra = pieces[r].shape[0] - height
            for q in range(height // extra):
                force[extra * q : extra * (q + 1), lanes] = pieces[r][
                    height : height + extra, width * q : width * (q + 1)
                ]

    for r in range(count):
        @pl.when(c == r)
        def _():
            lead[...] = pieces[r][0:height]

    for g, rows in groups(height):
        state = base[rows] + force_weight[rows] * force[rows]
        for r in range(count):
            s = lax.rem(c - r + count, count)
            state = state + weights[s, rows] * pieces[r][rows]
        to_chunks(offset, g, state)


def change_kernel(
    place, p0, p1, p2, p3, term, force, decay, inflow,
    change, decay_near, pressure,
):
    c = place[0]
    pieces = (p0, p1, p2, p3)
    count, height, _ = term.shape
    for r in range(count):
        pressure[lax.rem(c - r + count, count)] = pieces[r][0:height]
    for _, rows in groups(height):
        here = pressure[0, rows]
        entry = jnp.where(place[1] == 1, inflow[rows], -here)
        if change.shape[0] > count:
            change[count, rows] = entry
        for s in range(count):
            value = term[s, rows] + here
            if s == 0:
                value = value + force[rows]
            if s < count - 1:
                here = pressure[s + 1, rows]
                value = value - here
            d = decay[s, rows]
            decay_near[s, rows] = d
            if s == 0 and change.shape[0] == count:
                value = value + d * entry
            change[s, rows] = value


def scan_kernel(scale, offset, entering):
    entering[0] = jnp.zeros_like(entering[0])
    state = offset[0]
    for m in range(1, scale.shape[0]):
        entering[m] = state
        state = scale[m] * state + offset[m]


def march_rows(g, rows, entering, change, following, decay):
    stations = decay.shape[0]
    state = from_chunks(entering, g)
    if change.shape[0] > stations:
        state = state + change[stations, rows]
    states = [state]
    for s in range(stations):
        step = change[s, rows]
        if s == stations - 1:
            step = step - following[rows]
        state = decay[s, rows] * state + step
        states.append(state)
    return states


def middle_kernel(
    place, entering, change, following, decay, current, disc, x0, x1, x2, x3, source
):
    stations, height, _ = current.shape
    for g, rows in groups(height):
        states = march_rows(g, rows, entering, change, following, decay)
        for s in range(stations):
            current[s, rows] = states[s + 1]
            source[s, rows] = SOURCE_GAIN * (states[s + 1] - states[s])
    outs = (x0, x1, x2, x3)
    send_order(place, source, outs)
    send_edges(current, outs)
    disc[...] = current[0].astype(BF16)


def last_kernel(entering, change, following, decay, current):
    for g, rows in groups(current.shape[1]):
        states = march_rows(g, rows, entering, change, following, decay)
        for s in range(current.shape[0]):
            current[s, rows] = states[s + 1]


def cost(flops, size):
    return pl.CostEstimate(flops=int(flops), bytes_accessed=int(size), transcendentals=0)


def near(shape, dtype=F32):
    return pltpu.VMEM(shape, dtype)


def far(shape, dtype=F32):
    return pltpu.HBM(shape, dtype)


def stay(value):
    return pltpu.with_memory_space_constraint(value, pltpu.HBM)


def call(kernel, outs, args, work, scalars=0, limit=8, scratch=()):
    return pl.pallas_call(
        kernel,
        out_shape=outs,
        in_specs=[SMEM] * scalars + [VMEM] * (len(args) - scalars),
        out_specs=[VMEM] * len(outs),
        scratch_shapes=list(scratch),
        compiler_params=pltpu.CompilerParams(vmem_limit_bytes=limit * MIB),
        cost_estimate=work,
    )(*args)


def by_rows(kernel, height, outs, place, args, work, whole=(), scratch=()):
    part = height // STEPS

    def spec(shape, index):
        if index in whole:
            return pl.BlockSpec(shape, lambda i, p: (0,) * len(shape))
        if shape[-1] == LANE and len(shape) == 3:
            return pl.BlockSpec((shape[0] // STEPS,) + shape[1:], lambda i, p: (i, 0, 0))
        if len(shape) == 3:
            return pl.BlockSpec((shape[0], part, shape[2]), lambda i, p: (0, i, 0))
        return pl.BlockSpec((part, shape[1]), lambda i, p: (i, 0))

    count = len(args)
    return pl.pallas_call(
        kernel,
        grid_spec=pltpu.PrefetchScalarGridSpec(
            num_scalar_prefetch=1,
            grid=(STEPS,),
            in_specs=[spec(a.shape, None) for a in args],
            out_specs=[spec(a.inner_aval.shape, i) for i, a in enumerate(outs)],
            scratch_shapes=list(scratch),
        ),
        out_shape=outs,
        compiler_params=pltpu.CompilerParams(vmem_limit_bytes=12 * MIB),
        cost_estimate=work,
    )(place, *args)


def disc_forces(rows, where, blades, tabled=()):
    height, width = rows[0].shape
    count = len(rows)
    number = blades.shape[0]
    per_step, streams = 16, 4
    fixed = lambda shape: pl.BlockSpec(shape, lambda i: (0,) * len(shape))
    table = lambda k: pl.BlockSpec((per_step, width // streams, LANE), lambda i: (i, k, 0))
    discs = where[0].shape[0]
    return pl.pallas_call(
        disc_kernel,
        grid=(number // per_step,),
        out_shape=[near((height, LANE))] * count + [near(t.shape, t.dtype) for t in tabled],
        in_specs=[fixed((height, width))] * count
        + [fixed(w.shape) for w in where]
        + [table(k) for k in range(streams)]
        + [pl.BlockSpec(memory_space=pltpu.HBM)] * len(tabled),
        out_specs=[fixed((height, LANE))] * count
        + [pl.BlockSpec(memory_space=pltpu.VMEM)] * len(tabled),
        scratch_shapes=[
            pltpu.VMEM((discs, width), BF16),
            pltpu.VMEM((discs, LANE), F32),
            pltpu.SemaphoreType.DMA((3,)),
        ],
        compiler_params=pltpu.CompilerParams(vmem_limit_bytes=16 * MIB),
        cost_estimate=cost(2 * number * width * width * LANE, 5 * MIB),
    )(*rows, *map(stay, where), *[stay(blades)] * streams, *tabled)


def local(velocity_guess, damping, inflow, disc_rows, owner, blade):
    stations, height, width = velocity_guess.shape
    march_size = lax.axis_size("march")
    cross_size = lax.axis_size("cross")
    march_index = lax.axis_index("march")
    cross_index = lax.axis_index("cross")
    disc_slab = stations * march_size // 2 // stations
    at_disc = march_index == disc_slab
    first = march_index == 0
    place = jnp.stack(
        [
            cross_index.astype(jnp.int32),
            first.astype(jnp.int32),
            (cross_index == 0).astype(jnp.int32),
            (cross_index == cross_size - 1).astype(jnp.int32),
        ]
    )
    tabled = [stay(jnp.asarray(t)) for t in tables(width)]

    slab = (stations, height, width)
    plane = (height, width)
    edged = (height + EDGE, width)
    chunks = (march_size, height * width // march_size // LANE, LANE)
    sources = [near(plane), near(edged), near(plane), near(edged)]

    def turn(value, steps):
        return lax.ppermute(
            value, "cross", [(i, (i + steps) % cross_size) for i in range(cross_size)]
        )

    def turns(blocks, sign=1):
        return [blocks[0]] + [turn(blocks[r], sign * r) for r in range(1, cross_size)]

    def along_march(value, steps):
        count = march_size
        return lax.ppermute(
            value, "march", [(i, i + steps) for i in range(count) if 0 <= i + steps < count]
        )

    def across_march(value):
        return lax.all_to_all(value, "march", split_axis=0, concat_axis=0, tiled=True)

    blades = lax.all_gather(blade, "march", axis=0, tiled=True)
    turn_of = (cross_index - disc_rows // height + cross_size) % cross_size
    places = turn_of * height + disc_rows % height
    count = disc_rows.shape[0]
    where = (
        jnp.broadcast_to(places[:, None], (count, LANE)),
        jnp.broadcast_to(places[None, :], (SUB, count)),
        jnp.broadcast_to(jnp.where(at_disc, owner, -1)[:, None], (count, LANE)),
    )

    step = (stations, height // STEPS, width)
    near_inflow = stay(inflow)
    upstream = along_march(velocity_guess[-1], 1)
    current = stay(velocity_guess)
    disc = velocity_guess[0].astype(BF16)
    rows = turns([disc] * cross_size)
    source = by_rows(
        source_kernel,
        height,
        sources,
        place,
        (current, upstream, near_inflow),
        cost(1e6, 2 * MIB),
        whole=range(4),
        scratch=[pltpu.VMEM(step, F32)],
    )
    for sweep_index in range(SWEEPS):
        merged = sweep_index > 0
        final = sweep_index == SWEEPS - 1
        if merged:
            rows = turns([disc] * cross_size)
        guess, damp, *source = lax.optimization_barrier((current, damping, *source))
        arrived = turns(source)
        decay, scale, *kept = by_rows(
            decay_kernel,
            height,
            [far(slab), far(chunks)] + [far(slab)] * merged,
            place,
            (guess if merged else stay(guess), stay(damp)),
            cost(4e6, 3 * MIB),
        )
        solve_cost = cost(3 * 8 * width**3, 5 * MIB)
        if merged:
            scale, *arrived = lax.optimization_barrier((scale, *arrived))
            made = disc_forces(rows, where, blades, tabled)
            forces, near_tables = made[:cross_size], made[cross_size:]
            solved = call(
                near_solve_kernel,
                [near(plane)] * cross_size,
                (place, *arrived, *near_tables),
                solve_cost,
                scalars=1,
                limit=16,
                scratch=[pltpu.VMEM((width, width), F32)],
            )
            scales = across_march(scale)
            forces, solved = lax.optimization_barrier((turns(forces, -1), solved))
        else:
            scales = across_march(scale)
            solved = pl.pallas_call(
                far_solve_kernel,
                out_shape=[near(plane)] * cross_size,
                in_specs=[SMEM] + [VMEM] * cross_size + [pl.BlockSpec(memory_space=pltpu.HBM)] * 3,
                out_specs=[VMEM] * cross_size,
                scratch_shapes=[pltpu.VMEM((width, width), F32)]
                + [pltpu.VMEM((width, width), BF16)] * 2
                + [pltpu.VMEM((width, width), F32), pltpu.SemaphoreType.DMA((3,))],
                compiler_params=pltpu.CompilerParams(vmem_limit_bytes=20 * MIB),
                cost_estimate=solve_cost,
            )(place, *arrived, *tabled)
            rows, scales, solved, where = lax.optimization_barrier((rows, scales, solved, where))
            forces = turns(disc_forces(rows, where, blades), -1)
        pieces = turns(solved)
        decay = stay(decay)
        if merged:
            current = stay(kept[0])
        term, weights, base, force_weight = call(
            weights_kernel,
            [far(slab), near(slab), near(plane), near(plane)],
            (place, current, arrived[1], arrived[-1], decay, near_inflow),
            cost(8e6, 4 * MIB),
            scalars=1,
            limit=12,
        )
        lead, force, offset = call(
            offset_kernel,
            [near(plane), far(plane), far(chunks)],
            (place, *pieces, *forces, weights, base, force_weight),
            cost(2e6, 3 * MIB),
            scalars=1,
            limit=12,
        )
        following = along_march(lead, -1)
        offset, force, *pieces = lax.optimization_barrier((offset, force, *pieces))
        change, decay, *pressure = call(
            change_kernel,
            [near((stations + (not final), *plane)), near(slab)] + [far(slab)] * final,
            (place, *pieces, stay(term), stay(force), decay, near_inflow),
            cost(4e6, 4 * MIB),
            scalars=1,
            limit=12,
            scratch=[] if final else [pltpu.VMEM(slab, F32)],
        )
        offset = across_march(offset)
        (entering,) = call(scan_kernel, [far(chunks)], (scales, offset), cost(1e5, MIB))
        entering = across_march(entering)
        common = (entering, change, following, decay)
        if final:
            (current,) = call(
                last_kernel, [far(slab)], common, cost(4e6, 5 * MIB), limit=12
            )
            return (current, pressure[0])
        current, disc, *source = call(
            middle_kernel,
            [near(slab), near(plane, BF16)] + sources,
            (place, *common),
            cost(6e6, 5 * MIB),
            scalars=1,
            limit=12,
            scratch=[pltpu.VMEM(slab, F32)],
        )


def solution(mesh):
    in_specs = (
        P("march", "cross", None),
        P("march", "cross", None),
        P("cross", None),
        P(),
        P(),
        P("march", None, "cross"),
    )
    out_specs = (P("march", "cross", None), P("march", "cross", None))
    return jax.shard_map(local, mesh=mesh, in_specs=in_specs, out_specs=out_specs, check_vma=False)
```

```python
import ml_dtypes
import numpy as np
import jax
import jax.numpy as jnp
from jax import lax
from jax.experimental import pallas as pl
from jax.experimental.pallas import tpu as pltpu
from jax.sharding import PartitionSpec as P

SWEEPS = 2
SOURCE_GAIN = 0.04
SCREENING = 0.001
VISCOSITY = 0.1
DRAG_RATE = 0.01

F32 = jnp.float32
BF16 = jnp.bfloat16
SUB = 8
LANE = 128
EDGE = 8
STEPS = 4
MIB = 1024 * 1024
VMEM = pl.BlockSpec(memory_space=pltpu.VMEM)
SMEM = pl.BlockSpec(memory_space=pltpu.SMEM)


def tables(length):
    ordinal = np.arange(1, length + 1)
    product = np.outer(ordinal, ordinal) % (2 * (length + 1))
    sine = np.sqrt(2.0 / (length + 1)) * np.sin(np.pi * product / (length + 1))
    high = sine.astype(np.float32).astype(ml_dtypes.bfloat16)
    low = (sine - high.astype(np.float64)).astype(np.float32).astype(ml_dtypes.bfloat16)
    values = 2.0 - 2.0 * np.cos(np.pi * ordinal / (length + 1))
    inverse = 1.0 / (SCREENING + values[:, None] + values[None, :])
    return high, low, inverse.astype(np.float32)


def split(value):
    high = value.astype(BF16)
    return high, (value - high.astype(F32)).astype(BF16)


def groups(rows):
    return [(g, slice(SUB * g, SUB * g + SUB)) for g in range(rows // SUB)]


def to_chunks(ref, g, value):
    for h in range(2):
        for q in range(2):
            at = (2 * h + q) * LANE
            ref[2 * g + h, SUB * q : SUB * q + SUB, :] = value[:, at : at + LANE]


def from_chunks(ref, g):
    parts = []
    for h in range(2):
        for q in range(2):
            parts.append(ref[2 * g + h, SUB * q : SUB * q + SUB, :])
    return jnp.concatenate(parts, axis=1)


def decay_of(value, damping):
    return 1.0 - (damping + DRAG_RATE * jnp.abs(value))


def send_order(place, source, outs, i=None):
    count, height, _ = source.shape
    rows = slice(0, height) if i is None else pl.ds(pl.multiple_of(i * height, height), height)
    for r, ref in enumerate(outs):
        ref[rows, :] = source[lax.rem(place[0] + r, count)]


def send_edges(current, outs, first=True, last=True):
    stations, height, width = current.shape
    total = outs[1].shape[0]
    empty = jnp.zeros((EDGE - stations, width), F32)

    @pl.when(last)
    def _():
        rows = [current[s, height - 1 : height] for s in range(stations)]
        outs[1][total - EDGE : total] = jnp.concatenate(rows + [empty], axis=0)

    @pl.when(first)
    def _():
        rows = [current[s, 0:1] for s in range(stations)]
        outs[-1][total - EDGE : total] = jnp.concatenate(rows + [empty], axis=0)


def source_kernel(place, current, upstream, inflow, x0, x1, x2, x3, source):
    stations, height, _ = current.shape
    for _, rows in groups(height):
        previous = jnp.where(place[1] == 1, inflow[rows], upstream[rows])
        for s in range(stations):
            here = current[s, rows]
            source[s, rows] = SOURCE_GAIN * (here - previous)
            previous = here
    outs = (x0, x1, x2, x3)
    i = pl.program_id(0)
    send_order(place, source, outs, i)
    send_edges(current, outs, i == 0, i == pl.num_programs(0) - 1)


def decay_kernel(place, current, damping, decay, scale, *copy):
    for g, rows in groups(current.shape[1]):
        product = None
        for s in range(current.shape[0]):
            here = current[s, rows]
            for ref in copy:
                ref[s, rows] = here
            d = decay_of(here, damping[s, rows])
            decay[s, rows] = d
            product = d if product is None else product * d
        to_chunks(scale, g, product)


def weights_kernel(
    place, current, before, after, decay, inflow, term, weights, base, force_weight
):
    stations, height, width = current.shape
    first = place[1] == 1
    above = jnp.where(place[2] == 1, 0.0, before[height : height + EDGE])
    below = jnp.where(place[3] == 1, 0.0, after[height : height + EDGE])
    lane = lax.broadcasted_iota(jnp.int32, (SUB, width), 1)
    for g, rows in groups(height):
        lo, hi = SUB * g, SUB * g + SUB
        total = jnp.zeros((SUB, width), F32)
        factor = None
        for s in reversed(range(stations)):
            here = current[s, rows]
            if g == 0:
                up = jnp.concatenate([above[s : s + 1], current[s, 0 : SUB - 1]], axis=0)
            else:
                up = current[s, lo - 1 : hi - 1]
            if hi == height:
                down = jnp.concatenate([current[s, lo + 1 : hi], below[s : s + 1]], axis=0)
            else:
                down = current[s, lo + 1 : hi + 1]
            left = jnp.where(lane == 0, 0.0, pltpu.roll(here, 1, 1))
            right = jnp.where(lane == width - 1, 0.0, pltpu.roll(here, width - 1, 1))
            t = VISCOSITY * (up + down + left + right - 4.0 * here)
            term[s, rows] = t
            d = decay[s, rows]
            if factor is None:
                total, weight, factor = t, 1.0 - d, d
            else:
                if s == 0:
                    force_weight[rows] = factor
                total, weight, factor = total + factor * t, factor * (1.0 - d), factor * d
            if s == 0:
                entry = jnp.where(first, factor, 0.0)
                weight = weight + entry
                total = total + entry * inflow[rows]
            weights[s, rows] = weight
        base[rows] = total


def far_solve_kernel(
    place, x0, x1, x2, x3, high_far, low_far, inverse_far, p0, p1, p2, p3,
    plane, high, low, inverse, arrivals,
):
    copies = [
        pltpu.make_async_copy(far_ref, ref, arrivals.at[i])
        for i, (far_ref, ref) in enumerate(
            ((high_far, high), (low_far, low), (inverse_far, inverse))
        )
    ]
    solve(place, (x0, x1, x2, x3), (high, low, inverse), (), (p0, p1, p2, p3), plane, copies)


def near_solve_kernel(
    place, x0, x1, x2, x3, high, low, inverse, p0, p1, p2, p3, plane
):
    solve(place, (x0, x1, x2, x3), (high, low, inverse), (), (p0, p1, p2, p3), plane)


def solve(place, inputs, tables_near, forces, outputs, plane, copies=()):
    c = place[0]
    high, low, inverse = tables_near
    for copy in copies:
        copy.start()
    count = len(inputs)
    height = inputs[0].shape[0]
    for r, ref in enumerate(inputs):
        b = lax.rem(c - r + count, count)
        plane[pl.ds(pl.multiple_of(b * height, height), height), :] = ref[0:height]
    for copy in copies[:2]:
        copy.wait()
    sh, sl = high[...], low[...]
    by_left = jnp.concatenate([sh, sh, sl], axis=1)
    by_right = jnp.concatenate([sh, sl, sh], axis=0)

    def right(value):
        vh, vl = split(value)
        return jnp.dot(
            jnp.concatenate([vh, vh, vl], axis=1), by_right, preferred_element_type=F32
        )

    def left(value):
        vh, vl = split(value)
        return jnp.dot(
            by_left, jnp.concatenate([vh, vl, vh], axis=0), preferred_element_type=F32
        )

    modes = left(right(plane[...]))
    for copy in copies[2:]:
        copy.wait()
    modes = modes * inverse[...]
    plane[...] = right(left(modes))
    for r, ref in enumerate(outputs):
        b = lax.rem(c + r, count)
        ref[0:height] = plane[pl.ds(pl.multiple_of(b * height, height), height), :]
    if forces:
        extra = outputs[0].shape[0] - height
        for r, ref in enumerate(outputs):
            for q in range(height // extra):
                ref[height : height + extra, LANE * q : LANE * (q + 1)] = forces[-r][
                    extra * q : extra * (q + 1)
                ]


def disc_kernel(d0, d1, d2, d3, places, place_row, owners, *rest):
    streams, tabled = 4, (len(rest) - 11) // 2
    blades, tables_far = rest[:streams], rest[streams : streams + tabled]
    f0, f1, f2, f3 = rest[streams + tabled : streams + tabled + 4]
    tables_near = rest[streams + tabled + 4 : streams + 2 * tabled + 4]
    picked, total = rest[streams + 2 * tabled + 4 : streams + 2 * tabled + 6]
    step = pl.program_id(0)
    last = pl.num_programs(0) - 1
    height, width = d0.shape
    number = picked.shape[0]
    copies = [
        pltpu.make_async_copy(source, target, rest[-1].at[i])
        for i, (source, target) in enumerate(zip(tables_far, tables_near))
    ]

    @pl.when(step == 0)
    def _():
        for copy in copies:
            copy.start()
        plane = jnp.concatenate([d[...] for d in (d0, d1, d2, d3)], axis=0)
        lane = lax.broadcasted_iota(jnp.int32, (number, LANE), 1)
        chosen = [
            jnp.where(places[...] == lane + LANE * q, 1.0, 0.0).astype(BF16)
            for q in range(width // LANE)
        ]
        rows = jnp.dot(
            jnp.concatenate(chosen, axis=1), plane, preferred_element_type=F32
        )
        picked[...] = rows.astype(BF16)
        total[...] = jnp.zeros_like(total)

    per_step = blades[0].shape[0]
    for i in range(0, per_step, 2):
        pair = jnp.concatenate(
            [
                jnp.concatenate([blade[j] for blade in blades], axis=0)
                for j in (i, i + 1)
            ],
            axis=1,
        )
        response = jnp.dot(picked[...], pair, preferred_element_type=F32)
        first = step * per_step + i
        kept = jnp.where(owners[...] == first, response[:, :LANE], total[...])
        total[...] = jnp.where(owners[...] == first + 1, response[:, LANE:], kept)

    @pl.when(step == last)
    def _():
        rest_of, parts = jnp.tanh(total[...]), []
        for _ in range(3):
            parts.append(rest_of.astype(BF16))
            rest_of = rest_of - parts[-1].astype(F32)
        forces = jnp.concatenate(parts, axis=0)
        at = place_row[0:1]
        for r, ref in enumerate((f0, f1, f2, f3)):
            row = lax.broadcasted_iota(jnp.int32, (height, number), 0) + height * r
            back = jnp.where(row == at, 1.0, 0.0).astype(BF16)
            ref[...] = jnp.dot(
                jnp.concatenate([back] * 3, axis=1), forces, preferred_element_type=F32
            )
        for copy in copies:
            copy.wait()


def offset_kernel(place, *rest):
    c = place[0]
    pieces = rest[:4]
    *forces, weights, base, force_weight, lead, force, offset = rest[4:]
    count, height, full = weights.shape
    width = full // count
    for r in range(count):
        b = lax.rem(c + r if forces else c - r + count, count)
        lanes = pl.ds(pl.multiple_of(b * width, width), width)
        if forces:
            force[:, lanes] = forces[r][...]
        else:
            extra = pieces[r].shape[0] - height
            for q in range(height // extra):
                force[extra * q : extra * (q + 1), lanes] = pieces[r][
                    height : height + extra, width * q : width * (q + 1)
                ]

    for r in range(count):
        @pl.when(c == r)
        def _():
            lead[...] = pieces[r][0:height]

    for g, rows in groups(height):
        state = base[rows] + force_weight[rows] * force[rows]
        for r in range(count):
            s = lax.rem(c - r + count, count)
            state = state + weights[s, rows] * pieces[r][rows]
        to_chunks(offset, g, state)


def change_kernel(
    place, p0, p1, p2, p3, term, force, decay, inflow,
    change, decay_near, pressure,
):
    c = place[0]
    pieces = (p0, p1, p2, p3)
    count, height, _ = term.shape
    for r in range(count):
        pressure[lax.rem(c - r + count, count)] = pieces[r][0:height]
    for _, rows in groups(height):
        here = pressure[0, rows]
        entry = jnp.where(place[1] == 1, inflow[rows], -here)
        if change.shape[0] > count:
            change[count, rows] = entry
        for s in range(count):
            value = term[s, rows] + here
            if s == 0:
                value = value + force[rows]
            if s < count - 1:
                here = pressure[s + 1, rows]
                value = value - here
            d = decay[s, rows]
            decay_near[s, rows] = d
            if s == 0 and change.shape[0] == count:
                value = value + d * entry
            change[s, rows] = value


def scan_kernel(scale, offset, entering):
    entering[0] = jnp.zeros_like(entering[0])
    state = offset[0]
    for m in range(1, scale.shape[0]):
        entering[m] = state
        state = scale[m] * state + offset[m]


def march_rows(g, rows, entering, change, following, decay):
    stations = decay.shape[0]
    state = from_chunks(entering, g)
    if change.shape[0] > stations:
        state = state + change[stations, rows]
    states = [state]
    for s in range(stations):
        step = change[s, rows]
        if s == stations - 1:
            step = step - following[rows]
        state = decay[s, rows] * state + step
        states.append(state)
    return states


def middle_kernel(
    place, entering, change, following, decay, current, disc, x0, x1, x2, x3, source
):
    stations, height, _ = current.shape
    for g, rows in groups(height):
        states = march_rows(g, rows, entering, change, following, decay)
        for s in range(stations):
            current[s, rows] = states[s + 1]
            source[s, rows] = SOURCE_GAIN * (states[s + 1] - states[s])
    outs = (x0, x1, x2, x3)
    send_order(place, source, outs)
    send_edges(current, outs)
    disc[...] = current[0].astype(BF16)


def last_kernel(entering, change, following, decay, current):
    for g, rows in groups(current.shape[1]):
        states = march_rows(g, rows, entering, change, following, decay)
        for s in range(current.shape[0]):
            current[s, rows] = states[s + 1]


def cost(flops, size):
    return pl.CostEstimate(flops=int(flops), bytes_accessed=int(size), transcendentals=0)


def near(shape, dtype=F32):
    return pltpu.VMEM(shape, dtype)


def far(shape, dtype=F32):
    return pltpu.HBM(shape, dtype)


def stay(value):
    return pltpu.with_memory_space_constraint(value, pltpu.HBM)


def call(kernel, outs, args, work, scalars=0, limit=8, scratch=()):
    return pl.pallas_call(
        kernel,
        out_shape=outs,
        in_specs=[SMEM] * scalars + [VMEM] * (len(args) - scalars),
        out_specs=[VMEM] * len(outs),
        scratch_shapes=list(scratch),
        compiler_params=pltpu.CompilerParams(vmem_limit_bytes=limit * MIB),
        cost_estimate=work,
    )(*args)


def by_rows(kernel, height, outs, place, args, work, whole=(), scratch=()):
    part = height // STEPS

    def spec(shape, index):
        if index in whole:
            return pl.BlockSpec(shape, lambda i, p: (0,) * len(shape))
        if shape[-1] == LANE and len(shape) == 3:
            return pl.BlockSpec((shape[0] // STEPS,) + shape[1:], lambda i, p: (i, 0, 0))
        if len(shape) == 3:
            return pl.BlockSpec((shape[0], part, shape[2]), lambda i, p: (0, i, 0))
        return pl.BlockSpec((part, shape[1]), lambda i, p: (i, 0))

    count = len(args)
    return pl.pallas_call(
        kernel,
        grid_spec=pltpu.PrefetchScalarGridSpec(
            num_scalar_prefetch=1,
            grid=(STEPS,),
            in_specs=[spec(a.shape, None) for a in args],
            out_specs=[spec(a.inner_aval.shape, i) for i, a in enumerate(outs)],
            scratch_shapes=list(scratch),
        ),
        out_shape=outs,
        compiler_params=pltpu.CompilerParams(vmem_limit_bytes=12 * MIB),
        cost_estimate=work,
    )(place, *args)


def disc_forces(rows, where, blades, tabled=()):
    height, width = rows[0].shape
    count = len(rows)
    number = blades.shape[0]
    per_step, streams = 32, 4
    fixed = lambda shape: pl.BlockSpec(shape, lambda i: (0,) * len(shape))
    table = lambda k: pl.BlockSpec((per_step, width // streams, LANE), lambda i: (i, k, 0))
    discs = where[0].shape[0]
    return pl.pallas_call(
        disc_kernel,
        grid=(number // per_step,),
        out_shape=[near((height, LANE))] * count + [near(t.shape, t.dtype) for t in tabled],
        in_specs=[fixed((height, width))] * count
        + [fixed(w.shape) for w in where]
        + [table(k) for k in range(streams)]
        + [pl.BlockSpec(memory_space=pltpu.HBM)] * len(tabled),
        out_specs=[fixed((height, LANE))] * count
        + [pl.BlockSpec(memory_space=pltpu.VMEM)] * len(tabled),
        scratch_shapes=[
            pltpu.VMEM((discs, width), BF16),
            pltpu.VMEM((discs, LANE), F32),
            pltpu.SemaphoreType.DMA((3,)),
        ],
        compiler_params=pltpu.CompilerParams(vmem_limit_bytes=16 * MIB),
        cost_estimate=cost(2 * number * width * width * LANE, 5 * MIB),
    )(*rows, *map(stay, where), *[stay(blades)] * streams, *tabled)


def local(velocity_guess, damping, inflow, disc_rows, owner, blade):
    stations, height, width = velocity_guess.shape
    march_size = lax.axis_size("march")
    cross_size = lax.axis_size("cross")
    march_index = lax.axis_index("march")
    cross_index = lax.axis_index("cross")
    disc_slab = stations * march_size // 2 // stations
    at_disc = march_index == disc_slab
    first = march_index == 0
    place = jnp.stack(
        [
            cross_index.astype(jnp.int32),
            first.astype(jnp.int32),
            (cross_index == 0).astype(jnp.int32),
            (cross_index == cross_size - 1).astype(jnp.int32),
        ]
    )
    tabled = [stay(jnp.asarray(t)) for t in tables(width)]

    slab = (stations, height, width)
    plane = (height, width)
    edged = (height + EDGE, width)
    chunks = (march_size, height * width // march_size // LANE, LANE)
    sources = [near(plane), near(edged), near(plane), near(edged)]

    def turn(value, steps):
        return lax.ppermute(
            value, "cross", [(i, (i + steps) % cross_size) for i in range(cross_size)]
        )

    def turns(blocks, sign=1):
        return [blocks[0]] + [turn(blocks[r], sign * r) for r in range(1, cross_size)]

    def along_march(value, steps):
        count = march_size
        return lax.ppermute(
            value, "march", [(i, i + steps) for i in range(count) if 0 <= i + steps < count]
        )

    def across_march(value):
        return lax.all_to_all(value, "march", split_axis=0, concat_axis=0, tiled=True)

    blades = lax.all_gather(blade, "march", axis=0, tiled=True)
    turn_of = (cross_index - disc_rows // height + cross_size) % cross_size
    places = turn_of * height + disc_rows % height
    count = disc_rows.shape[0]
    where = (
        jnp.broadcast_to(places[:, None], (count, LANE)),
        jnp.broadcast_to(places[None, :], (SUB, count)),
        jnp.broadcast_to(jnp.where(at_disc, owner, -1)[:, None], (count, LANE)),
    )

    step = (stations, height // STEPS, width)
    near_inflow = stay(inflow)
    upstream = along_march(velocity_guess[-1], 1)
    current = stay(velocity_guess)
    disc = velocity_guess[0].astype(BF16)
    rows = turns([disc] * cross_size)
    source = by_rows(
        source_kernel,
        height,
        sources,
        place,
        (current, upstream, near_inflow),
        cost(1e6, 2 * MIB),
        whole=range(4),
        scratch=[pltpu.VMEM(step, F32)],
    )
    for sweep_index in range(SWEEPS):
        merged = sweep_index > 0
        final = sweep_index == SWEEPS - 1
        if merged:
            rows = turns([disc] * cross_size)
        guess, damp, *source = lax.optimization_barrier((current, damping, *source))
        arrived = turns(source)
        decay, scale, *kept = by_rows(
            decay_kernel,
            height,
            [far(slab), far(chunks)] + [far(slab)] * merged,
            place,
            (guess if merged else stay(guess), stay(damp)),
            cost(4e6, 3 * MIB),
        )
        solve_cost = cost(3 * 8 * width**3, 5 * MIB)
        if merged:
            scale, *arrived = lax.optimization_barrier((scale, *arrived))
            made = disc_forces(rows, where, blades, tabled)
            forces, near_tables = made[:cross_size], made[cross_size:]
            solved = call(
                near_solve_kernel,
                [near(plane)] * cross_size,
                (place, *arrived, *near_tables),
                solve_cost,
                scalars=1,
                limit=16,
                scratch=[pltpu.VMEM((width, width), F32)],
            )
            scales = across_march(scale)
            forces, solved = lax.optimization_barrier((turns(forces, -1), solved))
        else:
            scales = across_march(scale)
            solved = pl.pallas_call(
                far_solve_kernel,
                out_shape=[near(plane)] * cross_size,
                in_specs=[SMEM] + [VMEM] * cross_size + [pl.BlockSpec(memory_space=pltpu.HBM)] * 3,
                out_specs=[VMEM] * cross_size,
                scratch_shapes=[pltpu.VMEM((width, width), F32)]
                + [pltpu.VMEM((width, width), BF16)] * 2
                + [pltpu.VMEM((width, width), F32), pltpu.SemaphoreType.DMA((3,))],
                compiler_params=pltpu.CompilerParams(vmem_limit_bytes=20 * MIB),
                cost_estimate=solve_cost,
            )(place, *arrived, *tabled)
            rows, scales, solved, where = lax.optimization_barrier((rows, scales, solved, where))
            forces = turns(disc_forces(rows, where, blades), -1)
        pieces = turns(solved)
        decay = stay(decay)
        if merged:
            current = stay(kept[0])
        term, weights, base, force_weight = call(
            weights_kernel,
            [far(slab), near(slab), near(plane), near(plane)],
            (place, current, arrived[1], arrived[-1], decay, near_inflow),
            cost(8e6, 4 * MIB),
            scalars=1,
            limit=12,
        )
        lead, force, offset = call(
            offset_kernel,
            [near(plane), far(plane), far(chunks)],
            (place, *pieces, *forces, weights, base, force_weight),
            cost(2e6, 3 * MIB),
            scalars=1,
            limit=12,
        )
        following = along_march(lead, -1)
        offset, force, *pieces = lax.optimization_barrier((offset, force, *pieces))
        change, decay, *pressure = call(
            change_kernel,
            [near((stations + (not final), *plane)), near(slab)] + [far(slab)] * final,
            (place, *pieces, stay(term), stay(force), decay, near_inflow),
            cost(4e6, 4 * MIB),
            scalars=1,
            limit=12,
            scratch=[] if final else [pltpu.VMEM(slab, F32)],
        )
        offset = across_march(offset)
        (entering,) = call(scan_kernel, [far(chunks)], (scales, offset), cost(1e5, MIB))
        entering = across_march(entering)
        common = (entering, change, following, decay)
        if final:
            (current,) = call(
                last_kernel, [far(slab)], common, cost(4e6, 5 * MIB), limit=12
            )
            return (current, pressure[0])
        current, disc, *source = call(
            middle_kernel,
            [near(slab), near(plane, BF16)] + sources,
            (place, *common),
            cost(6e6, 5 * MIB),
            scalars=1,
            limit=12,
            scratch=[pltpu.VMEM(slab, F32)],
        )


def solution(mesh):
    in_specs = (
        P("march", "cross", None),
        P("march", "cross", None),
        P("cross", None),
        P(),
        P(),
        P("march", None, "cross"),
    )
    out_specs = (P("march", "cross", None), P("march", "cross", None))
    return jax.shard_map(local, mesh=mesh, in_specs=in_specs, out_specs=out_specs, check_vma=False)
```
